512 devices in a mesh: rep: 32 (over z_hi, x, core), exp: 16 (over z_lo, y).
Axes of the slice: x: 4, y: 4, z: 16 (z_hi: 4, z_lo: 4; z = z_hi * 4 + z_lo), core: 2. Of those that a mesh axis runs over, the one named last changes fastest.
Arguments:
- query: bfloat16 [512, 8192], P('rep', 'exp'), may hold values from -150 to 150
- new_key: bfloat16 [512, 2048], P('rep', 'exp'), may hold values from -5 to 5
- new_value: bfloat16 [512, 2048], P('rep', 'exp'), may hold values from -6 to 6
- page_pool: bfloat16 [1536, 16, 2, 16, 128], P('rep', 'exp'), may hold values from -6 to 6
- block_table: int32 [512, 8], P('rep'), may hold values from 0 to 47, as said below
- lengths: int32 [512], replicated, may hold values from 1 to 128
- anchor: int32 [512], replicated, may hold values from 0 to 511, as said below
- conv_input: bfloat16 [512, 8192], P('rep', 'exp'), may hold values from -6 to 6
- gate_input: bfloat16 [512, 8192], P('rep', 'exp'), may hold values from -6 to 6
- window_state: bfloat16 [512, 3, 8192], P('rep', None, 'exp'), may hold values from -6 to 6
- scan_state: float32 [512, 16, 8192], P('rep', None, 'exp'), may hold values from -6 to 6
- filter_taps: float32 [4, 8192], P(None, 'exp'), may hold values from -3 to 3
- filter_bias: float32 [8192], P('exp'), may hold values from -3 to 3
- mix_weight: bfloat16 [8192, 288], P('exp'), may hold values from -0.0625 to 0.0625
- step_weight: bfloat16 [256, 8192], P(None, 'exp'), may hold values from -0.375 to 0.375
- step_bias: float32 [8192], P('exp'), may hold values from -1 to 1
- log_decay: float32 [16, 8192], P(None, 'exp'), may hold values from -2 to 1.5
- skip_gain: float32 [8192], P('exp'), may hold values from 0.5 to 1.5
- routes: int32 [512, 2], P('rep'), may hold values from 0 to 15, all different within a row; in each aligned block of 16 rows (0 to 15, 16 to 31, ...) at most 4 rows name the same one
- route_weight: float32 [512, 2], P('rep'), may hold values from 0.2 to 1
- expert_hidden: bfloat16 [16, 128, 12288], P('exp', None, 'rep'), may hold values from -6 to 6
- down_weight: bfloat16 [16, 12288, 4096], P('exp', 'rep'), may hold values from -0.0546875 to 0.0546875
Outputs:
- attention_out: bfloat16 [512, 8192], P('rep', 'exp')
- moved_pages: bfloat16 [64, 16, 2, 128, 128], P('rep', 'exp')
- mamba_out: bfloat16 [512, 8192], P('rep', 'exp')
- expert_mix: bfloat16 [512, 4096], P('rep', 'exp')
The draws below stay inside these ranges and needn't reach their ends.
Inputs may be any that keep to these rules, and one draw needn't show every extreme that they name: anchor is a permutation. Exactly 2 new slots of each replica take requests from other replicas, each from a different replica, and exactly 2 requests of each replica leave it, each to a different replica. `block_table`: each replica has at least one request of length 128. The first ceil(lengths / 16) entries of a row are distinct pages of its replica's pool, used by no other request of that replica; later entries are arbitrary. `routes`: in the 16 rows of one replica no expert is named more than 4 times.
All inputs are finite; a program needn't handle non-finite values.
Results may differ from the reference program's by a relative error of at most 0.0065.
Values may be sent and summed in bfloat16 or wider, within the bound.
No kernel may reach another device: no remote copies, remote signals or barrier semaphores. Data moves between devices by JAX's collectives and lax.ppermute only.
A program may use at most 64 MiB of HBM per device.

```python
import math
import jax
import jax.numpy as jnp
import numpy as np
from jax import lax

REQ_REP = 16
REQUESTS = 512
MIG = 2
PAGE = 16
MAXP = 8
MAXLEN = 128
POOL = 48
HD = 128
HQ_DEV = 4
KVH = 16
HEADS = 64
CH = 8192
STATE = 16
CONV = 4
DTR = 256
D = 4096
FF = 12288
EXPERTS = 16
TOP = 2
CAP = 4
N_REP = 32


def shared_keys(key):
    return jnp.clip(jax.random.normal(key, (REQUESTS, KVH * HD), jnp.float32), -5.0, 5.0)


def page_layout(key):
    columns = jnp.arange(REQ_REP, dtype=jnp.int32)[None, :]
    ranking = jax.random.randint(key, (N_REP, REQ_REP), 0, 1 << 20) * REQ_REP + columns
    order = jnp.argsort(ranking, axis=1)
    place = jnp.argsort(order, axis=1)
    long_len = jax.random.randint(jax.random.fold_in(key, 1), (N_REP, REQ_REP), MAXLEN // 2 + 1, MAXLEN + 1)
    short_len = jax.random.randint(jax.random.fold_in(key, 2), (N_REP, REQ_REP), 1, 2 * PAGE + 1)
    sizes_all = jnp.where(place == 0, MAXLEN, jnp.where(place == 1, long_len, short_len))
    page_count = (sizes_all + PAGE - 1) // PAGE
    starting = jnp.cumsum(page_count, axis=1) - page_count
    pool_rank = jax.random.randint(jax.random.fold_in(key, 3), (N_REP, POOL), 0, 1 << 20) * POOL + jnp.arange(POOL, dtype=jnp.int32)[None, :]
    pool_order = jnp.argsort(pool_rank, axis=1)
    filler = jax.random.randint(jax.random.fold_in(key, 4), (N_REP, REQ_REP, MAXP), 0, POOL)
    steps_in = jnp.arange(MAXP, dtype=jnp.int32)[None, None, :]
    where_at = jnp.minimum(starting[:, :, None] + steps_in, POOL - 1).reshape(N_REP, REQ_REP * MAXP)
    picked = jnp.take_along_axis(pool_order, where_at, axis=1).reshape(N_REP, REQ_REP, MAXP)
    table = jnp.where(steps_in < page_count[:, :, None], picked, filler)
    return (sizes_all.reshape(REQUESTS).astype(jnp.int32), table.reshape(REQUESTS, MAXP).astype(jnp.int32))


def draw_lengths(key, part):
    sizes_all, table = page_layout(key)
    return sizes_all


def draw_block_table(key, part):
    sizes_all, table = page_layout(key)
    return table


def draw_anchor(key, part):
    key = jax.random.fold_in(key, 7)
    first_key, second_key = jax.random.split(key)
    ranking = jax.random.randint(first_key, (N_REP, REQ_REP), 0, 1 << 20) * REQ_REP + jnp.arange(REQ_REP, dtype=jnp.int32)[None, :]
    leaving = jnp.argsort(ranking, axis=1)[:, :MIG]
    replica_rank = jax.random.randint(second_key, (N_REP,), 0, 1 << 20) * N_REP + jnp.arange(N_REP, dtype=jnp.int32)
    replica_order = jnp.argsort(replica_rank)
    place = jnp.argsort(replica_order)
    offsets = jnp.arange(MIG, dtype=jnp.int32)[None, :] + 1
    target = replica_order[(place[:, None] + offsets) % N_REP]
    source_slot = jnp.arange(N_REP, dtype=jnp.int32)[:, None] * REQ_REP + leaving
    target_slot = target * REQ_REP + leaving[target, jnp.arange(MIG, dtype=jnp.int32)[None, :]]
    result = jnp.arange(REQUESTS, dtype=jnp.int32).at[target_slot.reshape(-1)].set(source_slot.reshape(-1))
    return result.astype(jnp.int32)


def draw_new_key(key, part):
    base = shared_keys(key)
    return base.astype(jnp.bfloat16)


def draw_query(key, part):
    key = jax.random.fold_in(key, 11)
    values_all = jnp.clip(jax.random.normal(key, (REQUESTS, HEADS * HD), jnp.float32), -5.0, 5.0)
    return values_all.astype(jnp.bfloat16)


def strengthened(values, rng, source, target, shards_of, factor):
    def block_of(axis_at):
        return (jnp.arange(values.shape[axis_at]) // (values.shape[axis_at] // shards_of)).reshape((-1,) + (1,) * (values.ndim - 1 - axis_at))

    one_side = jax.random.permutation(rng, shards_of)[block_of(target)]
    second = (block_of(target) + shards_of // 2) % shards_of
    return jnp.where((block_of(source) == one_side) | (block_of(source) == second), factor * values, values)


def block_scale(stream_key, dims, pieces, smallest, largest):
    def one(dim, blocks):
        heights = jax.random.uniform(jax.random.fold_in(jax.random.fold_in(stream_key, 6), dim), (blocks,), jnp.float32, smallest / len(pieces), largest / len(pieces))
        return jnp.repeat(jnp.exp(heights), dims[dim] // blocks).reshape((-1,) + (1,) * (len(dims) - dim - 1))

    level = one(*pieces[0])
    for cut in pieces[1:]:
        level = level * one(*cut)
    return level


def deal_out(key, own, number, rows, number_of, top, bound, lean):
    order = jax.random.permutation(key, number_of)
    crowded, usual = load_shares(number_of, rows * top, bound, lean, True), load_shares(number_of, rows * top, bound, lean, False)
    places = jnp.arange(number_of)

    def named(tallies, turn):
        used = int((tallies > 0).sum())
        fixed = max(1, used // 4)
        moved = fixed + (places - fixed + turn * (used - fixed)) % max(1, number_of - fixed)
        return jnp.zeros((number_of,), jnp.int32).at[order[jnp.where(places < fixed, places, moved)]].set(jnp.asarray(tallies, jnp.int32))

    tallies = jnp.where(number % 4 == 0, named(crowded, number // 4), named(usual, number - number // 4 - 1))
    mixed = jax.random.permutation(jax.random.fold_in(own, 3), number_of)
    donor, sink = mixed[0:number_of // 2 * 2:2], mixed[1:number_of // 2 * 2:2]
    margin = jnp.minimum(tallies[donor] - 1, bound - tallies[sink]) // 2
    margin = jnp.where((donor == order[0]) | (sink == order[0]) | (tallies[sink] == 0), 0, jnp.maximum(margin, 0))
    moved = jax.random.randint(jax.random.fold_in(own, 4), (number_of // 2,), 0, 1 << 20) % (margin + 1)
    tallies = tallies.at[donor].add(-moved).at[sink].add(moved)
    members = jnp.searchsorted(jnp.cumsum(tallies), jnp.arange(rows * top), side="right").astype(jnp.int32)
    listing = members.reshape(top, rows).T
    listing = listing[jax.random.permutation(jax.random.fold_in(own, 1), rows)]
    turn = jax.random.randint(jax.random.fold_in(own, 2), (rows, 1), 0, top)
    return jnp.take_along_axis(listing, (jnp.arange(top)[None, :] + turn) % top, axis=1)


def load_shares(number_of, total, limit, slope, full):
    loads = [(1 << 20) // math.isqrt(standing ** slope) + 1 for standing in range(1, number_of + 1)]
    largest = limit if full else min(limit, max(-(-total // number_of), total * loads[0] // sum(loads)))
    least = 1 if total - largest >= number_of - 1 else 0
    given, surplus = [largest] + [least] * (number_of - 1), total - largest - least * (number_of - 1)
    while surplus > 0:
        free = [i for i in range(1, number_of) if given[i] < largest] or [i for i in range(1, number_of) if given[i] < limit]
        whole, left = sum([loads[i] for i in free]), surplus
        for i in free:
            addition = min(limit - given[i], max(1, left * loads[i] // whole), surplus)
            given[i] = given[i] + addition
            surplus = surplus - addition
    return np.array(given)


def scatter_about(key, dims, width, reach, cuts=(), held_as=jnp.bfloat16):
    entries = width * jax.random.normal(key, dims, jnp.float32)
    if cuts:
        entries = entries * block_scale(key, dims, cuts, -0.22, 0.18)
    return jnp.clip(entries, -reach, reach).astype(held_as)


def gaussian_with(rng, extent, scale, most, shards, heavy, kind=jnp.bfloat16):
    entries = scale * jax.random.normal(rng, extent, jnp.float32)
    if shards:
        entries = entries * block_scale(rng, extent, shards, -0.22, 0.18)
    return jnp.clip(strengthened(entries, jax.random.fold_in(rng, 3), *heavy), -most, most).astype(kind)


def setup_inputs(seed: int = 0) -> dict:
    streams_of = jax.random.split(jax.random.key(seed), 23)
    query = draw_query(jax.random.fold_in(streams_of[22], 71), 0)
    new_key = draw_new_key(jax.random.fold_in(streams_of[22], 71), 0)
    new_value = scatter_about(streams_of[2], (REQUESTS, KVH * HD), 1.0, 6.0, ((0, 32), (1, 16)))
    page_pool = scatter_about(streams_of[3], (N_REP * POOL, KVH, 2, PAGE, HD), 1.0, 6.0, ((0, 32), (1, 16)))
    block_table = draw_block_table(jax.random.fold_in(streams_of[22], 71), 0)
    lengths = draw_lengths(jax.random.fold_in(streams_of[22], 71), 0)
    anchor = draw_anchor(jax.random.fold_in(streams_of[22], 71), 0)
    conv_input = scatter_about(streams_of[7], (REQUESTS, CH), 1.0, 6.0, ((0, 32), (1, 16)))
    gate_input = scatter_about(streams_of[8], (REQUESTS, CH), 1.0, 6.0, ((0, 32), (1, 16)))
    window_state = scatter_about(streams_of[9], (REQUESTS, CONV - 1, CH), 1.0, 6.0, ((0, 32), (2, 16)))
    scan_state = scatter_about(streams_of[10], (REQUESTS, STATE, CH), 1.0, 6.0, ((0, 32), (2, 16)), jnp.float32)
    filter_taps = scatter_about(streams_of[11], (CONV, CH), CONV ** -0.5, 3.0, ((1, 16),), jnp.float32)
    filter_bias = scatter_about(streams_of[12], (CH,), 0.5, 3.0, ((0, 16),), jnp.float32)
    mix_weight = scatter_about(streams_of[13], (CH, DTR + 2 * STATE), CH ** -0.5, 0.0625, ((0, 16),))
    step_weight = scatter_about(streams_of[14], (DTR, CH), DTR ** -0.5, 0.375, ((1, 16),))
    step_bias = jnp.clip(jax.random.uniform(streams_of[15], (CH,), jnp.float32, -1.0, 1.0) * block_scale(streams_of[15], (CH,), ((0, 16),), -0.4, 0.0), -1.0, 1.0)
    log_decay = jnp.clip(-2.0 + 3.5 * jax.random.uniform(streams_of[16], (STATE, CH), jnp.float32) ** block_scale(streams_of[16], (STATE, CH), ((1, 16),), -0.2, 0.2), -2.0, 1.5)
    skip_gain = jnp.clip(0.5 + 1.0 * jax.random.uniform(streams_of[17], (CH,), jnp.float32) ** block_scale(streams_of[17], (CH,), ((0, 16),), -0.2, 0.2), 0.5, 1.5)
    routes_keys = jax.random.split(jax.random.fold_in(streams_of[18], 1), REQUESTS // REQ_REP)
    routes_turns = jax.random.permutation(jax.random.fold_in(streams_of[18], 3), REQUESTS // REQ_REP)
    routes = jax.vmap(lambda own, number: deal_out(jax.random.fold_in(streams_of[18], 2), own, number, REQ_REP, EXPERTS, TOP, CAP, 2))(routes_keys, routes_turns).reshape((REQUESTS, TOP))
    route_weight = jnp.clip(0.2 + 0.8 * jax.random.uniform(streams_of[19], (REQUESTS, TOP), jnp.float32) ** block_scale(streams_of[19], (REQUESTS, TOP), ((0, 32),), -0.2, 0.2), 0.2, 1.0)
    expert_hidden = gaussian_with(streams_of[20], (EXPERTS, N_REP * CAP, FF), 1.0, 6.0, ((0, 16), (2, 32)), (2, 1, 32, 2.75))
    down_weight = scatter_about(streams_of[21], (EXPERTS, FF, D), FF ** -0.5, 0.0546875, ((0, 16), (1, 32)))
    return {"query": query, "new_key": new_key, "new_value": new_value, "page_pool": page_pool, "block_table": block_table, "lengths": lengths, "anchor": anchor, "conv_input": conv_input, "gate_input": gate_input, "window_state": window_state, "scan_state": scan_state, "filter_taps": filter_taps, "filter_bias": filter_bias, "mix_weight": mix_weight, "step_weight": step_weight, "step_bias": step_bias, "log_decay": log_decay, "skip_gain": skip_gain, "routes": routes, "route_weight": route_weight, "expert_hidden": expert_hidden, "down_weight": down_weight}


def reference(query, new_key, new_value, page_pool, block_table, lengths, anchor, conv_input, gate_input, window_state, scan_state, filter_taps, filter_bias, mix_weight, step_weight, step_bias, log_decay, skip_gain, routes, route_weight, expert_hidden, down_weight):
    scale = 1.0 / math.sqrt(HD)

    def replica_step(replica):
        first = replica * REQ_REP
        anchors = lax.dynamic_slice_in_dim(anchor, first, REQ_REP)
        source = anchors // REQ_REP
        pages = block_table[anchors] + source[:, None] * POOL
        blocks = page_pool[pages]
        cached = jnp.transpose(blocks, (0, 2, 3, 1, 4, 5)).reshape(REQ_REP, KVH, 2, MAXLEN, HD)
        queries = lax.dynamic_slice_in_dim(query, first, REQ_REP).astype(jnp.float32).reshape(REQ_REP, KVH, HQ_DEV, HD)
        fresh_key = lax.dynamic_slice_in_dim(new_key, first, REQ_REP).astype(jnp.float32).reshape(REQ_REP, KVH, HD)
        fresh_value = lax.dynamic_slice_in_dim(new_value, first, REQ_REP).astype(jnp.float32).reshape(REQ_REP, KVH, HD)
        keys_full = cached[:, :, 0].astype(jnp.float32)
        values_full = cached[:, :, 1].astype(jnp.float32)
        scores = jnp.einsum('rkhd,rktd->rkht', queries, keys_full) * scale
        own_score = jnp.einsum('rkhd,rkd->rkh', queries, fresh_key) * scale
        live = lengths[anchors]
        visible = jnp.arange(MAXLEN, dtype=jnp.int32)[None, None, None, :] < live[:, None, None, None]
        scores = jnp.where(visible, scores, -jnp.inf)
        highest = jnp.maximum(lax.optimization_barrier(jnp.max(scores, axis=-1)), own_score)
        expweights = jnp.exp(scores - highest[..., None])
        own_exp = jnp.exp(own_score - highest)
        denominator = lax.optimization_barrier(jnp.sum(expweights, axis=-1)) + own_exp
        weights = lax.optimization_barrier((expweights / denominator[..., None]).astype(jnp.bfloat16)).astype(jnp.float32)
        own_weight = lax.optimization_barrier((own_exp / denominator).astype(jnp.bfloat16)).astype(jnp.float32)
        context = jnp.einsum('rkht,rktd->rkhd', weights, values_full) + own_weight[..., None] * fresh_value[:, :, None, :]
        attended = context.reshape(REQ_REP, HEADS * HD).astype(jnp.bfloat16)
        arrivals = jnp.nonzero(source != replica, size=MIG)[0]
        arrival_live = live[arrivals]
        keep = jnp.arange(MAXLEN, dtype=jnp.int32)[None, None, None, :, None] < arrival_live[:, None, None, None, None]
        moved = jnp.where(keep, cached[arrivals], jnp.zeros((), cached.dtype))
        window = jnp.concatenate([window_state[anchors].astype(jnp.float32), lax.dynamic_slice_in_dim(conv_input, first, REQ_REP)[:, None, :].astype(jnp.float32)], axis=1)
        mixed = lax.optimization_barrier(jnp.sum(window * filter_taps[None], axis=1)) + filter_bias
        activated = jax.nn.silu(mixed)
        projected = jnp.dot(activated.astype(jnp.bfloat16), mix_weight, preferred_element_type=jnp.float32)
        step_size = jax.nn.softplus(jnp.dot(projected[:, :DTR].astype(jnp.bfloat16), step_weight, preferred_element_type=jnp.float32) + step_bias)
        inflow = projected[:, DTR:DTR + STATE]
        readout = projected[:, DTR + STATE:]
        decay = jnp.exp(step_size[:, None, :] * (-jnp.exp(log_decay))[None])
        state = decay * scan_state[anchors] + step_size[:, None, :] * inflow[:, :, None] * activated[:, None, :]
        output = lax.optimization_barrier(jnp.sum(readout[:, :, None] * state, axis=1)) + skip_gain * activated
        gate_rows = lax.dynamic_slice_in_dim(gate_input, first, REQ_REP).astype(jnp.float32)
        gated = (output * jax.nn.silu(gate_rows)).astype(jnp.bfloat16)
        return (attended, moved, gated)
    attended, moved, gated = lax.map(replica_step, jnp.arange(N_REP, dtype=jnp.int32))
    attention_out = attended.reshape(REQUESTS, HEADS * HD)
    moved_pages = moved.reshape(N_REP * MIG, KVH, 2, MAXLEN, HD)
    mamba_out = gated.reshape(REQUESTS, CH)

    def expert_rows(pair):
        hidden, weight = pair
        return jnp.dot(hidden, weight, preferred_element_type=jnp.float32).astype(jnp.bfloat16)
    expert_out = lax.map(expert_rows, (expert_hidden, down_weight))
    flat_routes = routes.reshape(N_REP, REQ_REP * TOP)
    matches = (flat_routes[:, :, None] == jnp.arange(EXPERTS, dtype=jnp.int32)[None, None, :]).astype(jnp.int32)
    earlier = jnp.cumsum(matches, axis=1) - matches
    position = lax.optimization_barrier(jnp.sum(earlier * matches, axis=2))
    slot = jnp.arange(N_REP, dtype=jnp.int32)[:, None] * CAP + position
    row_index = (flat_routes * (N_REP * CAP) + slot).reshape(REQUESTS * TOP)
    picked = expert_out.reshape(EXPERTS * N_REP * CAP, D)[row_index].astype(jnp.float32).reshape(REQUESTS, TOP, D)
    expert_mix = lax.optimization_barrier(jnp.sum(picked * route_weight[:, :, None], axis=1)).astype(jnp.bfloat16)
    return (attention_out, moved_pages, mamba_out, expert_mix)
```

```python
import math

import jax
import jax.numpy as jnp
from jax import lax
from jax.experimental import pallas as pl
from jax.experimental.pallas import tpu as pltpu
from jax.sharding import PartitionSpec as P

MIG = 2
LANES = 128
SUB = 8
F32 = jnp.float32
BF16 = jnp.bfloat16


def _smem():
    return pl.BlockSpec(memory_space=pltpu.SMEM)


def _vmem():
    return pl.BlockSpec(memory_space=pltpu.VMEM)


def _call(body, name, out_shape, ins, outs, args, scratch=(), flops=0, nbytes=0):
    return pl.pallas_call(
        body,
        name=name,
        out_shape=out_shape,
        in_specs=ins,
        out_specs=outs,
        scratch_shapes=list(scratch),
        compiler_params=pltpu.CompilerParams(vmem_limit_bytes=32 * 1024 * 1024),
        cost_estimate=pl.CostEstimate(flops=flops, bytes_accessed=nbytes, transcendentals=0),
    )(*args)


def _present(anchor_ref, base, requests):
    mask = jnp.int32(0)
    for g in range(requests):
        a = anchor_ref[base + g] - base
        inside = (a >= 0) & (a < requests)
        mask = mask | jnp.where(inside, jnp.int32(1) << jnp.clip(a, 0, requests - 1), 0)
    return mask


def _slots(rep_ref, anchor_ref, requests):
    base = rep_ref[0] * requests
    count = jnp.int32(0)
    found = []
    for g in range(requests):
        a = anchor_ref[base + g]
        local = a - base
        arrived = (local < 0) | (local >= requests)
        found.append((a, jnp.clip(local, 0, requests - 1), arrived, jnp.minimum(count, MIG - 1)))
        count = count + jnp.where(arrived, 1, 0)
    return found


def _pack_body(requests, rep_ref, anchor_ref, table_ref, pool_ref, window_ref, scan_ref, out_ref, win_ref):
    base = rep_ref[0] * requests
    mask = _present(anchor_ref, base, requests)
    first, second = jnp.int32(0), jnp.int32(0)
    for o in reversed(range(requests)):
        leaves = ((mask >> o) & 1) == 0
        second = jnp.where(leaves, first, second)
        first = jnp.where(leaves, o, first)
    pages = table_ref.shape[1]
    blocks = scan_ref.shape[2] // LANES
    taps = window_ref.shape[1]
    win_ref[...] = jnp.zeros_like(win_ref)
    for j, o in enumerate((first, second)):
        scan = scan_ref[o]
        high = scan.astype(BF16).astype(F32)
        rest = scan - high
        middle = rest.astype(BF16).astype(F32)
        low = rest - middle
        win_ref[0:taps, :] = window_ref[o].astype(F32)
        win = win_ref[...]
        tails = []
        for part in (high, middle, low):
            for b in range(blocks):
                for h in range(scan.shape[0] // SUB):
                    tails.append(part[h * SUB : (h + 1) * SUB, b * LANES : (b + 1) * LANES])
        for b in range(blocks):
            tails.append(win[:, b * LANES : (b + 1) * LANES])
        for m in range(pages):
            page = pool_ref[table_ref[o, m], 0].astype(F32)
            for c in range(2):
                for h in range(2):
                    i = 4 * m + 2 * c + h
                    tail = tails[i] if i < len(tails) else jnp.zeros((SUB, LANES), F32)
                    head = page[c, h * SUB : (h + 1) * SUB, :]
                    out_ref[i, j] = jnp.concatenate([head, tail], axis=0).astype(BF16)


def _route_body(replicas, requests, anchor_ref, dep_ref, out_ref, bit_ref):
    def note(s, carry):
        mask = _present(anchor_ref, s * requests, requests)
        bit_ref[s] = (~mask) & (mask + 1)
        return carry

    lax.fori_loop(0, replicas, note, 0)

    def place(d, carry):
        count = jnp.int32(0)
        for g in range(requests):
            a = anchor_ref[d * requests + g]
            s = a // requests
            bit = jnp.int32(1) << (a - s * requests)
            out_ref[d * MIG + count] = s * MIG + jnp.where(bit_ref[s] != bit, 1, 0)
            count = count + jnp.where(s != d, 1, 0)
        return carry

    lax.fori_loop(0, replicas, place, 0)


def _select_body(count, index_ref, in_ref, out_ref):
    for k in range(count):
        i = index_ref[k]
        out_ref[k // MIG, k % MIG] = in_ref[i // MIG, i % MIG]


def _expert_body(rep_ref, hidden_ref, weight_ref, keep_ref, send_ref, rows_ref):
    slots = hidden_ref.shape[1]
    cap = slots // 32
    r = rep_ref[0]

    @pl.when(pl.program_id(0) == 0)
    def _():
        row = lax.broadcasted_iota(jnp.int32, (slots, slots), 0)
        col = lax.broadcasted_iota(jnp.int32, (slots, slots), 1)
        zh, x, c = r // 8, (r // 2) % 4, r % 2
        to_c = (c + row // (slots // 2)) % 2
        to_x = (x + (row // (slots // 8)) % 4) % 4
        to_z = (zh + (row // cap) % 4) % 4
        want = ((to_z * 4 + to_x) * 2 + to_c) * cap + row % cap
        pick = jnp.where(want == col, 1.0, 0.0).astype(BF16)
        rows_ref[...] = jnp.dot(pick, hidden_ref[0], preferred_element_type=F32).astype(BF16)

    total = jnp.dot(rows_ref[...], weight_ref[0], preferred_element_type=F32)
    half = slots // 2
    keep_ref[...] = total[:half].astype(BF16)
    send_ref[...] = total[half:].astype(BF16)


def _fold2_body(keep_ref, got_ref, o0, o1, o2, o3):
    total = keep_ref[...].astype(F32) + got_ref[...].astype(F32)
    n = total.shape[0] // 4
    for k, o in enumerate((o0, o1, o2, o3)):
        o[...] = total[k * n : (k + 1) * n].astype(BF16)


def _fold4_body(a, b, c, d, o0, o1, o2, o3):
    total = (a[...].astype(F32) + b[...].astype(F32)) + (c[...].astype(F32) + d[...].astype(F32))
    n = total.shape[0] // 4
    for k, o in enumerate((o0, o1, o2, o3)):
        o[...] = total[k * n : (k + 1) * n].astype(BF16)


def _act_body(
    requests, rep_ref, anchor_ref, moved_ref, window_ref, conv_ref, taps_ref, bias_ref, mix_ref,
    e0, e1, e2, e3, out_ref, act_ref, win_ref, mixed_ref,
):
    blocks = conv_ref.shape[1] // LANES
    taps = window_ref.shape[1]
    first = 3 * blocks * 2
    for j in range(MIG):
        for b in range(blocks):
            win_ref[j, :, b * LANES : (b + 1) * LANES] = moved_ref[first + b, j].astype(F32)[SUB : 2 * SUB]
    weights = taps_ref[...]
    for g, (_, local, arrived, order) in enumerate(_slots(rep_ref, anchor_ref, requests)):
        mine = window_ref[local].astype(F32)
        other = win_ref[order][0:taps]
        window = jnp.where(arrived, other, mine)
        mixed_ref[g : g + 1, :] = jnp.sum(window * weights[0:taps], axis=0, keepdims=True)
    mixed = mixed_ref[...] + conv_ref[...].astype(F32) * weights[taps : taps + 1] + bias_ref[...]
    act = mixed * (1.0 / (1.0 + jnp.exp(-mixed)))
    act_ref[...] = act
    partial = jnp.dot(act.astype(BF16), mix_ref[...], preferred_element_type=F32)
    rank = 2 * LANES
    high = partial.astype(BF16).astype(F32)
    low = (partial - high)[:, rank:]
    fill = jnp.zeros((requests, LANES - 2 * low.shape[1]), F32)
    tail = jnp.concatenate([high[:, rank:], low, fill], axis=1)
    packed = jnp.concatenate([high[:, :rank], tail], axis=1)
    total = (e0[...].astype(F32) + e1[...].astype(F32)) + (e2[...].astype(F32) + e3[...].astype(F32))
    experts = out_ref.shape[0]
    width = total.shape[1] // experts
    empty = jnp.zeros((requests - 2 * total.shape[0], LANES), F32)
    for e in range(experts):
        left = total[:, e * width : e * width + LANES]
        right = total[:, e * width + LANES : (e + 1) * width]
        block = jnp.concatenate([left, right, empty], axis=0)
        out_ref[e] = jnp.concatenate([packed, block], axis=1).astype(BF16)


def _final_body(
    requests, states, rep_ref, anchor_ref, routes_ref, share_ref, sums_ref, moved_ref, act_ref, gate_ref, scan_ref,
    step_ref, bias_ref, decay_ref, skip_ref, gated_ref, mix_ref, arr_ref, count_ref, y_ref,
):
    experts = sums_ref.shape[0]
    blocks = act_ref.shape[1] // LANES
    rank = 2 * LANES
    for e in range(experts):
        count_ref[e] = 0
    row = lax.broadcasted_iota(jnp.int32, (requests, LANES), 0)
    col = lax.broadcasted_iota(jnp.int32, (requests, LANES), 1)
    share = jnp.zeros((requests, LANES), F32)
    cap = SUB // 2
    for t in range(requests):
        for k in range(routes_ref.shape[1]):
            e = routes_ref[t, k]
            place = count_ref[e]
            count_ref[e] = place + 1
            share = share + jnp.where((row == t) & (col == e * SUB + place), share_ref[t, k], 0.0)
    parts = []
    rest = share
    for _ in range(3):
        part = rest.astype(BF16)
        parts.append(part)
        rest = rest - part.astype(F32)
    outs = sums_ref[:, :, rank + LANES :].astype(F32)[:, 0:SUB].reshape(experts * SUB, LANES).astype(BF16)
    left = sum(jnp.dot(p, outs, preferred_element_type=F32) for p in reversed(parts))
    shifted = [pltpu.roll(p.astype(F32), cap, 1).astype(BF16) for p in parts]
    right = sum(jnp.dot(p, outs, preferred_element_type=F32) for p in reversed(shifted))
    mix_ref[...] = jnp.concatenate([left, right], axis=1).astype(BF16)
    projected = sums_ref[0, :, 0 : rank + LANES].astype(F32)
    for e in range(1, experts):
        projected = projected + sums_ref[e, :, 0 : rank + LANES].astype(F32)
    step = jnp.dot(projected[:, :rank].astype(BF16), step_ref[...], preferred_element_type=F32) + bias_ref[...]
    step = jnp.maximum(step, 0.0) + jnp.log1p(jnp.exp(-jnp.abs(step)))
    tail = projected[:, rank:]
    both = tail + pltpu.roll(tail, LANES - 2 * states, 1)
    columns = jnp.transpose(both)
    for j in range(MIG):
        for b in range(blocks):
            for h in range(states // SUB):
                i = b * (states // SUB) + h
                n = blocks * (states // SUB)
                high = moved_ref[i, j].astype(F32)[SUB : 2 * SUB]
                middle = moved_ref[n + i, j].astype(F32)[SUB : 2 * SUB]
                lowest = moved_ref[2 * n + i, j].astype(F32)[SUB : 2 * SUB]
                arr_ref[j, h * SUB : (h + 1) * SUB, b * LANES : (b + 1) * LANES] = high + (middle + lowest)
    rate = -jnp.exp(decay_ref[...])
    act = act_ref[...]
    flow = step * act
    for g, (_, local, arrived, order) in enumerate(_slots(rep_ref, anchor_ref, requests)):
        old = jnp.where(arrived, arr_ref[order], scan_ref[local])
        inflow = columns[0:states, g : g + 1]
        readout = columns[states : 2 * states, g : g + 1]
        state = jnp.exp(step[g : g + 1] * rate) * old + inflow * flow[g : g + 1]
        y_ref[g : g + 1, :] = jnp.sum(readout * state, axis=0, keepdims=True)
    gate = gate_ref[...].astype(F32)
    output = y_ref[...] + skip_ref[...] * act
    gated_ref[...] = (output * (gate * (1.0 / (1.0 + jnp.exp(-gate))))).astype(BF16)


def _attend_body(
    requests, rep_ref, anchor_ref, len_ref, table_ref, query_ref, key_ref, value_ref, pool_ref, moved_ref, dep_ref,
    out_ref, pages_ref, keys_ref, values_ref,
):
    head = key_ref.shape[1]
    heads = query_ref.shape[1] // head
    pool, _, _, page, _ = pool_ref.shape
    table = table_ref[...].astype(F32).astype(BF16)
    pages = table.shape[1]
    span = pages * page
    slots = _slots(rep_ref, anchor_ref, requests)
    row1 = lax.broadcasted_iota(jnp.int32, (requests, 1), 0)
    row = lax.broadcasted_iota(jnp.int32, (requests, requests), 0)
    col = lax.broadcasted_iota(jnp.int32, (requests, requests), 1)
    live = jnp.zeros((requests, 1), jnp.int32)
    order = jnp.full((requests, 1), -1, jnp.int32)
    pick = jnp.zeros((requests, requests), F32)
    live_of = [jnp.int32(0)] * MIG
    for g, (a, local, arrived, place) in enumerate(slots):
        length = len_ref[a]
        live = jnp.where(row1 == g, length, live)
        order = jnp.where((row1 == g) & arrived, place, order)
        pick = jnp.where((row == g) & (col == local), 1.0, pick)
        live_of = [jnp.where(arrived & (place == j), length, live_of[j]) for j in range(MIG)]
    mine = jnp.dot(pick.astype(BF16), table, preferred_element_type=F32).astype(jnp.int32)
    here = jnp.where(order < 0, live, 0)
    at = lax.broadcasted_iota(jnp.int32, (requests, pool * page), 1)
    which, token = at // page, at % page
    seen = jnp.zeros((requests, pool * page), jnp.bool_)
    for m in range(pages):
        seen = seen | ((mine[:, m : m + 1] == which) & (token + m * page < here))
    at = lax.broadcasted_iota(jnp.int32, (requests, MIG * span), 1)
    seen_moved = (at // span == order) & (at % span < live)
    down = lax.broadcasted_iota(jnp.int32, (span, head), 0)
    for j in range(MIG):
        for m in range(pages):
            for h in range(2):
                for c, ref in ((0, keys_ref), (1, values_ref)):
                    start = j * span + m * page + h * SUB
                    ref[start : start + SUB, :] = moved_ref[4 * m + 2 * c + h, j].astype(F32)[0:SUB]
        for c, ref in ((0, keys_ref), (1, values_ref)):
            block = ref[j * span : (j + 1) * span, :]
            pages_ref[j, 0, c] = jnp.where(down < live_of[j], block, 0.0).astype(BF16)
    moved_keys = keys_ref[...].astype(BF16)
    moved_values = values_ref[...].astype(BF16)
    pool_keys = pool_ref[:, 0, 0].reshape(pool * page, head)
    pool_values = pool_ref[:, 0, 1].reshape(pool * page, head)
    query = query_ref[...]
    queries = jnp.concatenate([query[:, h * head : (h + 1) * head] for h in range(heads)], axis=0)
    scale = 1.0 / math.sqrt(head)
    turn = (((1,), (1,)), ((), ()))
    scores = lax.dot_general(queries, pool_keys, turn, preferred_element_type=F32) * scale
    scores_moved = lax.dot_general(queries, moved_keys, turn, preferred_element_type=F32) * scale
    new_key = jnp.concatenate([key_ref[...].astype(F32)] * heads, axis=0)
    new_value = jnp.concatenate([value_ref[...].astype(F32)] * heads, axis=0)
    own = jnp.sum(queries.astype(F32) * new_key, axis=1, keepdims=True) * scale
    far = F32(-1e30)
    seen = jnp.concatenate([jnp.where(seen, 1.0, 0.0)] * heads, axis=0) > 0.5
    seen_moved = jnp.concatenate([jnp.where(seen_moved, 1.0, 0.0)] * heads, axis=0) > 0.5
    scores = jnp.where(seen, scores, far)
    scores_moved = jnp.where(seen_moved, scores_moved, far)
    highest = jnp.maximum(
        jnp.maximum(jnp.max(scores, axis=1, keepdims=True), jnp.max(scores_moved, axis=1, keepdims=True)), own
    )
    e_pool = jnp.exp(scores - highest)
    e_moved = jnp.exp(scores_moved - highest)
    e_own = jnp.exp(own - highest)
    total = jnp.sum(e_pool, axis=1, keepdims=True) + jnp.sum(e_moved, axis=1, keepdims=True) + e_own
    w_pool = (e_pool / total).astype(BF16)
    w_moved = (e_moved / total).astype(BF16)
    w_own = (e_own / total).astype(BF16).astype(F32)
    context = jnp.dot(w_pool, pool_values, preferred_element_type=F32)
    context = context + jnp.dot(w_moved, moved_values, preferred_element_type=F32) + w_own * new_value
    for h in range(heads):
        out_ref[:, h * head : (h + 1) * head] = context[h * requests : (h + 1) * requests].astype(BF16)


def per_device(
    query,
    new_key,
    new_value,
    page_pool,
    block_table,
    lengths,
    anchor,
    conv_input,
    gate_input,
    window_state,
    scan_state,
    filter_taps,
    filter_bias,
    mix_weight,
    step_weight,
    step_bias,
    log_decay,
    skip_gain,
    routes,
    route_weight,
    expert_hidden,
    down_weight,
):
    requests, channels = query.shape
    replicas = lax.axis_size("rep")
    experts = lax.axis_size("exp")
    rep = lax.axis_index("rep").astype(jnp.int32).reshape(1)
    states = log_decay.shape[0]
    head = new_key.shape[1]
    pages, page = block_table.shape[1], page_pool.shape[3]
    slots = expert_hidden.shape[1]
    features = down_weight.shape[2]
    piece = jax.ShapeDtypeStruct((replicas, MIG, 2 * SUB, LANES), BF16)

    packed = _call(
        lambda *refs: _pack_body(requests, *refs),
        "pack_leaving",
        piece,
        [_smem()] * 3 + [_vmem()] * 3,
        _vmem(),
        (rep, anchor, block_table, page_pool, window_state, scan_state),
        scratch=[pltpu.VMEM((SUB, channels), F32)],
        nbytes=1 << 20,
    )
    spread = lax.all_to_all(packed, "rep", split_axis=0, concat_axis=0, tiled=True)

    index = _call(
        lambda *refs: _route_body(replicas, requests, *refs),
        "route_pieces",
        jax.ShapeDtypeStruct((replicas * MIG + SUB,), jnp.int32),
        [_smem(), pl.BlockSpec(memory_space=pl.ANY)],
        _smem(),
        (anchor, packed),
        scratch=[pltpu.SMEM((replicas,), jnp.int32)],
        nbytes=8 << 20,
    )

    tile = features // 4
    keep, send = pl.pallas_call(
        _expert_body,
        name="expert_terms",
        grid=(features // tile,),
        out_shape=[jax.ShapeDtypeStruct((slots // 2, features), BF16)] * 2,
        in_specs=[
            _smem(),
            pl.BlockSpec((1, slots, expert_hidden.shape[2]), lambda i: (0, 0, 0)),
            pl.BlockSpec((1, down_weight.shape[1], tile), lambda i: (0, 0, i)),
        ],
        out_specs=[pl.BlockSpec((slots // 2, tile), lambda i: (0, i))] * 2,
        scratch_shapes=[pltpu.VMEM((slots, expert_hidden.shape[2]), BF16)],
        compiler_params=pltpu.CompilerParams(vmem_limit_bytes=32 * 1024 * 1024),
        cost_estimate=pl.CostEstimate(flops=2 * slots * 384 * features, bytes_accessed=5 << 20, transcendentals=0),
    )(rep, expert_hidden, down_weight)

    def at(z, x, c):
        return (z * 4 + x) * 2 + c

    every = [(z, x, c) for z in range(4) for x in range(4) for c in range(2)]
    got = lax.ppermute(send, "rep", [(at(z, x, c), at(z, x, 1 - c)) for z, x, c in every])
    part = jax.ShapeDtypeStruct((slots // 8, features), BF16)
    by_x = _call(_fold2_body, "fold_cores", [part] * 4, [_vmem()] * 2, [_vmem()] * 4, (keep, got), nbytes=2 << 20)
    came = [by_x[0]] + [
        lax.ppermute(by_x[k], "rep", [(at(z, x, c), at(z, (x + k) % 4, c)) for z, x, c in every]) for k in (2, 1, 3)
    ]
    part = jax.ShapeDtypeStruct((slots // 32, features), BF16)
    by_z = _call(_fold4_body, "fold_x", [part] * 4, [_vmem()] * 4, [_vmem()] * 4, came, nbytes=1 << 20)
    own = [by_z[0]] + [
        lax.ppermute(by_z[k], "rep", [(at(z, x, c), at((z + k) % 4, x, c)) for z, x, c in every]) for k in (2, 1, 3)
    ]

    onward = _call(
        lambda *refs: _select_body(replicas * MIG, *refs),
        "select_pieces",
        piece,
        [_smem(), _vmem()],
        _vmem(),
        (index, spread),
        nbytes=1 << 19,
    )
    moved = lax.all_to_all(onward, "rep", split_axis=0, concat_axis=0, tiled=True)

    sums, act = _call(
        lambda *refs: _act_body(requests, *refs),
        "filter_and_project",
        [
            jax.ShapeDtypeStruct((experts, requests, 4 * LANES), BF16),
            jax.ShapeDtypeStruct((requests, channels), F32),
        ],
        [_smem()] * 2 + [_vmem()] * 10,
        [_vmem()] * 2,
        (rep, anchor, moved, window_state, conv_input, filter_taps, filter_bias.reshape(1, channels), mix_weight, *own),
        scratch=[pltpu.VMEM((MIG, SUB, channels), F32), pltpu.VMEM((requests, channels), F32)],
        nbytes=1 << 20,
    )
    sums_all = lax.all_to_all(sums, "exp", split_axis=0, concat_axis=0, tiled=True)

    attended, pages_out = _call(
        lambda *refs: _attend_body(requests, *refs),
        "attend",
        [
            jax.ShapeDtypeStruct((requests, channels), BF16),
            jax.ShapeDtypeStruct((MIG, 1, 2, pages * page, head), BF16),
        ],
        [_smem()] * 3 + [_vmem()] * 6 + [pl.BlockSpec(memory_space=pl.ANY)],
        [_vmem()] * 2,
        (rep, anchor, lengths, block_table, query, new_key, new_value, page_pool, moved, act),
        scratch=[pltpu.VMEM((MIG * pages * page, head), F32)] * 2,
        nbytes=4 << 20,
    )

    gated, mixed = _call(
        lambda *refs: _final_body(requests, states, *refs),
        "update_state",
        [
            jax.ShapeDtypeStruct((requests, channels), BF16),
            jax.ShapeDtypeStruct((requests, features // experts), BF16),
        ],
        [_smem()] * 4 + [_vmem()] * 9,
        [_vmem()] * 2,
        (
            rep, anchor, routes, route_weight, sums_all, moved, act, gate_input, scan_state, step_weight,
            step_bias.reshape(1, channels), log_decay, skip_gain.reshape(1, channels),
        ),
        scratch=[
            pltpu.VMEM((MIG, states, channels), F32),
            pltpu.SMEM((experts,), jnp.int32),
            pltpu.VMEM((requests, channels), F32),
        ],
        nbytes=1 << 20,
    )
    return (attended, pages_out, gated, mixed)


def solution(mesh):
    placed = (
        P("rep", "exp"),
        P("rep", "exp"),
        P("rep", "exp"),
        P("rep", "exp", None, None, None),
        P("rep", None),
        P(),
        P(),
        P("rep", "exp"),
        P("rep", "exp"),
        P("rep", None, "exp"),
        P("rep", None, "exp"),
        P(None, "exp"),
        P("exp"),
        P("exp", None),
        P(None, "exp"),
        P("exp"),
        P(None, "exp"),
        P("exp"),
        P("rep", None),
        P("rep", None),
        P("exp", None, "rep"),
        P("exp", "rep", None),
    )
    return jax.shard_map(
        per_device,
        mesh=mesh,
        in_specs=placed,
        out_specs=(
            P("rep", "exp"),
            P("rep", "exp", None, None, None),
            P("rep", "exp"),
            P("rep", "exp"),
        ),
        check_vma=False,
    )
```

```python
import math

import jax
import jax.numpy as jnp
from jax import lax
from jax.experimental import pallas as pl
from jax.experimental.pallas import tpu as pltpu
from jax.sharding import PartitionSpec as P

MIG = 2
LANES = 128
SUB = 8
F32 = jnp.float32
BF16 = jnp.bfloat16


def _smem():
    return pl.BlockSpec(memory_space=pltpu.SMEM)


def _vmem():
    return pl.BlockSpec(memory_space=pltpu.VMEM)


def _any():
    return pl.BlockSpec(memory_space=pl.ANY)


def _hbm():
    return pl.BlockSpec(memory_space=pltpu.HBM)


def _shape(shape, dtype):
    return jax.ShapeDtypeStruct(shape, dtype)


def _call(body, name, out_shape, ins, outs, args, scratch=(), us=1.0, room=32):
    return pl.pallas_call(
        body,
        name=name,
        out_shape=out_shape,
        in_specs=ins,
        out_specs=outs,
        scratch_shapes=list(scratch),
        compiler_params=pltpu.CompilerParams(vmem_limit_bytes=room * 1024 * 1024),
        cost_estimate=pl.CostEstimate(flops=0, bytes_accessed=int(us * 3.5e6), transcendentals=0),
    )(*args)


def _present(anchor_ref, base, requests):
    mask = jnp.int32(0)
    for g in range(requests):
        a = anchor_ref[base + g] - base
        inside = (a >= 0) & (a < requests)
        mask = mask | jnp.where(inside, jnp.int32(1) << jnp.clip(a, 0, requests - 1), 0)
    return mask


def _slots(rep_ref, anchor_ref, requests):
    base = rep_ref[0] * requests
    count = jnp.int32(0)
    found = []
    for g in range(requests):
        a = anchor_ref[base + g]
        local = a - base
        arrived = (local < 0) | (local >= requests)
        found.append((a, jnp.clip(local, 0, requests - 1), arrived, jnp.minimum(count, MIG - 1)))
        count = count + jnp.where(arrived, 1, 0)
    return found


def _pack_body(
    requests, rep_ref, anchor_ref, table_ref, pool_ref, window_ref, scan_ref, out_ref,
    scans_ref, pages_ref, win_ref, sems,
):
    pages = table_ref.shape[0]
    taps, _, channels = window_ref.shape
    blocks = channels // LANES
    whole = pltpu.make_async_copy(window_ref, win_ref, sems.at[0])
    whole.start()
    base = rep_ref[0] * requests
    mask = _present(anchor_ref, base, requests)
    first, second = jnp.int32(0), jnp.int32(0)
    for o in reversed(range(requests)):
        leaves = ((mask >> o) & 1) == 0
        second = jnp.where(leaves, first, second)
        first = jnp.where(leaves, o, first)
    leaving = (first, second)
    copies = [whole]
    for j, o in enumerate(leaving):
        copies.append(pltpu.make_async_copy(scan_ref.at[o], scans_ref.at[j], sems.at[len(copies)]))
        copies[-1].start()
        for m in range(pages):
            copies.append(
                pltpu.make_async_copy(pool_ref.at[table_ref[m, o], 0], pages_ref.at[j, m], sems.at[len(copies)])
            )
            copies[-1].start()
    for copy in copies:
        copy.wait()
    row = lax.broadcasted_iota(jnp.int32, (requests, channels), 0)
    for j, o in enumerate(leaving):
        scan = scans_ref[j]
        high = scan.astype(BF16).astype(F32)
        rest = scan - high
        middle = rest.astype(BF16).astype(F32)
        low = rest - middle
        tails = []
        for part in (high, middle, low):
            for b in range(blocks):
                for h in range(scan.shape[0] // SUB):
                    tails.append(part[h * SUB : (h + 1) * SUB, b * LANES : (b + 1) * LANES])
        lines = [
            jnp.sum(jnp.where(row == o, win_ref[t].astype(F32), 0.0), axis=0, keepdims=True) for t in range(taps)
        ]
        win = jnp.concatenate([*lines, jnp.zeros((SUB - taps, channels), F32)], axis=0)
        for b in range(blocks):
            tails.append(win[:, b * LANES : (b + 1) * LANES])
        for m in range(pages):
            page = pages_ref[j, m].astype(F32)
            for c in range(2):
                for h in range(2):
                    i = 4 * m + 2 * c + h
                    tail = tails[i] if i < len(tails) else jnp.zeros((SUB, LANES), F32)
                    head = page[c, h * SUB : (h + 1) * SUB, :]
                    out_ref[i, j] = jnp.concatenate([head, tail], axis=0).astype(BF16)


def _route_body(requests, anchor_ref, dep_ref, out_ref):
    anchors = anchor_ref[...]
    replicas = anchors.shape[0]
    home = lax.broadcasted_iota(jnp.int32, anchors.shape, 0)
    place = lax.broadcasted_iota(jnp.int32, anchors.shape, 1).astype(F32)
    source = anchors // requests
    bit = (jnp.int32(1) << (anchors - source * requests)).astype(F32)
    arrived = source != home
    staying = jnp.sum(jnp.where(arrived, 0.0, bit), axis=1, keepdims=True).astype(jnp.int32)
    first = ((~staying) & (staying + 1)).astype(F32)
    lowest = jnp.zeros(anchors.shape, F32)
    for s in range(replicas):
        lowest = jnp.where(source == s, first[s : s + 1], lowest)
    item = (source * MIG).astype(F32) + jnp.where(lowest != bit, 1.0, 0.0)
    early = jnp.min(jnp.where(arrived, place, 99.0), axis=1, keepdims=True)
    one = jnp.sum(jnp.where(arrived & (place == early), item, 0.0), axis=1, keepdims=True)
    two = jnp.sum(jnp.where(arrived & (place != early), item, 0.0), axis=1, keepdims=True)
    lane = lax.broadcasted_iota(jnp.int32, out_ref.shape, 1)
    out_ref[...] = jnp.where(lane == 0, one, jnp.where(lane == 1, two, 0.0)).astype(jnp.int32)


def _own_bits(r):
    c, x = r % 2, (r // 2) % 4
    return (x // 2) * 4 + ((x // 2) ^ (x % 2)) * 2 + c


def _expert_body(rep_ref, hidden_ref, weight_ref, dep_ref, keep_ref, send_ref):
    width = weight_ref.shape[2] // 8
    own = _own_bits(rep_ref[0])
    hidden = hidden_ref[0]
    for p in (4, 5, 6, 7, 0, 1, 2, 3):
        block = own ^ ((p % 2) * 4 + (p // 2 % 2) * 2 + p // 4)
        columns = pl.ds(pl.multiple_of(block * width, width), width)
        total = jnp.dot(hidden, weight_ref[0, :, columns], preferred_element_type=F32)
        at = slice(p % 4 * width, (p % 4 + 1) * width)
        if p < 4:
            keep_ref[:, at] = total
        else:
            send_ref[:, at] = total.astype(BF16)


def _fold_body(keep_ref, got_ref, next_ref, send_ref):
    half = next_ref.shape[1]
    next_ref[...] = keep_ref[:, :half] + got_ref[:, :half].astype(F32)
    send_ref[...] = (keep_ref[:, half:] + got_ref[:, half:].astype(F32)).astype(BF16)


def _select_body(index_ref, in_ref, keep_ref, got_ref, out_ref):
    replicas = out_ref.shape[0]
    cap = keep_ref.shape[0] // replicas
    blocks = keep_ref.shape[1] // LANES
    for d in range(replicas):
        for j in range(MIG):
            i = index_ref[d, j]
            out_ref[d, j] = in_ref[i // MIG, i % MIG]
    total = keep_ref[...] + got_ref[...].astype(F32)
    for d in range(replicas):
        rows = total[d * cap : (d + 1) * cap]
        out_ref[d, MIG] = jnp.concatenate(
            [rows[:, b * LANES : (b + 1) * LANES] for b in range(blocks)], axis=0
        ).astype(BF16)


def _local_body(
    requests, rep_ref, anchor_ref, window_ref, conv_ref, taps_ref, bias_ref, mix_ref, dep_ref,
    base_ref, which_ref, taps_out_ref, mix_out_ref,
):
    taps = window_ref.shape[0]
    weights = taps_ref[...]
    row = lax.broadcasted_iota(jnp.int32, (requests, requests), 0)
    col = lax.broadcasted_iota(jnp.int32, (requests, requests), 1)
    row_w = lax.broadcasted_iota(jnp.int32, which_ref.shape, 0)
    col_w = lax.broadcasted_iota(jnp.int32, which_ref.shape, 1)
    pick = jnp.zeros((requests, requests), F32)
    which = jnp.zeros(which_ref.shape, F32)
    for g, (_, local, arrived, order) in enumerate(_slots(rep_ref, anchor_ref, requests)):
        pick = jnp.where((row == g) & (col == local) & ~arrived, 1.0, pick)
        which = jnp.where((row_w == g) & (col_w == order) & arrived, 1.0, which)
    pick = pick.astype(BF16)
    mixed = conv_ref[...].astype(F32) * weights[taps : taps + 1] + bias_ref[...]
    for t in range(taps):
        mixed = mixed + jnp.dot(pick, window_ref[t], preferred_element_type=F32) * weights[t : t + 1]
    base_ref[...] = mixed
    which_ref[...] = which
    taps_out_ref[...] = weights
    mix_out_ref[...] = mix_ref[...]


def _act_body(moved_ref, base_ref, which_ref, taps_ref, mix_ref, out_ref, act_ref, win_ref):
    requests, channels = base_ref.shape
    blocks = channels // LANES
    first = 3 * blocks * 2
    weights = taps_ref[...]
    taps = weights.shape[0] - 1
    mixed = base_ref[...]
    for j in range(MIG):
        for b in range(blocks):
            win_ref[:, b * LANES : (b + 1) * LANES] = moved_ref[first + b, j].astype(F32)[SUB : 2 * SUB]
        line = jnp.sum(win_ref[0:taps, :] * weights[0:taps], axis=0, keepdims=True)
        mixed = mixed + which_ref[:, j : j + 1] * line
    act = mixed * (1.0 / (1.0 + jnp.exp(-mixed)))
    act_ref[...] = act
    turn = (((1,), (1,)), ((), ()))
    partial = lax.dot_general(act.astype(BF16), mix_ref[...], turn, preferred_element_type=F32)
    rank = 2 * LANES
    high = partial.astype(BF16).astype(F32)
    low = (partial - high)[:, rank:]
    fill = jnp.zeros((requests, LANES - 2 * low.shape[1]), F32)
    packed = jnp.concatenate([high[:, :rank], high[:, rank:], low, fill], axis=1)
    experts = out_ref.shape[0]
    replicas = moved_ref.shape[0]
    sums = {}
    for r in range(8):
        total = moved_ref[r, MIG].astype(F32)
        for z in range(1, replicas // 8):
            total = total + moved_ref[z * 8 + r, MIG].astype(F32)
        sums[_own_bits(r)] = total
    empty = jnp.zeros((requests - SUB, LANES), F32)
    for e in range(experts):
        block = sums[e // 2][e % 2 * SUB : (e % 2 + 1) * SUB]
        block = jnp.concatenate([block, empty], axis=0)
        out_ref[e] = jnp.concatenate([packed, block], axis=1).astype(BF16)


def _ready_body(
    requests, states, rep_ref, anchor_ref, routes_ref, share_ref, moved_ref, act_ref, gate_ref, scan_ref, step_ref,
    bias_ref, decay_ref, skip_ref, old_ref, rate_ref, gate_out_ref, skip_out_ref, step_out_ref, bias_out_ref,
    share_out_ref, arr_ref, count_ref,
):
    channels = act_ref.shape[1]
    blocks = channels // LANES
    halves = states // SUB
    n = blocks * halves
    for j in range(MIG):
        for b in range(blocks):
            for h in range(halves):
                i = b * halves + h
                high = moved_ref[i, j].astype(F32)[SUB : 2 * SUB]
                middle = moved_ref[n + i, j].astype(F32)[SUB : 2 * SUB]
                lowest = moved_ref[2 * n + i, j].astype(F32)[SUB : 2 * SUB]
                arr_ref[j, h * SUB : (h + 1) * SUB, b * LANES : (b + 1) * LANES] = high + (middle + lowest)
    for g, (_, local, arrived, order) in enumerate(_slots(rep_ref, anchor_ref, requests)):
        old_ref[g] = jnp.where(arrived, arr_ref[order], scan_ref[local])
    rate_ref[...] = -jnp.exp(decay_ref[...])
    gate = gate_ref[...].astype(F32)
    gate_out_ref[...] = gate * (1.0 / (1.0 + jnp.exp(-gate)))
    skip_out_ref[...] = skip_ref[...] * act_ref[...]
    step_out_ref[...] = step_ref[...]
    bias_out_ref[...] = jnp.broadcast_to(bias_ref[...], bias_out_ref.shape)
    for e in range(count_ref.shape[0]):
        count_ref[e] = 0
    row = lax.broadcasted_iota(jnp.int32, (requests, LANES), 0)
    col = lax.broadcasted_iota(jnp.int32, (requests, LANES), 1)
    share = jnp.zeros((requests, LANES), F32)
    for t in range(requests):
        for k in range(routes_ref.shape[0]):
            e = routes_ref[k, t]
            place = count_ref[e]
            count_ref[e] = place + 1
            share = share + jnp.where((row == t) & (col == e * SUB + place), share_ref[k, t], 0.0)
    share_out_ref[...] = share


def _final_body(
    states, sums_ref, act_ref, old_ref, rate_ref, gate_ref, skip_ref, step_ref, bias_ref, share_ref,
    gated_ref, mix_ref, y_ref,
):
    experts, requests, _ = sums_ref.shape
    rank = 2 * LANES
    projected = sums_ref[0, :, 0 : rank + LANES].astype(F32)
    for e in range(1, experts):
        projected = projected + sums_ref[e, :, 0 : rank + LANES].astype(F32)
    step = jnp.dot(projected[:, :rank].astype(BF16), step_ref[...], preferred_element_type=F32) + bias_ref[0:1]
    step = jnp.maximum(step, 0.0) + jnp.log1p(jnp.exp(-jnp.abs(step)))
    tail = projected[:, rank:]
    columns = jnp.transpose(tail + pltpu.roll(tail, LANES - 2 * states, 1))
    rest = share_ref[...]
    parts = []
    for _ in range(3):
        part = rest.astype(BF16).astype(F32)
        parts.append(part)
        rest = rest - part
    outs = sums_ref[:, :, rank + LANES :].astype(F32)[:, 0:SUB].reshape(experts * SUB, LANES).astype(BF16)
    both = jnp.concatenate([*parts, *(pltpu.roll(p, SUB // 2, 1) for p in parts)], axis=0).astype(BF16)
    terms = jnp.dot(both, outs, preferred_element_type=F32)
    halves = [
        sum(terms[(3 * h + i) * requests : (3 * h + i + 1) * requests] for i in reversed(range(3))) for h in range(2)
    ]
    mix_ref[...] = jnp.concatenate(halves, axis=1).astype(BF16)
    rate = rate_ref[...]
    flow = step * act_ref[...]
    for g in range(requests):
        inflow = columns[0:states, g : g + 1]
        readout = columns[states : 2 * states, g : g + 1]
        state = jnp.exp(step[g : g + 1] * rate) * old_ref[g] + inflow * flow[g : g + 1]
        y_ref[g : g + 1, :] = jnp.sum(readout * state, axis=0, keepdims=True)
    gated_ref[...] = ((y_ref[...] + skip_ref[...]) * gate_ref[...]).astype(BF16)


def _attend_body(
    requests, rep_ref, anchor_ref, len_ref, table_ref, query_ref, key_ref, value_ref, pool_ref, moved_ref, dep_ref,
    out_ref, pages_ref, keys_ref, values_ref,
):
    turn = (((1,), (1,)), ((), ()))
    head = key_ref.shape[1]
    heads = query_ref.shape[1] // head
    pool, _, _, page, _ = pool_ref.shape
    table = table_ref[...].astype(F32).astype(BF16)
    pages = table.shape[0]
    span = pages * page
    slots = _slots(rep_ref, anchor_ref, requests)
    row1 = lax.broadcasted_iota(jnp.int32, (requests, 1), 0)
    row = lax.broadcasted_iota(jnp.int32, (requests, requests), 0)
    col = lax.broadcasted_iota(jnp.int32, (requests, requests), 1)
    live = jnp.zeros((requests, 1), jnp.int32)
    order = jnp.full((requests, 1), -1, jnp.int32)
    pick = jnp.zeros((requests, requests), F32)
    live_of = [jnp.int32(0)] * MIG
    for g, (a, local, arrived, place) in enumerate(slots):
        length = len_ref[a]
        live = jnp.where(row1 == g, length, live)
        order = jnp.where((row1 == g) & arrived, place, order)
        pick = jnp.where((row == g) & (col == local), 1.0, pick)
        live_of = [jnp.where(arrived & (place == j), length, live_of[j]) for j in range(MIG)]
    mine = lax.dot_general(pick.astype(BF16), table, turn, preferred_element_type=F32).astype(jnp.int32)
    here = jnp.where(order < 0, live, 0)
    at = lax.broadcasted_iota(jnp.int32, (requests, pool * page), 1)
    which, token = at // page, at % page
    seen = jnp.zeros((requests, pool * page), jnp.bool_)
    for m in range(pages):
        seen = seen | ((mine[:, m : m + 1] == which) & (token + m * page < here))
    at = lax.broadcasted_iota(jnp.int32, (requests, MIG * span), 1)
    seen_moved = (at // span == order) & (at % span < live)
    down = lax.broadcasted_iota(jnp.int32, (span, head), 0)
    for j in range(MIG):
        for m in range(pages):
            for h in range(2):
                for c, ref in ((0, keys_ref), (1, values_ref)):
                    start = j * span + m * page + h * SUB
                    ref[start : start + SUB, :] = moved_ref[4 * m + 2 * c + h, j].astype(F32)[0:SUB]
        for c, ref in ((0, keys_ref), (1, values_ref)):
            block = ref[j * span : (j + 1) * span, :]
            pages_ref[j, 0, c] = jnp.where(down < live_of[j], block, 0.0).astype(BF16)
    moved_keys = keys_ref[...].astype(BF16)
    moved_values = values_ref[...].astype(BF16)
    pool_keys = pool_ref[:, 0, 0].reshape(pool * page, head)
    pool_values = pool_ref[:, 0, 1].reshape(pool * page, head)
    query = query_ref[...]
    queries = jnp.concatenate([query[:, h * head : (h + 1) * head] for h in range(heads)], axis=0)
    scale = 1.0 / math.sqrt(head)
    scores = lax.dot_general(queries, pool_keys, turn, preferred_element_type=F32) * scale
    scores_moved = lax.dot_general(queries, moved_keys, turn, preferred_element_type=F32) * scale
    new_key = jnp.concatenate([key_ref[...].astype(F32)] * heads, axis=0)
    new_value = jnp.concatenate([value_ref[...].astype(F32)] * heads, axis=0)
    own = jnp.sum(queries.astype(F32) * new_key, axis=1, keepdims=True) * scale
    far = F32(-1e30)
    seen = jnp.concatenate([jnp.where(seen, 1.0, 0.0)] * heads, axis=0) > 0.5
    seen_moved = jnp.concatenate([jnp.where(seen_moved, 1.0, 0.0)] * heads, axis=0) > 0.5
    scores = jnp.where(seen, scores, far)
    scores_moved = jnp.where(seen_moved, scores_moved, far)
    highest = jnp.maximum(
        jnp.maximum(jnp.max(scores, axis=1, keepdims=True), jnp.max(scores_moved, axis=1, keepdims=True)), own
    )
    e_pool = jnp.exp(scores - highest)
    e_moved = jnp.exp(scores_moved - highest)
    e_own = jnp.exp(own - highest)
    total = jnp.sum(e_pool, axis=1, keepdims=True) + jnp.sum(e_moved, axis=1, keepdims=True) + e_own
    w_pool = (e_pool / total).astype(BF16)
    w_moved = (e_moved / total).astype(BF16)
    w_own = (e_own / total).astype(BF16).astype(F32)
    context = jnp.dot(w_pool, pool_values, preferred_element_type=F32)
    context = context + jnp.dot(w_moved, moved_values, preferred_element_type=F32) + w_own * new_value
    for h in range(heads):
        out_ref[:, h * head : (h + 1) * head] = context[h * requests : (h + 1) * requests].astype(BF16)


def per_device(
    query,
    new_key,
    new_value,
    page_pool,
    block_table,
    lengths,
    anchor,
    conv_input,
    gate_input,
    window_state,
    scan_state,
    filter_taps,
    filter_bias,
    mix_weight,
    step_weight,
    step_bias,
    log_decay,
    skip_gain,
    routes,
    route_weight,
    expert_hidden,
    down_weight,
):
    requests, channels = query.shape
    replicas = lax.axis_size("rep")
    experts = lax.axis_size("exp")
    rep = lax.axis_index("rep").astype(jnp.int32).reshape(1)
    states = log_decay.shape[0]
    head = new_key.shape[1]
    pages, page = block_table.shape[1], page_pool.shape[3]
    slots = expert_hidden.shape[1]
    features = down_weight.shape[2]
    table = block_table.T
    window = jnp.transpose(window_state, (1, 0, 2))

    def piece(tiles):
        return _shape((replicas, tiles, 2 * SUB, LANES), BF16)

    packed = _call(
        lambda *refs: _pack_body(requests, *refs),
        "pack_leaving",
        piece(MIG),
        [_smem()] * 3 + [_hbm()] * 3,
        _vmem(),
        (rep, anchor, table, page_pool, window, scan_state),
        scratch=[
            pltpu.VMEM((MIG, states, channels), F32),
            pltpu.VMEM((MIG, pages, 2, page, head), BF16),
            pltpu.VMEM(window.shape, BF16),
            pltpu.SemaphoreType.DMA((1 + MIG * (1 + pages),)),
        ],
        us=1.5,
        room=60,
    )
    spread = lax.all_to_all(packed, "rep", split_axis=0, concat_axis=0, tiled=True)

    keep, send = _call(
        _expert_body,
        "expert_terms",
        [_shape((slots, features // 2), F32), _shape((slots, features // 2), BF16)],
        [_smem()] + [_vmem()] * 2 + [_any()],
        [_vmem()] * 2,
        (rep, expert_hidden, down_weight, packed),
        us=2,
    )

    def at(z, x, c):
        return (z * 4 + x) * 2 + c

    every = [(z, x, c) for z in range(4) for x in range(4) for c in range(2)]
    got = lax.ppermute(send, "rep", [(at(z, x, c), at(z, x, 1 - c)) for z, x, c in every])
    for part, partner in ((4, (1, 0, 3, 2)), (8, (3, 2, 1, 0))):
        keep, send = _call(
            _fold_body,
            "fold",
            [_shape((slots, features // part), F32), _shape((slots, features // part), BF16)],
            [_vmem()] * 2,
            [_vmem()] * 2,
            (keep, got),
            us=0.5,
        )
        got = lax.ppermute(send, "rep", [(at(z, x, c), at(z, partner[x], c)) for z, x, c in every])

    index = _call(
        lambda *refs: _route_body(requests, *refs),
        "route_pieces",
        _shape((replicas, LANES), jnp.int32),
        [_vmem(), _any()],
        _vmem(),
        (anchor.reshape(replicas, requests), packed),
        us=1,
    )
    onward = _call(
        _select_body,
        "select_pieces",
        piece(MIG + 1),
        [_smem()] + [_vmem()] * 3,
        _vmem(),
        (index, spread, keep, got),
        us=1,
    )
    moved = lax.all_to_all(onward, "rep", split_axis=0, concat_axis=0, tiled=True)

    base, which, taps, mix = _call(
        lambda *refs: _local_body(requests, *refs),
        "filter_local",
        [
            _shape((requests, channels), F32),
            _shape((requests, LANES), F32),
            _shape(filter_taps.shape, F32),
            _shape(mix_weight.shape[::-1], BF16),
        ],
        [_smem()] * 2 + [_vmem()] * 5 + [_any()],
        [_vmem()] * 4,
        (rep, anchor, window, conv_input, filter_taps, filter_bias.reshape(1, channels), mix_weight.T, onward),
        us=1.5,
    )
    sums, act = _call(
        _act_body,
        "filter_and_project",
        [_shape((experts, requests, 4 * LANES), BF16), _shape((requests, channels), F32)],
        [_vmem()] * 5,
        [_vmem()] * 2,
        (moved, base, which, taps, mix),
        scratch=[pltpu.VMEM((SUB, channels), F32)],
        us=1.5,
    )
    sums_all = lax.all_to_all(sums, "exp", split_axis=0, concat_axis=0, tiled=True)

    attended, pages_out = _call(
        lambda *refs: _attend_body(requests, *refs),
        "attend",
        [_shape((requests, channels), BF16), _shape((MIG, 1, 2, pages * page, head), BF16)],
        [_smem()] * 3 + [_vmem()] * 6 + [_any()],
        [_vmem()] * 2,
        (rep, anchor, lengths, table, query, new_key, new_value, page_pool, moved, act),
        scratch=[pltpu.VMEM((MIG * pages * page, head), F32)] * 2,
        us=2,
    )
    ready = _call(
        lambda *refs: _ready_body(requests, states, *refs),
        "ready_state",
        [
            _shape((requests, states, channels), F32),
            _shape((states, channels), F32),
            _shape((requests, channels), F32),
            _shape((requests, channels), F32),
            _shape(step_weight.shape, BF16),
            _shape((SUB, channels), F32),
            _shape((requests, LANES), F32),
        ],
        [_smem()] * 4 + [_vmem()] * 8,
        [_vmem()] * 7,
        (
            rep, anchor, routes.T, route_weight.T, moved, act, gate_input, scan_state, step_weight,
            step_bias.reshape(1, channels), log_decay, skip_gain.reshape(1, channels),
        ),
        scratch=[pltpu.VMEM((MIG, states, channels), F32), pltpu.SMEM((experts,), jnp.int32)],
        us=2,
    )
    gated, mixed = _call(
        lambda *refs: _final_body(states, *refs),
        "update_state",
        [_shape((requests, channels), BF16), _shape((requests, features // experts), BF16)],
        [_vmem()] * 9,
        [_vmem()] * 2,
        (sums_all, act, *ready),
        scratch=[pltpu.VMEM((requests, channels), F32)],
        us=2,
    )
    return (attended, pages_out, gated, mixed)


def solution(mesh):
    placed = (
        P("rep", "exp"),
        P("rep", "exp"),
        P("rep", "exp"),
        P("rep", "exp", None, None, None),
        P("rep", None),
        P(),
        P(),
        P("rep", "exp"),
        P("rep", "exp"),
        P("rep", None, "exp"),
        P("rep", None, "exp"),
        P(None, "exp"),
        P("exp"),
        P("exp", None),
        P(None, "exp"),
        P("exp"),
        P(None, "exp"),
        P("exp"),
        P("rep", None),
        P("rep", None),
        P("exp", None, "rep"),
        P("exp", "rep", None),
    )
    return jax.shard_map(
        per_device,
        mesh=mesh,
        in_specs=placed,
        out_specs=(
            P("rep", "exp"),
            P("rep", "exp", None, None, None),
            P("rep", "exp"),
            P("rep", "exp"),
        ),
        check_vma=False,
    )
```

```python
import math

import jax
import jax.numpy as jnp
from jax import lax
from jax.experimental import pallas as pl
from jax.experimental.pallas import tpu as pltpu
from jax.sharding import PartitionSpec as P

MIG = 2
LANES = 128
SUB = 8
ROWS = 16
PLANE = 8
F32 = jnp.float32
BF16 = jnp.bfloat16


def _smem():
    return pl.BlockSpec(memory_space=pltpu.SMEM)


def _vmem():
    return pl.BlockSpec(memory_space=pltpu.VMEM)


def _any():
    return pl.BlockSpec(memory_space=pl.ANY)


def _hbm():
    return pl.BlockSpec(memory_space=pltpu.HBM)


def _shape(shape, dtype):
    return jax.ShapeDtypeStruct(shape, dtype)


def _call(body, name, out_shape, ins, outs, args, scratch=(), us=1.0, room=32):
    return pl.pallas_call(
        body,
        name=name,
        out_shape=out_shape,
        in_specs=ins,
        out_specs=outs,
        scratch_shapes=list(scratch),
        compiler_params=pltpu.CompilerParams(vmem_limit_bytes=room * 1024 * 1024),
        cost_estimate=pl.CostEstimate(flops=0, bytes_accessed=int(us * 3.5e6), transcendentals=0),
    )(*args)


def _present(anchor_ref, base, requests):
    mask = jnp.int32(0)
    for g in range(requests):
        a = anchor_ref[base + g] - base
        inside = (a >= 0) & (a < requests)
        mask = mask | jnp.where(inside, jnp.int32(1) << jnp.clip(a, 0, requests - 1), 0)
    return mask


def _slots(rep_ref, anchor_ref, requests):
    base = rep_ref[0] * requests
    count = jnp.int32(0)
    found = []
    for g in range(requests):
        a = anchor_ref[base + g]
        local = a - base
        arrived = (local < 0) | (local >= requests)
        found.append((a, jnp.clip(local, 0, requests - 1), arrived, jnp.minimum(count, MIG - 1)))
        count = count + jnp.where(arrived, 1, 0)
    return found


def _levels(slots, requests):
    found = [jnp.int32(0)] * MIG
    for a, _, arrived, order in slots:
        found = [jnp.where(arrived & (order == j), a // (requests * PLANE), found[j]) for j in range(MIG)]
    return found


def _pack_body(
    requests, rep_ref, anchor_ref, table_ref, pool_ref, window_ref, scan_ref, hidden_ref, weight_ref, out_ref, token_ref,
    scans_ref, pages_ref, win_ref, rows_ref, blocks_ref, sems,
):
    pages = table_ref.shape[0]
    taps, _, channels = window_ref.shape
    blocks = channels // LANES
    plane = out_ref.shape[0]
    width = weight_ref.shape[2] // plane
    copies = [
        pltpu.make_async_copy(hidden_ref.at[0], rows_ref, sems.at[0]),
        pltpu.make_async_copy(window_ref, win_ref, sems.at[1]),
    ]
    for copy in copies:
        copy.start()
    base = rep_ref[0] * requests
    mask = _present(anchor_ref, base, requests)
    first, second = jnp.int32(0), jnp.int32(0)
    for o in reversed(range(requests)):
        leaves = ((mask >> o) & 1) == 0
        second = jnp.where(leaves, first, second)
        first = jnp.where(leaves, o, first)
    leaving = (first, second)
    for j, o in enumerate(leaving):
        copies.append(pltpu.make_async_copy(scan_ref.at[o], scans_ref.at[j], sems.at[len(copies)]))
        copies[-1].start()
        for m in range(pages):
            copies.append(
                pltpu.make_async_copy(pool_ref.at[table_ref[m, o], 0], pages_ref.at[j, m], sems.at[len(copies)])
            )
            copies[-1].start()
    weights = []
    for f in range(plane):
        weights.append(
            pltpu.make_async_copy(
                weight_ref.at[0, :, pl.ds(f * width, width)], blocks_ref.at[f], sems.at[len(copies) + f]
            )
        )
        weights[-1].start()
    for copy in copies:
        copy.wait()
    row = lax.broadcasted_iota(jnp.int32, (requests, channels), 0)
    for j, o in enumerate(leaving):
        scan = scans_ref[j]
        lines = [
            jnp.sum(jnp.where(row == o, win_ref[t].astype(F32), 0.0), axis=0, keepdims=True) for t in range(taps)
        ]
        win = jnp.concatenate([*lines, jnp.zeros((SUB - taps, channels), F32)], axis=0)
        for i in range(plane):
            b, h = i // 2, i % 2
            head = scan[h * SUB : (h + 1) * SUB, b * LANES : (b + 1) * LANES]
            tail = win[:, i * LANES : (i + 1) * LANES] if i < blocks else jnp.zeros((SUB, LANES), F32)
            for c in range(2):
                out_ref[i, 3 * j + c] = pages_ref[j, i, c]
            out_ref[i, 3 * j + 2] = jnp.concatenate([head, tail], axis=0).astype(BF16)
    hidden = rows_ref[...]
    for f in range(plane):
        weights[f].wait()
        total = jnp.dot(hidden, blocks_ref[f], preferred_element_type=F32).astype(BF16)
        for q in range(hidden.shape[0] // ROWS):
            for b in range(width // LANES):
                out_ref[f, 3 * MIG + q * (width // LANES) + b] = total[
                    q * ROWS : (q + 1) * ROWS, b * LANES : (b + 1) * LANES
                ]
    token_ref[...] = jnp.zeros_like(token_ref)


def _route_body(requests, anchor_ref, dep_ref, out_ref):
    anchors = anchor_ref[...]
    replicas = anchors.shape[0]
    home = lax.broadcasted_iota(jnp.int32, anchors.shape, 0)
    place = lax.broadcasted_iota(jnp.int32, anchors.shape, 1).astype(F32)
    source = anchors // requests
    bit = (jnp.int32(1) << (anchors - source * requests)).astype(F32)
    arrived = source != home
    staying = jnp.sum(jnp.where(arrived, 0.0, bit), axis=1, keepdims=True).astype(jnp.int32)
    first = ((~staying) & (staying + 1)).astype(F32)
    lowest = jnp.zeros(anchors.shape, F32)
    for s in range(replicas):
        lowest = jnp.where(source == s, first[s : s + 1], lowest)
    item = (source * MIG).astype(F32) + jnp.where(lowest != bit, 1.0, 0.0)
    early = jnp.min(jnp.where(arrived, place, 99.0), axis=1, keepdims=True)
    one = jnp.sum(jnp.where(arrived & (place == early), item, 0.0), axis=1, keepdims=True)
    two = jnp.sum(jnp.where(arrived & (place != early), item, 0.0), axis=1, keepdims=True)
    lane = lax.broadcasted_iota(jnp.int32, out_ref.shape, 1)
    out_ref[...] = jnp.where(lane == 0, one, jnp.where(lane == 1, two, 0.0)).astype(jnp.int32)


def _select_body(index_ref, in_ref, out_ref):
    replicas, tiles = out_ref.shape[0], out_ref.shape[1]
    plane = in_ref.shape[0]
    cap = 4
    blocks = ROWS // cap
    for d in range(replicas):
        for j in range(MIG):
            i = index_ref[d, j]
            member = (i // MIG) % plane
            for k in range(3):
                out_ref[d, 3 * j + k] = in_ref[member, 3 * (i % MIG) + k]
    for q in range(replicas // blocks):
        totals = []
        for b in range(blocks):
            at = 3 * MIG + q * blocks + b
            total = in_ref[0, at].astype(F32)
            for p in range(1, plane):
                total = total + in_ref[p, at].astype(F32)
            totals.append(total)
        for n in range(blocks):
            out_ref[q * blocks + n, tiles - 1] = jnp.concatenate(
                [total[n * cap : (n + 1) * cap] for total in totals], axis=0
            ).astype(BF16)


def _local_body(
    requests, rep_ref, anchor_ref, window_ref, conv_ref, taps_ref, bias_ref, mix_ref, dep_ref,
    base_ref, which_ref, taps_out_ref, mix_out_ref,
):
    taps = window_ref.shape[0]
    weights = taps_ref[...]
    row = lax.broadcasted_iota(jnp.int32, (requests, requests), 0)
    col = lax.broadcasted_iota(jnp.int32, (requests, requests), 1)
    row_w = lax.broadcasted_iota(jnp.int32, which_ref.shape, 0)
    col_w = lax.broadcasted_iota(jnp.int32, which_ref.shape, 1)
    pick = jnp.zeros((requests, requests), F32)
    which = jnp.zeros(which_ref.shape, F32)
    for g, (a, local, arrived, order) in enumerate(_slots(rep_ref, anchor_ref, requests)):
        pick = jnp.where((row == g) & (col == local) & ~arrived, 1.0, pick)
        level = a // (requests * PLANE)
        which = jnp.where((row_w == g) & (col_w == level * MIG + order) & arrived, 1.0, which)
    pick = pick.astype(BF16)
    mixed = conv_ref[...].astype(F32) * weights[taps : taps + 1] + bias_ref[...]
    for t in range(taps):
        mixed = mixed + jnp.dot(pick, window_ref[t], preferred_element_type=F32) * weights[t : t + 1]
    base_ref[...] = mixed
    which_ref[...] = which
    taps_out_ref[...] = weights
    mix_out_ref[...] = mix_ref[...]


def _act_body(moved_ref, base_ref, which_ref, taps_ref, mix_ref, out_ref, act_ref, win_ref):
    requests, channels = base_ref.shape
    blocks = channels // LANES
    weights = taps_ref[...]
    taps = weights.shape[0] - 1
    mixed = base_ref[...]
    levels = moved_ref.shape[0] // PLANE
    for z in range(levels):
        for j in range(MIG):
            for b in range(blocks):
                tile = moved_ref[z * PLANE + b, 3 * j + 2].astype(F32)
                win_ref[:, b * LANES : (b + 1) * LANES] = tile[SUB : 2 * SUB]
            line = jnp.sum(win_ref[0:taps, :] * weights[0:taps], axis=0, keepdims=True)
            mixed = mixed + which_ref[:, z * MIG + j : z * MIG + j + 1] * line
    act = mixed * (1.0 / (1.0 + jnp.exp(-mixed)))
    act_ref[...] = act
    turn = (((1,), (1,)), ((), ()))
    partial = lax.dot_general(act.astype(BF16), mix_ref[...], turn, preferred_element_type=F32)
    rank = 2 * LANES
    high = partial.astype(BF16).astype(F32)
    low = (partial - high)[:, rank:]
    fill = jnp.zeros((requests, LANES - 2 * low.shape[1]), F32)
    packed = jnp.concatenate([high[:, :rank], high[:, rank:], low, fill], axis=1)
    experts = out_ref.shape[0]
    sums = []
    for r in range(PLANE):
        total = moved_ref[r, 3 * MIG].astype(F32)
        for z in range(1, levels):
            total = total + moved_ref[z * PLANE + r, 3 * MIG].astype(F32)
        sums.append(total)
    empty = jnp.zeros((requests - SUB, LANES), F32)
    for e in range(experts):
        block = sums[e // 2][e % 2 * SUB : (e % 2 + 1) * SUB]
        block = jnp.concatenate([block, empty], axis=0)
        out_ref[e] = jnp.concatenate([packed, block], axis=1).astype(BF16)


def _ready_body(
    requests, states, rep_ref, anchor_ref, routes_ref, share_ref, moved_ref, act_ref, gate_ref, scan_ref, step_ref,
    bias_ref, decay_ref, skip_ref, old_ref, rate_ref, gate_out_ref, skip_out_ref, step_out_ref, bias_out_ref,
    share_out_ref, arr_ref, count_ref,
):
    slots = _slots(rep_ref, anchor_ref, requests)
    for j, level in enumerate(_levels(slots, requests)):
        for i in range(PLANE):
            b, h = i // 2, i % 2
            tile = moved_ref[level * PLANE + i, 3 * j + 2].astype(F32)
            arr_ref[j, h * SUB : (h + 1) * SUB, b * LANES : (b + 1) * LANES] = tile[0:SUB]
    for g, (_, local, arrived, order) in enumerate(slots):
        old_ref[g] = jnp.where(arrived, arr_ref[order], scan_ref[local])
    rate_ref[...] = -jnp.exp(decay_ref[...])
    gate = gate_ref[...].astype(F32)
    gate_out_ref[...] = gate * (1.0 / (1.0 + jnp.exp(-gate)))
    skip_out_ref[...] = skip_ref[...] * act_ref[...]
    step_out_ref[...] = step_ref[...]
    bias_out_ref[...] = jnp.broadcast_to(bias_ref[...], bias_out_ref.shape)
    for e in range(count_ref.shape[0]):
        count_ref[e] = 0
    row = lax.broadcasted_iota(jnp.int32, (requests, LANES), 0)
    col = lax.broadcasted_iota(jnp.int32, (requests, LANES), 1)
    share = jnp.zeros((requests, LANES), F32)
    for t in range(requests):
        for k in range(routes_ref.shape[0]):
            e = routes_ref[k, t]
            place = count_ref[e]
            count_ref[e] = place + 1
            share = share + jnp.where((row == t) & (col == e * SUB + place), share_ref[k, t], 0.0)
    share_out_ref[...] = share


def _final_body(
    states, sums_ref, act_ref, old_ref, rate_ref, gate_ref, skip_ref, step_ref, bias_ref, share_ref,
    gated_ref, mix_ref, y_ref,
):
    experts, requests, _ = sums_ref.shape
    rank = 2 * LANES
    projected = sums_ref[0, :, 0 : rank + LANES].astype(F32)
    for e in range(1, experts):
        projected = projected + sums_ref[e, :, 0 : rank + LANES].astype(F32)
    step = jnp.dot(projected[:, :rank].astype(BF16), step_ref[...], preferred_element_type=F32) + bias_ref[0:1]
    step = jnp.maximum(step, 0.0) + jnp.log1p(jnp.exp(-jnp.abs(step)))
    tail = projected[:, rank:]
    columns = jnp.transpose(tail + pltpu.roll(tail, LANES - 2 * states, 1))
    rest = share_ref[...]
    parts = []
    for _ in range(3):
        part = rest.astype(BF16).astype(F32)
        parts.append(part)
        rest = rest - part
    outs = sums_ref[:, :, rank + LANES :].astype(F32)[:, 0:SUB].reshape(experts * SUB, LANES).astype(BF16)
    both = jnp.concatenate([*parts, *(pltpu.roll(p, SUB // 2, 1) for p in parts)], axis=0).astype(BF16)
    terms = jnp.dot(both, outs, preferred_element_type=F32)
    halves = [
        sum(terms[(3 * h + i) * requests : (3 * h + i + 1) * requests] for i in reversed(range(3))) for h in range(2)
    ]
    mix_ref[...] = jnp.concatenate(halves, axis=1).astype(BF16)
    rate = rate_ref[...]
    flow = step * act_ref[...]
    for g in range(requests):
        inflow = columns[0:states, g : g + 1]
        readout = columns[states : 2 * states, g : g + 1]
        state = jnp.exp(step[g : g + 1] * rate) * old_ref[g] + inflow * flow[g : g + 1]
        y_ref[g : g + 1, :] = jnp.sum(readout * state, axis=0, keepdims=True)
    gated_ref[...] = ((y_ref[...] + skip_ref[...]) * gate_ref[...]).astype(BF16)


def _attend_body(
    requests, rep_ref, anchor_ref, len_ref, table_ref, query_ref, key_ref, value_ref, pool_ref, moved_ref, dep_ref,
    out_ref, pages_ref, keys_ref, values_ref,
):
    turn = (((1,), (1,)), ((), ()))
    head = key_ref.shape[1]
    heads = query_ref.shape[1] // head
    pool, _, _, page, _ = pool_ref.shape
    table = table_ref[...].astype(F32).astype(BF16)
    pages = table.shape[0]
    span = pages * page
    slots = _slots(rep_ref, anchor_ref, requests)
    row1 = lax.broadcasted_iota(jnp.int32, (requests, 1), 0)
    row = lax.broadcasted_iota(jnp.int32, (requests, requests), 0)
    col = lax.broadcasted_iota(jnp.int32, (requests, requests), 1)
    live = jnp.zeros((requests, 1), jnp.int32)
    order = jnp.full((requests, 1), -1, jnp.int32)
    pick = jnp.zeros((requests, requests), F32)
    live_of = [jnp.int32(0)] * MIG
    for g, (a, local, arrived, place) in enumerate(slots):
        length = len_ref[a]
        live = jnp.where(row1 == g, length, live)
        order = jnp.where((row1 == g) & arrived, place, order)
        pick = jnp.where((row == g) & (col == local), 1.0, pick)
        live_of = [jnp.where(arrived & (place == j), length, live_of[j]) for j in range(MIG)]
    mine = lax.dot_general(pick.astype(BF16), table, turn, preferred_element_type=F32).astype(jnp.int32)
    here = jnp.where(order < 0, live, 0)
    at = lax.broadcasted_iota(jnp.int32, (requests, pool * page), 1)
    which, token = at // page, at % page
    seen = jnp.zeros((requests, pool * page), jnp.bool_)
    for m in range(pages):
        seen = seen | ((mine[:, m : m + 1] == which) & (token + m * page < here))
    at = lax.broadcasted_iota(jnp.int32, (requests, MIG * span), 1)
    seen_moved = (at // span == order) & (at % span < live)
    down = lax.broadcasted_iota(jnp.int32, (span, head), 0)
    for j, level in enumerate(_levels(slots, requests)):
        for c, ref in ((0, keys_ref), (1, values_ref)):
            for m in range(pages):
                start = j * span + m * page
                ref[start : start + page, :] = moved_ref[level * PLANE + m, 3 * j + c]
            block = ref[j * span : (j + 1) * span, :].astype(F32)
            pages_ref[j, 0, c] = jnp.where(down < live_of[j], block, 0.0).astype(BF16)
    moved_keys = keys_ref[...]
    moved_values = values_ref[...]
    pool_keys = pool_ref[:, 0, 0].reshape(pool * page, head)
    pool_values = pool_ref[:, 0, 1].reshape(pool * page, head)
    query = query_ref[...]
    queries = jnp.concatenate([query[:, h * head : (h + 1) * head] for h in range(heads)], axis=0)
    scale = 1.0 / math.sqrt(head)
    scores = lax.dot_general(queries, pool_keys, turn, preferred_element_type=F32) * scale
    scores_moved = lax.dot_general(queries, moved_keys, turn, preferred_element_type=F32) * scale
    new_key = jnp.concatenate([key_ref[...].astype(F32)] * heads, axis=0)
    new_value = jnp.concatenate([value_ref[...].astype(F32)] * heads, axis=0)
    own = jnp.sum(queries.astype(F32) * new_key, axis=1, keepdims=True) * scale
    far = F32(-1e30)
    seen = jnp.concatenate([jnp.where(seen, 1.0, 0.0)] * heads, axis=0) > 0.5
    seen_moved = jnp.concatenate([jnp.where(seen_moved, 1.0, 0.0)] * heads, axis=0) > 0.5
    scores = jnp.where(seen, scores, far)
    scores_moved = jnp.where(seen_moved, scores_moved, far)
    highest = jnp.maximum(
        jnp.maximum(jnp.max(scores, axis=1, keepdims=True), jnp.max(scores_moved, axis=1, keepdims=True)), own
    )
    e_pool = jnp.exp(scores - highest)
    e_moved = jnp.exp(scores_moved - highest)
    e_own = jnp.exp(own - highest)
    total = jnp.sum(e_pool, axis=1, keepdims=True) + jnp.sum(e_moved, axis=1, keepdims=True) + e_own
    w_pool = (e_pool / total).astype(BF16)
    w_moved = (e_moved / total).astype(BF16)
    w_own = (e_own / total).astype(BF16).astype(F32)
    context = jnp.dot(w_pool, pool_values, preferred_element_type=F32)
    context = context + jnp.dot(w_moved, moved_values, preferred_element_type=F32) + w_own * new_value
    for h in range(heads):
        out_ref[:, h * head : (h + 1) * head] = context[h * requests : (h + 1) * requests].astype(BF16)


def per_device(
    query,
    new_key,
    new_value,
    page_pool,
    block_table,
    lengths,
    anchor,
    conv_input,
    gate_input,
    window_state,
    scan_state,
    filter_taps,
    filter_bias,
    mix_weight,
    step_weight,
    step_bias,
    log_decay,
    skip_gain,
    routes,
    route_weight,
    expert_hidden,
    down_weight,
):
    requests, channels = query.shape
    replicas = lax.axis_size("rep")
    experts = lax.axis_size("exp")
    rep = lax.axis_index("rep").astype(jnp.int32).reshape(1)
    states = log_decay.shape[0]
    head = new_key.shape[1]
    pages, page = block_table.shape[1], page_pool.shape[3]
    slots = expert_hidden.shape[1]
    features = down_weight.shape[2]
    table = block_table.T
    window = jnp.transpose(window_state, (1, 0, 2))

    tiles = 3 * MIG + slots * features // (PLANE * ROWS * LANES)
    packed, token = _call(
        lambda *refs: _pack_body(requests, *refs),
        "pack_leaving",
        [_shape((PLANE, tiles, ROWS, LANES), BF16), _shape((SUB, LANES), F32)],
        [_smem()] * 3 + [_hbm()] * 5,
        [_vmem()] * 2,
        (rep, anchor, table, page_pool, window, scan_state, expert_hidden, down_weight),
        scratch=[
            pltpu.VMEM((MIG, states, channels), F32),
            pltpu.VMEM((MIG, pages, 2, page, head), BF16),
            pltpu.VMEM(window.shape, BF16),
            pltpu.VMEM(expert_hidden.shape[1:], BF16),
            pltpu.VMEM((PLANE, down_weight.shape[1], features // PLANE), BF16),
            pltpu.SemaphoreType.DMA((2 + MIG * (1 + pages) + PLANE,)),
        ],
        us=4,
        room=60,
    )
    planes = [[z * PLANE + i for i in range(PLANE)] for z in range(replicas // PLANE)]
    spread = lax.all_to_all(packed, "rep", split_axis=0, concat_axis=0, tiled=True, axis_index_groups=planes)

    index = _call(
        lambda *refs: _route_body(requests, *refs),
        "route_pieces",
        _shape((replicas, LANES), jnp.int32),
        [_vmem(), _any()],
        _vmem(),
        (anchor.reshape(replicas, requests), token),
        us=1,
    )
    onward = _call(
        _select_body,
        "select_pieces",
        _shape((replicas, 3 * MIG + 1, ROWS, LANES), BF16),
        [_smem(), _vmem()],
        _vmem(),
        (index, spread),
        us=1.5,
    )
    moved = lax.all_to_all(onward, "rep", split_axis=0, concat_axis=0, tiled=True)

    base, which, taps, mix = _call(
        lambda *refs: _local_body(requests, *refs),
        "filter_local",
        [
            _shape((requests, channels), F32),
            _shape((requests, LANES), F32),
            _shape(filter_taps.shape, F32),
            _shape(mix_weight.shape[::-1], BF16),
        ],
        [_smem()] * 2 + [_vmem()] * 5 + [_any()],
        [_vmem()] * 4,
        (rep, anchor, window, conv_input, filter_taps, filter_bias.reshape(1, channels), mix_weight.T, index),
        us=1.5,
    )
    sums, act = _call(
        _act_body,
        "filter_and_project",
        [_shape((experts, requests, 4 * LANES), BF16), _shape((requests, channels), F32)],
        [_vmem()] * 5,
        [_vmem()] * 2,
        (moved, base, which, taps, mix),
        scratch=[pltpu.VMEM((SUB, channels), F32)],
        us=1.5,
    )
    sums_all = lax.all_to_all(sums, "exp", split_axis=0, concat_axis=0, tiled=True)

    attended, pages_out = _call(
        lambda *refs: _attend_body(requests, *refs),
        "attend",
        [_shape((requests, channels), BF16), _shape((MIG, 1, 2, pages * page, head), BF16)],
        [_smem()] * 3 + [_vmem()] * 6 + [_any()],
        [_vmem()] * 2,
        (rep, anchor, lengths, table, query, new_key, new_value, page_pool, moved, act),
        scratch=[pltpu.VMEM((MIG * pages * page, head), BF16)] * 2,
        us=2,
    )
    ready = _call(
        lambda *refs: _ready_body(requests, states, *refs),
        "ready_state",
        [
            _shape((requests, states, channels), F32),
            _shape((states, channels), F32),
            _shape((requests, channels), F32),
            _shape((requests, channels), F32),
            _shape(step_weight.shape, BF16),
            _shape((SUB, channels), F32),
            _shape((requests, LANES), F32),
        ],
        [_smem()] * 4 + [_vmem()] * 8,
        [_vmem()] * 7,
        (
            rep, anchor, routes.T, route_weight.T, moved, act, gate_input, scan_state, step_weight,
            step_bias.reshape(1, channels), log_decay, skip_gain.reshape(1, channels),
        ),
        scratch=[pltpu.VMEM((MIG, states, channels), F32), pltpu.SMEM((experts,), jnp.int32)],
        us=2,
    )
    gated, mixed = _call(
        lambda *refs: _final_body(states, *refs),
        "update_state",
        [_shape((requests, channels), BF16), _shape((requests, features // experts), BF16)],
        [_vmem()] * 9,
        [_vmem()] * 2,
        (sums_all, act, *ready),
        scratch=[pltpu.VMEM((requests, channels), F32)],
        us=2,
    )
    return (attended, pages_out, gated, mixed)


def solution(mesh):
    placed = (
        P("rep", "exp"),
        P("rep", "exp"),
        P("rep", "exp"),
        P("rep", "exp", None, None, None),
        P("rep", None),
        P(),
        P(),
        P("rep", "exp"),
        P("rep", "exp"),
        P("rep", None, "exp"),
        P("rep", None, "exp"),
        P(None, "exp"),
        P("exp"),
        P("exp", None),
        P(None, "exp"),
        P("exp"),
        P(None, "exp"),
        P("exp"),
        P("rep", None),
        P("rep", None),
        P("exp", None, "rep"),
        P("exp", "rep", None),
    )
    return jax.shard_map(
        per_device,
        mesh=mesh,
        in_specs=placed,
        out_specs=(
            P("rep", "exp"),
            P("rep", "exp", None, None, None),
            P("rep", "exp"),
            P("rep", "exp"),
        ),
        check_vma=False,
    )
```

```python
import math

import jax
import jax.numpy as jnp
from jax import lax
from jax.experimental import pallas as pl
from jax.experimental.pallas import tpu as pltpu
from jax.sharding import PartitionSpec as P

MIG = 2
LANES = 128
SUB = 8
ROWS = 16
PLANE = 8
F32 = jnp.float32
BF16 = jnp.bfloat16


def _smem():
    return pl.BlockSpec(memory_space=pltpu.SMEM)


def _vmem():
    return pl.BlockSpec(memory_space=pltpu.VMEM)


def _any():
    return pl.BlockSpec(memory_space=pl.ANY)


def _hbm():
    return pl.BlockSpec(memory_space=pltpu.HBM)


def _shape(shape, dtype):
    return jax.ShapeDtypeStruct(shape, dtype)


def _call(body, name, out_shape, ins, outs, args, scratch=(), us=1.0, room=32):
    return pl.pallas_call(
        body,
        name=name,
        out_shape=out_shape,
        in_specs=ins,
        out_specs=outs,
        scratch_shapes=list(scratch),
        compiler_params=pltpu.CompilerParams(vmem_limit_bytes=room * 1024 * 1024),
        cost_estimate=pl.CostEstimate(flops=0, bytes_accessed=int(us * 3.5e6), transcendentals=0),
    )(*args)


def _present(anchor_ref, base, requests):
    mask = jnp.int32(0)
    for g in range(requests):
        a = anchor_ref[base + g] - base
        inside = (a >= 0) & (a < requests)
        mask = mask | jnp.where(inside, jnp.int32(1) << jnp.clip(a, 0, requests - 1), 0)
    return mask


def _slots(rep_ref, anchor_ref, requests):
    base = rep_ref[0] * requests
    count = jnp.int32(0)
    found = []
    for g in range(requests):
        a = anchor_ref[base + g]
        local = a - base
        arrived = (local < 0) | (local >= requests)
        found.append((a, jnp.clip(local, 0, requests - 1), arrived, jnp.minimum(count, MIG - 1)))
        count = count + jnp.where(arrived, 1, 0)
    return found


def _pack_body(
    requests, rep_ref, anchor_ref, table_ref, pool_ref, window_ref, scan_ref, hidden_ref, weight_ref, out_ref, keep_ref, send_ref,
    scans_ref, pages_ref, win_ref, rows_ref, blocks_ref, sems,
):
    pages = table_ref.shape[0]
    taps, _, channels = window_ref.shape
    blocks = channels // LANES
    plane = PLANE
    width = weight_ref.shape[2] // plane
    r = rep_ref[0]
    x, core = (r // 2) % 4, r % 2
    copies = [
        pltpu.make_async_copy(hidden_ref.at[0], rows_ref, sems.at[0]),
        pltpu.make_async_copy(window_ref, win_ref, sems.at[1]),
    ]
    for copy in copies:
        copy.start()
    base = rep_ref[0] * requests
    mask = _present(anchor_ref, base, requests)
    first, second = jnp.int32(0), jnp.int32(0)
    for o in reversed(range(requests)):
        leaves = ((mask >> o) & 1) == 0
        second = jnp.where(leaves, first, second)
        first = jnp.where(leaves, o, first)
    leaving = (first, second)
    for j, o in enumerate(leaving):
        copies.append(pltpu.make_async_copy(scan_ref.at[o], scans_ref.at[j], sems.at[len(copies)]))
        copies[-1].start()
        for m in range(pages):
            copies.append(
                pltpu.make_async_copy(pool_ref.at[table_ref[m, o], 0], pages_ref.at[j, m], sems.at[len(copies)])
            )
            copies[-1].start()
    weights = []
    order = (4, 5, 6, 7, 0, 1, 2, 3)
    for f, p in enumerate(order):
        block = ((x + p) % 4) * 2 + (core + p // 4) % 2
        columns = pl.ds(pl.multiple_of(block * width, width), width)
        weights.append(
            pltpu.make_async_copy(weight_ref.at[0, :, columns], blocks_ref.at[f], sems.at[len(copies) + f])
        )
        weights[-1].start()
    for copy in copies:
        copy.wait()
    row = lax.broadcasted_iota(jnp.int32, (requests, channels), 0)
    wins = []
    for j, o in enumerate(leaving):
        lines = [
            jnp.sum(jnp.where(row == o, win_ref[t].astype(F32), 0.0), axis=0, keepdims=True) for t in range(taps)
        ]
        wins.append([line[:, b * LANES : (b + 1) * LANES] for line in lines for b in range(blocks)])
    rows_each = scans_ref.shape[1] * blocks // out_ref.shape[0]
    per_block = scans_ref.shape[1] // rows_each
    blank = jnp.zeros((1, LANES), F32)
    for i in range(out_ref.shape[0]):
        b, q = i // per_block, i % per_block
        tail = []
        for j in range(MIG):
            tail.append(scans_ref[j, q * rows_each : (q + 1) * rows_each, b * LANES : (b + 1) * LANES])
            tail.append(wins[j][i] if i < len(wins[j]) else blank)
            tail.extend([blank] * (SUB // MIG - rows_each - 1))
        m, c, h = i // 4, i // 2 % 2, i % 2
        heads = [pages_ref[j, m, c].astype(F32)[h * SUB : (h + 1) * SUB] for j in range(MIG)]
        out_ref[i] = jnp.concatenate([*heads, *tail], axis=0).astype(BF16)
    hidden = rows_ref[...]
    for f, p in enumerate(order):
        weights[f].wait()
        total = jnp.dot(hidden, blocks_ref[f], preferred_element_type=F32)
        at = slice(p % 4 * width, (p % 4 + 1) * width)
        if p < 4:
            keep_ref[:, at] = total
        else:
            send_ref[:, at] = total.astype(BF16)


def _route_body(requests, anchor_ref, dep_ref, out_ref):
    anchors = anchor_ref[...]
    replicas = anchors.shape[0]
    home = lax.broadcasted_iota(jnp.int32, anchors.shape, 0)
    place = lax.broadcasted_iota(jnp.int32, anchors.shape, 1).astype(F32)
    source = anchors // requests
    bit = (jnp.int32(1) << (anchors - source * requests)).astype(F32)
    arrived = source != home
    staying = jnp.sum(jnp.where(arrived, 0.0, bit), axis=1, keepdims=True).astype(jnp.int32)
    first = ((~staying) & (staying + 1)).astype(F32)
    lowest = jnp.zeros(anchors.shape, F32)
    for s in range(replicas):
        lowest = jnp.where(source == s, first[s : s + 1], lowest)
    item = (source * MIG).astype(F32) + jnp.where(lowest != bit, 1.0, 0.0)
    early = jnp.min(jnp.where(arrived, place, 99.0), axis=1, keepdims=True)
    one = jnp.sum(jnp.where(arrived & (place == early), item, 0.0), axis=1, keepdims=True)
    two = jnp.sum(jnp.where(arrived & (place != early), item, 0.0), axis=1, keepdims=True)
    lane = lax.broadcasted_iota(jnp.int32, out_ref.shape, 1)
    out_ref[...] = jnp.where(lane == 0, one, jnp.where(lane == 1, two, 0.0)).astype(jnp.int32)


def _fold_body(keep_ref, got_ref, o0, o1, o2, o3):
    width = o0.shape[1]
    for k, o in enumerate((o0, o1, o2, o3)):
        at = slice(k * width, (k + 1) * width)
        o[...] = (keep_ref[:, at] + got_ref[:, at].astype(F32)).astype(o.dtype)


def _select_body(index_ref, in_ref, e0, e1, e2, e3, dep_ref, out_ref):
    replicas = out_ref.shape[0]
    row = lax.broadcasted_iota(jnp.int32, (SUB, LANES), 0)
    half = SUB // MIG
    cap = e0.shape[0] // replicas
    blocks = e0.shape[1] // LANES
    total = (e0[...] + e1[...].astype(F32)) + (e2[...].astype(F32) + e3[...].astype(F32))
    for d in range(replicas):
        heads, tails = [], []
        for j in range(MIG):
            i = index_ref[d, j]
            rank = i % MIG
            item = in_ref[i // MIG].astype(F32)
            heads.append(jnp.where(rank == 0, item[0:SUB], item[SUB : 2 * SUB]))
            tail = item[2 * SUB : 3 * SUB]
            tails.append(jnp.where(rank == j, tail, pltpu.roll(tail, half, 0)))
        tail = jnp.where(row < half, tails[0], tails[1])
        rows = total[d * cap : (d + 1) * cap]
        experts = [rows[:, b * LANES : (b + 1) * LANES] for b in range(blocks)]
        out_ref[d] = jnp.concatenate([*heads, tail, *experts], axis=0).astype(BF16)


def _local_body(
    requests, rep_ref, anchor_ref, window_ref, conv_ref, taps_ref, bias_ref, mix_ref, dep_ref,
    base_ref, which_ref, taps_out_ref, mix_out_ref,
):
    taps = window_ref.shape[0]
    weights = taps_ref[...]
    row = lax.broadcasted_iota(jnp.int32, (requests, requests), 0)
    col = lax.broadcasted_iota(jnp.int32, (requests, requests), 1)
    row_w = lax.broadcasted_iota(jnp.int32, which_ref.shape, 0)
    col_w = lax.broadcasted_iota(jnp.int32, which_ref.shape, 1)
    pick = jnp.zeros((requests, requests), F32)
    which = jnp.zeros(which_ref.shape, F32)
    for g, (_, local, arrived, order) in enumerate(_slots(rep_ref, anchor_ref, requests)):
        pick = jnp.where((row == g) & (col == local) & ~arrived, 1.0, pick)
        which = jnp.where((row_w == g) & (col_w == order) & arrived, 1.0, which)
    pick = pick.astype(BF16)
    mixed = conv_ref[...].astype(F32) * weights[taps : taps + 1] + bias_ref[...]
    for t in range(taps):
        mixed = mixed + jnp.dot(pick, window_ref[t], preferred_element_type=F32) * weights[t : t + 1]
    base_ref[...] = mixed
    which_ref[...] = which
    taps_out_ref[...] = weights
    mix_out_ref[...] = mix_ref[...]


def _act_body(moved_ref, base_ref, which_ref, taps_ref, mix_ref, out_ref, act_ref, win_ref):
    requests, channels = base_ref.shape
    blocks = channels // LANES
    weights = taps_ref[...]
    taps = weights.shape[0] - 1
    mixed = base_ref[...]
    for j in range(MIG):
        for t in range(taps):
            for b in range(blocks):
                at = 2 * SUB + j * (SUB // MIG) + 2
                win_ref[t : t + 1, b * LANES : (b + 1) * LANES] = moved_ref[t * blocks + b].astype(F32)[at : at + 1]
        line = jnp.sum(win_ref[0:taps, :] * weights[0:taps], axis=0, keepdims=True)
        mixed = mixed + which_ref[:, j : j + 1] * line
    act = mixed * (1.0 / (1.0 + jnp.exp(-mixed)))
    act_ref[...] = act
    turn = (((1,), (1,)), ((), ()))
    partial = lax.dot_general(act.astype(BF16), mix_ref[...], turn, preferred_element_type=F32)
    rank = 2 * LANES
    high = partial.astype(BF16).astype(F32)
    low = (partial - high)[:, rank:]
    fill = jnp.zeros((requests, LANES - 2 * low.shape[1]), F32)
    packed = jnp.concatenate([high[:, :rank], high[:, rank:], low, fill], axis=1)
    experts = out_ref.shape[0]
    sums = []
    for r in range(PLANE):
        total = moved_ref[r].astype(F32)[3 * SUB :]
        for z in range(1, moved_ref.shape[0] // PLANE):
            total = total + moved_ref[z * PLANE + r].astype(F32)[3 * SUB :]
        sums.append(total)
    empty = jnp.zeros((requests - SUB, LANES), F32)
    for e in range(experts):
        block = sums[e // 2][e % 2 * SUB : (e % 2 + 1) * SUB]
        block = jnp.concatenate([block, empty], axis=0)
        out_ref[e] = jnp.concatenate([packed, block], axis=1).astype(BF16)


def _ready_body(
    requests, states, rep_ref, anchor_ref, routes_ref, share_ref, moved_ref, act_ref, gate_ref, scan_ref, step_ref,
    bias_ref, decay_ref, skip_ref, old_ref, rate_ref, gate_out_ref, skip_out_ref, step_out_ref, bias_out_ref,
    share_out_ref, arr_ref, count_ref,
):
    slots = _slots(rep_ref, anchor_ref, requests)
    blocks = act_ref.shape[1] // LANES
    rows_each = states * blocks // moved_ref.shape[0]
    per_block = states // rows_each
    for i in range(moved_ref.shape[0]):
        b, q = i // per_block, i % per_block
        tail = moved_ref[i].astype(F32)[2 * SUB : 3 * SUB]
        for j in range(MIG):
            at = j * (SUB // MIG)
            arr_ref[j, q * rows_each : (q + 1) * rows_each, b * LANES : (b + 1) * LANES] = tail[at : at + rows_each]
    for g, (_, local, arrived, order) in enumerate(slots):
        old_ref[g] = jnp.where(arrived, arr_ref[order], scan_ref[local])
    rate_ref[...] = -jnp.exp(decay_ref[...])
    gate = gate_ref[...].astype(F32)
    gate_out_ref[...] = gate * (1.0 / (1.0 + jnp.exp(-gate)))
    skip_out_ref[...] = skip_ref[...] * act_ref[...]
    step_out_ref[...] = step_ref[...]
    bias_out_ref[...] = jnp.broadcast_to(bias_ref[...], bias_out_ref.shape)
    for e in range(count_ref.shape[0]):
        count_ref[e] = 0
    row = lax.broadcasted_iota(jnp.int32, (requests, LANES), 0)
    col = lax.broadcasted_iota(jnp.int32, (requests, LANES), 1)
    share = jnp.zeros((requests, LANES), F32)
    for t in range(requests):
        for k in range(routes_ref.shape[0]):
            e = routes_ref[k, t]
            place = count_ref[e]
            count_ref[e] = place + 1
            share = share + jnp.where((row == t) & (col == e * SUB + place), share_ref[k, t], 0.0)
    share_out_ref[...] = share


def _final_body(
    states, sums_ref, act_ref, old_ref, rate_ref, gate_ref, skip_ref, step_ref, bias_ref, share_ref,
    gated_ref, mix_ref, y_ref,
):
    experts, requests, _ = sums_ref.shape
    rank = 2 * LANES
    projected = sums_ref[0, :, 0 : rank + LANES].astype(F32)
    for e in range(1, experts):
        projected = projected + sums_ref[e, :, 0 : rank + LANES].astype(F32)
    step = jnp.dot(projected[:, :rank].astype(BF16), step_ref[...], preferred_element_type=F32) + bias_ref[0:1]
    step = jnp.maximum(step, 0.0) + jnp.log1p(jnp.exp(-jnp.abs(step)))
    tail = projected[:, rank:]
    columns = jnp.transpose(tail + pltpu.roll(tail, LANES - 2 * states, 1))
    rest = share_ref[...]
    parts = []
    for _ in range(3):
        part = rest.astype(BF16).astype(F32)
        parts.append(part)
        rest = rest - part
    outs = sums_ref[:, :, rank + LANES :].astype(F32)[:, 0:SUB].reshape(experts * SUB, LANES).astype(BF16)
    both = jnp.concatenate([*parts, *(pltpu.roll(p, SUB // 2, 1) for p in parts)], axis=0).astype(BF16)
    terms = jnp.dot(both, outs, preferred_element_type=F32)
    halves = [
        sum(terms[(3 * h + i) * requests : (3 * h + i + 1) * requests] for i in reversed(range(3))) for h in range(2)
    ]
    mix_ref[...] = jnp.concatenate(halves, axis=1).astype(BF16)
    rate = rate_ref[...]
    flow = step * act_ref[...]
    for g in range(requests):
        inflow = columns[0:states, g : g + 1]
        readout = columns[states : 2 * states, g : g + 1]
        state = jnp.exp(step[g : g + 1] * rate) * old_ref[g] + inflow * flow[g : g + 1]
        y_ref[g : g + 1, :] = jnp.sum(readout * state, axis=0, keepdims=True)
    gated_ref[...] = ((y_ref[...] + skip_ref[...]) * gate_ref[...]).astype(BF16)


def _attend_body(
    requests, rep_ref, anchor_ref, len_ref, table_ref, query_ref, key_ref, value_ref, pool_ref, moved_ref, dep_ref,
    out_ref, pages_ref, keys_ref, values_ref,
):
    turn = (((1,), (1,)), ((), ()))
    head = key_ref.shape[1]
    heads = query_ref.shape[1] // head
    pool, _, _, page, _ = pool_ref.shape
    table = table_ref[...].astype(F32).astype(BF16)
    pages = table.shape[0]
    span = pages * page
    slots = _slots(rep_ref, anchor_ref, requests)
    row1 = lax.broadcasted_iota(jnp.int32, (requests, 1), 0)
    row = lax.broadcasted_iota(jnp.int32, (requests, requests), 0)
    col = lax.broadcasted_iota(jnp.int32, (requests, requests), 1)
    live = jnp.zeros((requests, 1), jnp.int32)
    order = jnp.full((requests, 1), -1, jnp.int32)
    pick = jnp.zeros((requests, requests), F32)
    live_of = [jnp.int32(0)] * MIG
    for g, (a, local, arrived, place) in enumerate(slots):
        length = len_ref[a]
        live = jnp.where(row1 == g, length, live)
        order = jnp.where((row1 == g) & arrived, place, order)
        pick = jnp.where((row == g) & (col == local), 1.0, pick)
        live_of = [jnp.where(arrived & (place == j), length, live_of[j]) for j in range(MIG)]
    mine = lax.dot_general(pick.astype(BF16), table, turn, preferred_element_type=F32).astype(jnp.int32)
    here = jnp.where(order < 0, live, 0)
    at = lax.broadcasted_iota(jnp.int32, (requests, pool * page), 1)
    which, token = at // page, at % page
    seen = jnp.zeros((requests, pool * page), jnp.bool_)
    for m in range(pages):
        seen = seen | ((mine[:, m : m + 1] == which) & (token + m * page < here))
    at = lax.broadcasted_iota(jnp.int32, (requests, MIG * span), 1)
    seen_moved = (at // span == order) & (at % span < live)
    down = lax.broadcasted_iota(jnp.int32, (span, head), 0)
    for i in range(moved_ref.shape[0]):
        m, c, h = i // 4, i // 2 % 2, i % 2
        item = moved_ref[i].astype(F32)
        ref = (keys_ref, values_ref)[c]
        for j in range(MIG):
            start = j * span + m * page + h * SUB
            ref[start : start + SUB, :] = item[j * SUB : (j + 1) * SUB]
    for j in range(MIG):
        for c, ref in ((0, keys_ref), (1, values_ref)):
            block = ref[j * span : (j + 1) * span, :]
            pages_ref[j, 0, c] = jnp.where(down < live_of[j], block, 0.0).astype(BF16)
    moved_keys = keys_ref[...].astype(BF16)
    moved_values = values_ref[...].astype(BF16)
    pool_keys = pool_ref[:, 0, 0].reshape(pool * page, head)
    pool_values = pool_ref[:, 0, 1].reshape(pool * page, head)
    query = query_ref[...]
    queries = jnp.concatenate([query[:, h * head : (h + 1) * head] for h in range(heads)], axis=0)
    scale = 1.0 / math.sqrt(head)
    scores = lax.dot_general(queries, pool_keys, turn, preferred_element_type=F32) * scale
    scores_moved = lax.dot_general(queries, moved_keys, turn, preferred_element_type=F32) * scale
    new_key = jnp.concatenate([key_ref[...].astype(F32)] * heads, axis=0)
    new_value = jnp.concatenate([value_ref[...].astype(F32)] * heads, axis=0)
    own = jnp.sum(queries.astype(F32) * new_key, axis=1, keepdims=True) * scale
    far = F32(-1e30)
    seen = jnp.concatenate([jnp.where(seen, 1.0, 0.0)] * heads, axis=0) > 0.5
    seen_moved = jnp.concatenate([jnp.where(seen_moved, 1.0, 0.0)] * heads, axis=0) > 0.5
    scores = jnp.where(seen, scores, far)
    scores_moved = jnp.where(seen_moved, scores_moved, far)
    highest = jnp.maximum(
        jnp.maximum(jnp.max(scores, axis=1, keepdims=True), jnp.max(scores_moved, axis=1, keepdims=True)), own
    )
    e_pool = jnp.exp(scores - highest)
    e_moved = jnp.exp(scores_moved - highest)
    e_own = jnp.exp(own - highest)
    total = jnp.sum(e_pool, axis=1, keepdims=True) + jnp.sum(e_moved, axis=1, keepdims=True) + e_own
    w_pool = (e_pool / total).astype(BF16)
    w_moved = (e_moved / total).astype(BF16)
    w_own = (e_own / total).astype(BF16).astype(F32)
    context = jnp.dot(w_pool, pool_values, preferred_element_type=F32)
    context = context + jnp.dot(w_moved, moved_values, preferred_element_type=F32) + w_own * new_value
    for h in range(heads):
        out_ref[:, h * head : (h + 1) * head] = context[h * requests : (h + 1) * requests].astype(BF16)


def per_device(
    query,
    new_key,
    new_value,
    page_pool,
    block_table,
    lengths,
    anchor,
    conv_input,
    gate_input,
    window_state,
    scan_state,
    filter_taps,
    filter_bias,
    mix_weight,
    step_weight,
    step_bias,
    log_decay,
    skip_gain,
    routes,
    route_weight,
    expert_hidden,
    down_weight,
):
    requests, channels = query.shape
    replicas = lax.axis_size("rep")
    experts = lax.axis_size("exp")
    rep = lax.axis_index("rep").astype(jnp.int32).reshape(1)
    states = log_decay.shape[0]
    head = new_key.shape[1]
    pages, page = block_table.shape[1], page_pool.shape[3]
    slots = expert_hidden.shape[1]
    features = down_weight.shape[2]
    table = block_table.T
    window = jnp.transpose(window_state, (1, 0, 2))

    packed, keep, send = _call(
        lambda *refs: _pack_body(requests, *refs),
        "pack_leaving",
        [
            _shape((replicas, 3 * SUB, LANES), BF16),
            _shape((slots, features // 2), F32),
            _shape((slots, features // 2), BF16),
        ],
        [_smem()] * 3 + [_hbm()] * 5,
        [_vmem()] * 3,
        (rep, anchor, table, page_pool, window, scan_state, expert_hidden, down_weight),
        scratch=[
            pltpu.VMEM((MIG, states, channels), F32),
            pltpu.VMEM((MIG, pages, 2, page, head), BF16),
            pltpu.VMEM(window.shape, BF16),
            pltpu.VMEM(expert_hidden.shape[1:], BF16),
            pltpu.VMEM((PLANE, down_weight.shape[1], features // PLANE), BF16),
            pltpu.SemaphoreType.DMA((2 + MIG * (1 + pages) + PLANE,)),
        ],
        us=4,
        room=60,
    )
    spread = lax.all_to_all(packed, "rep", split_axis=0, concat_axis=0, tiled=True)

    def at(z, x, c):
        return (z * 4 + x) * 2 + c

    every = [(z, x, c) for z in range(4) for x in range(4) for c in range(2)]
    got = lax.ppermute(send, "rep", [(at(z, x, c), at(z, x, 1 - c)) for z, x, c in every])
    width = features // PLANE
    by_x = _call(
        _fold_body,
        "fold_cores",
        [_shape((slots, width), F32)] + [_shape((slots, width), BF16)] * 3,
        [_vmem()] * 2,
        [_vmem()] * 4,
        (keep, got),
        us=0.5,
    )
    came = [by_x[0]] + [
        lax.ppermute(by_x[k], "rep", [(at(z, x, c), at(z, (x + k) % 4, c)) for z, x, c in every]) for k in (2, 1, 3)
    ]

    index = _call(
        lambda *refs: _route_body(requests, *refs),
        "route_pieces",
        _shape((replicas, LANES), jnp.int32),
        [_vmem(), _any()],
        _vmem(),
        (anchor.reshape(replicas, requests), by_x[0]),
        us=1,
    )
    base, which, taps, mix = _call(
        lambda *refs: _local_body(requests, *refs),
        "filter_local",
        [
            _shape((requests, channels), F32),
            _shape((requests, LANES), F32),
            _shape(filter_taps.shape, F32),
            _shape(mix_weight.shape[::-1], BF16),
        ],
        [_smem()] * 2 + [_vmem()] * 5 + [_any()],
        [_vmem()] * 4,
        (rep, anchor, window, conv_input, filter_taps, filter_bias.reshape(1, channels), mix_weight.T, index),
        us=1.5,
    )
    onward = _call(
        _select_body,
        "select_pieces",
        _shape((replicas, 3 * SUB + ROWS, LANES), BF16),
        [_smem()] + [_vmem()] * 5 + [_any()],
        _vmem(),
        (index, spread, *came, which),
        us=1.5,
    )
    moved = lax.all_to_all(onward, "rep", split_axis=0, concat_axis=0, tiled=True)

    sums, act = _call(
        _act_body,
        "filter_and_project",
        [_shape((experts, requests, 4 * LANES), BF16), _shape((requests, channels), F32)],
        [_vmem()] * 5,
        [_vmem()] * 2,
        (moved, base, which, taps, mix),
        scratch=[pltpu.VMEM((SUB, channels), F32)],
        us=1.5,
    )
    sums_all = lax.all_to_all(sums, "exp", split_axis=0, concat_axis=0, tiled=True)

    attended, pages_out = _call(
        lambda *refs: _attend_body(requests, *refs),
        "attend",
        [_shape((requests, channels), BF16), _shape((MIG, 1, 2, pages * page, head), BF16)],
        [_smem()] * 3 + [_vmem()] * 6 + [_any()],
        [_vmem()] * 2,
        (rep, anchor, lengths, table, query, new_key, new_value, page_pool, moved, act),
        scratch=[pltpu.VMEM((MIG * pages * page, head), F32)] * 2,
        us=2,
    )
    ready = _call(
        lambda *refs: _ready_body(requests, states, *refs),
        "ready_state",
        [
            _shape((requests, states, channels), F32),
            _shape((states, channels), F32),
            _shape((requests, channels), F32),
            _shape((requests, channels), F32),
            _shape(step_weight.shape, BF16),
            _shape((SUB, channels), F32),
            _shape((requests, LANES), F32),
        ],
        [_smem()] * 4 + [_vmem()] * 8,
        [_vmem()] * 7,
        (
            rep, anchor, routes.T, route_weight.T, moved, act, gate_input, scan_state, step_weight,
            step_bias.reshape(1, channels), log_decay, skip_gain.reshape(1, channels),
        ),
        scratch=[pltpu.VMEM((MIG, states, channels), F32), pltpu.SMEM((experts,), jnp.int32)],
        us=2,
    )
    gated, mixed = _call(
        lambda *refs: _final_body(states, *refs),
        "update_state",
        [_shape((requests, channels), BF16), _shape((requests, features // experts), BF16)],
        [_vmem()] * 9,
        [_vmem()] * 2,
        (sums_all, act, *ready),
        scratch=[pltpu.VMEM((requests, channels), F32)],
        us=2,
    )
    return (attended, pages_out, gated, mixed)


def solution(mesh):
    placed = (
        P("rep", "exp"),
        P("rep", "exp"),
        P("rep", "exp"),
        P("rep", "exp", None, None, None),
        P("rep", None),
        P(),
        P(),
        P("rep", "exp"),
        P("rep", "exp"),
        P("rep", None, "exp"),
        P("rep", None, "exp"),
        P(None, "exp"),
        P("exp"),
        P("exp", None),
        P(None, "exp"),
        P("exp"),
        P(None, "exp"),
        P("exp"),
        P("rep", None),
        P("rep", None),
        P("exp", None, "rep"),
        P("exp", "rep", None),
    )
    return jax.shard_map(
        per_device,
        mesh=mesh,
        in_specs=placed,
        out_specs=(
            P("rep", "exp"),
            P("rep", "exp", None, None, None),
            P("rep", "exp"),
            P("rep", "exp"),
        ),
        check_vma=False,
    )
```

```python
import math

import jax
import jax.numpy as jnp
from jax import lax
from jax.experimental import pallas as pl
from jax.experimental.pallas import tpu as pltpu
from jax.sharding import PartitionSpec as P

MIG = 2
LANES = 128
SUB = 8
ROWS = 16
PLANE = 8
FIRST = (16, 8, 8)
F32 = jnp.float32
BF16 = jnp.bfloat16


def _smem():
    return pl.BlockSpec(memory_space=pltpu.SMEM)


def _vmem():
    return pl.BlockSpec(memory_space=pltpu.VMEM)


def _any():
    return pl.BlockSpec(memory_space=pl.ANY)


def _hbm():
    return pl.BlockSpec(memory_space=pltpu.HBM)


def _shape(shape, dtype):
    return jax.ShapeDtypeStruct(shape, dtype)


def _call(body, name, out_shape, ins, outs, args, scratch=(), us=1.0, room=32):
    return pl.pallas_call(
        body,
        name=name,
        out_shape=out_shape,
        in_specs=ins,
        out_specs=outs,
        scratch_shapes=list(scratch),
        compiler_params=pltpu.CompilerParams(vmem_limit_bytes=room * 1024 * 1024),
        cost_estimate=pl.CostEstimate(flops=0, bytes_accessed=int(us * 3.5e6), transcendentals=0),
    )(*args)


def _turned(size, first):
    return [[(k + first) % size for k in range(size)]]


def _present(anchor_ref, base, requests):
    mask = jnp.int32(0)
    for g in range(requests):
        a = anchor_ref[base + g] - base
        inside = (a >= 0) & (a < requests)
        mask = mask | jnp.where(inside, jnp.int32(1) << jnp.clip(a, 0, requests - 1), 0)
    return mask


def _slots(rep_ref, anchor_ref, requests):
    base = rep_ref[0] * requests
    count = jnp.int32(0)
    found = []
    for g in range(requests):
        a = anchor_ref[base + g]
        local = a - base
        arrived = (local < 0) | (local >= requests)
        found.append((a, jnp.clip(local, 0, requests - 1), arrived, jnp.minimum(count, MIG - 1)))
        count = count + jnp.where(arrived, 1, 0)
    return found


def _pack_body(
    requests, rep_ref, anchor_ref, table_ref, pool_ref, window_ref, scan_ref, hidden_ref, weight_ref,
    out_ref, keep_ref, send_ref, scans_ref, pages_ref, win_ref, rows_ref, blocks_ref, sems,
):
    pages = table_ref.shape[0]
    taps, _, channels = window_ref.shape
    blocks = channels // LANES
    plane = PLANE
    width = weight_ref.shape[2] // plane
    r = rep_ref[0]
    x, core = (r // 2) % 4, r % 2
    hidden_copy = pltpu.make_async_copy(hidden_ref.at[0], rows_ref, sems.at[plane])
    hidden_copy.start()
    weights = []
    order = (4, 5, 6, 7, 0, 1, 2, 3)
    for f, p in enumerate(order):
        block = ((x + p) % 4) * 2 + (core + p // 4) % 2
        columns = pl.ds(pl.multiple_of(block * width, width), width)
        weights.append(
            pltpu.make_async_copy(weight_ref.at[0, :, columns], blocks_ref.at[f], sems.at[f])
        )
        weights[-1].start()
    copies = [pltpu.make_async_copy(window_ref, win_ref, sems.at[plane + 1])]
    copies[0].start()
    base = rep_ref[0] * requests
    mask = _present(anchor_ref, base, requests)
    first, second = jnp.int32(0), jnp.int32(0)
    for o in reversed(range(requests)):
        leaves = ((mask >> o) & 1) == 0
        second = jnp.where(leaves, first, second)
        first = jnp.where(leaves, o, first)
    leaving = (first, second)
    for j, o in enumerate(leaving):
        copies.append(pltpu.make_async_copy(scan_ref.at[o], scans_ref.at[j], sems.at[plane + 1 + len(copies)]))
        copies[-1].start()
        for m in range(pages):
            page = pool_ref.at[table_ref[m, o], 0]
            copies.append(pltpu.make_async_copy(page, pages_ref.at[j, m], sems.at[plane + 1 + len(copies)]))
            copies[-1].start()
    hidden_copy.wait()
    hidden = rows_ref[...]
    for f, p in enumerate(order):
        weights[f].wait()
        total = jnp.dot(hidden, blocks_ref[f], preferred_element_type=F32)
        at = slice(p % 4 * width, (p % 4 + 1) * width)
        if p < 4:
            keep_ref[:, at] = total.astype(BF16)
        else:
            send_ref[:, at] = total.astype(BF16)
    for copy in copies:
        copy.wait()
    row = lax.broadcasted_iota(jnp.int32, (requests, channels), 0)
    wins = []
    for j, o in enumerate(leaving):
        lines = [
            jnp.sum(jnp.where(row == o, win_ref[t].astype(F32), 0.0), axis=0, keepdims=True) for t in range(taps)
        ]
        wins.append([line[:, b * LANES : (b + 1) * LANES] for line in lines for b in range(blocks)])
    rows_each = scans_ref.shape[1] * blocks // out_ref.shape[0]
    per_block = scans_ref.shape[1] // rows_each
    blank = jnp.zeros((1, LANES), F32)
    for i in range(out_ref.shape[0]):
        b, q = i // per_block, i % per_block
        tail = []
        for j in range(MIG):
            tail.append(scans_ref[j, q * rows_each : (q + 1) * rows_each, b * LANES : (b + 1) * LANES])
            tail.append(wins[j][i] if i < len(wins[j]) else blank)
            tail.extend([blank] * (SUB // MIG - rows_each - 1))
        m, c, h = i // 4, i // 2 % 2, i % 2
        heads = [pages_ref[j, m, c].astype(F32)[h * SUB : (h + 1) * SUB] for j in range(MIG)]
        for j in range(MIG):
            out_ref[i, j] = heads[j].astype(BF16)
        out_ref[i, MIG] = jnp.concatenate(tail, axis=0).astype(BF16)


def _route_body(requests, anchor_ref, dep_ref, out_ref):
    anchors = anchor_ref[...]
    replicas = anchors.shape[0]
    home = lax.broadcasted_iota(jnp.int32, anchors.shape, 0)
    place = lax.broadcasted_iota(jnp.int32, anchors.shape, 1).astype(F32)
    source = anchors // requests
    bit = (jnp.int32(1) << (anchors - source * requests)).astype(F32)
    arrived = source != home
    staying = jnp.sum(jnp.where(arrived, 0.0, bit), axis=1, keepdims=True).astype(jnp.int32)
    first = ((~staying) & (staying + 1)).astype(F32)
    lowest = jnp.zeros(anchors.shape, F32)
    for s in range(replicas):
        lowest = jnp.where(source == s, first[s : s + 1], lowest)
    place_of = (source + replicas - FIRST[0]) % replicas
    item = (place_of * MIG).astype(F32) + jnp.where(lowest != bit, 1.0, 0.0)
    early = jnp.min(jnp.where(arrived, place, 99.0), axis=1, keepdims=True)
    one = jnp.sum(jnp.where(arrived & (place == early), item, 0.0), axis=1, keepdims=True)
    two = jnp.sum(jnp.where(arrived & (place != early), item, 0.0), axis=1, keepdims=True)
    lane = lax.broadcasted_iota(jnp.int32, out_ref.shape, 1)
    out_ref[...] = jnp.where(lane == 0, one, jnp.where(lane == 1, two, 0.0)).astype(jnp.int32)


def _fold_body(keep_ref, got_ref, o0, o1, o2, o3):
    width = o0.shape[1]
    for k, o in enumerate((o0, o1, o2, o3)):
        at = slice(k * width, (k + 1) * width)
        o[...] = (keep_ref[:, at].astype(F32) + got_ref[:, at].astype(F32)).astype(o.dtype)


def _piece(i, replicas):
    return (i + FIRST[0] - FIRST[1]) % replicas


def _select_body(index_ref, in_ref, e0, e1, e2, e3, out_ref):
    replicas = out_ref.shape[0]
    row = lax.broadcasted_iota(jnp.int32, (SUB, LANES), 0)
    half = SUB // MIG
    cap = e0.shape[0] // replicas
    blocks = e0.shape[1] // LANES
    total = (e0[...] + e1[...].astype(F32)) + (e2[...].astype(F32) + e3[...].astype(F32))
    for t in range(replicas):
        d = (t + FIRST[1]) % replicas
        tails = []
        for j in range(MIG):
            i = index_ref[d, j]
            rank = i % MIG
            out_ref[t, j] = in_ref[i // MIG, rank]
            tail = in_ref[i // MIG, MIG].astype(F32)
            tails.append(jnp.where(rank == j, tail, pltpu.roll(tail, half, 0)))
        tail = jnp.where(row < half, tails[0], tails[1])
        rows = total[d * cap : (d + 1) * cap]
        experts = [rows[:, b * LANES : (b + 1) * LANES] for b in range(blocks)]
        out_ref[t, MIG] = tail.astype(BF16)
        for h in range(2):
            pair = experts[h * blocks // 2 : (h + 1) * blocks // 2]
            out_ref[t, MIG + 1 + h] = jnp.concatenate(pair, axis=0).astype(BF16)


def _local_body(
    requests, rep_ref, anchor_ref, window_ref, conv_ref, taps_ref, bias_ref, mix_ref, dep_ref,
    base_ref, which_ref, taps_out_ref, mix_out_ref,
):
    taps = window_ref.shape[0]
    weights = taps_ref[...]
    row = lax.broadcasted_iota(jnp.int32, (requests, requests), 0)
    col = lax.broadcasted_iota(jnp.int32, (requests, requests), 1)
    row_w = lax.broadcasted_iota(jnp.int32, which_ref.shape, 0)
    col_w = lax.broadcasted_iota(jnp.int32, which_ref.shape, 1)
    pick = jnp.zeros((requests, requests), F32)
    which = jnp.zeros(which_ref.shape, F32)
    for g, (_, local, arrived, order) in enumerate(_slots(rep_ref, anchor_ref, requests)):
        pick = jnp.where((row == g) & (col == local) & ~arrived, 1.0, pick)
        which = jnp.where((row_w == g) & (col_w == order) & arrived, 1.0, which)
    pick = pick.astype(BF16)
    mixed = conv_ref[...].astype(F32) * weights[taps : taps + 1] + bias_ref[...]
    for t in range(taps):
        mixed = mixed + jnp.dot(pick, window_ref[t], preferred_element_type=F32) * weights[t : t + 1]
    base_ref[...] = mixed
    which_ref[...] = which
    taps_out_ref[...] = weights
    mix_out_ref[...] = mix_ref[...]


def _act_body(moved_ref, base_ref, which_ref, taps_ref, mix_ref, out_ref, act_ref, win_ref):
    requests, channels = base_ref.shape
    blocks = channels // LANES
    weights = taps_ref[...]
    taps = weights.shape[0] - 1
    mixed = base_ref[...]
    for j in range(MIG):
        for t in range(taps):
            for b in range(blocks):
                at = j * (SUB // MIG) + 2
                tile = moved_ref[_piece(t * blocks + b, moved_ref.shape[0]), MIG].astype(F32)
                win_ref[t : t + 1, b * LANES : (b + 1) * LANES] = tile[at : at + 1]
        line = jnp.sum(win_ref[0:taps, :] * weights[0:taps], axis=0, keepdims=True)
        mixed = mixed + which_ref[:, j : j + 1] * line
    act = mixed * (1.0 / (1.0 + jnp.exp(-mixed)))
    act_ref[...] = act
    turn = (((1,), (1,)), ((), ()))
    partial = lax.dot_general(act.astype(BF16), mix_ref[...], turn, preferred_element_type=F32)
    rank = 2 * LANES
    high = partial.astype(BF16).astype(F32)
    low = (partial - high)[:, rank:]
    fill = jnp.zeros((requests, LANES - 2 * low.shape[1]), F32)
    tail = jnp.concatenate([high[:, rank:], low, fill], axis=1)
    experts, replicas = out_ref.shape[0], moved_ref.shape[0]
    lane = lax.broadcasted_iota(jnp.int32, (SUB, LANES), 1)
    steps = [
        high[h * SUB : (h + 1) * SUB, b * LANES : (b + 1) * LANES].astype(BF16) for h in range(2) for b in range(2)
    ]
    for f in range(PLANE):
        for q in range(2):
            block = moved_ref[(f - FIRST[1]) % replicas, MIG + 1 + q].astype(F32)
            for z in range(1, replicas // PLANE):
                block = block + moved_ref[(z * PLANE + f - FIRST[1]) % replicas, MIG + 1 + q].astype(F32)
            e = (2 * f + q - FIRST[2]) % experts
            for n, step in enumerate(steps):
                out_ref[e, n] = step
            for h, part in enumerate((pltpu.roll(block, LANES // 2, 1), block)):
                rows = tail[h * SUB : (h + 1) * SUB]
                out_ref[e, len(steps) + h] = jnp.where(lane < LANES // 2, rows, part).astype(BF16)


def _ready_body(
    requests, states, rep_ref, anchor_ref, routes_ref, share_ref, moved_ref, act_ref, gate_ref, scan_ref, step_ref,
    bias_ref, decay_ref, skip_ref, old_ref, rate_ref, gate_out_ref, skip_out_ref, step_out_ref, bias_out_ref,
    share_out_ref, arr_ref, count_ref,
):
    slots = _slots(rep_ref, anchor_ref, requests)
    blocks = act_ref.shape[1] // LANES
    rows_each = states * blocks // moved_ref.shape[0]
    per_block = states // rows_each
    for i in range(moved_ref.shape[0]):
        b, q = i // per_block, i % per_block
        tail = moved_ref[_piece(i, moved_ref.shape[0]), MIG].astype(F32)
        for j in range(MIG):
            at = j * (SUB // MIG)
            arr_ref[j, q * rows_each : (q + 1) * rows_each, b * LANES : (b + 1) * LANES] = tail[at : at + rows_each]
    for g, (_, local, arrived, order) in enumerate(slots):
        old_ref[g] = jnp.where(arrived, arr_ref[order], scan_ref[local])
    rate_ref[...] = -jnp.exp(decay_ref[...])
    gate = gate_ref[...].astype(F32)
    gate_out_ref[...] = gate * (1.0 / (1.0 + jnp.exp(-gate)))
    skip_out_ref[...] = skip_ref[...] * act_ref[...]
    step_out_ref[...] = step_ref[...]
    bias_out_ref[...] = jnp.broadcast_to(bias_ref[...], bias_out_ref.shape)
    experts = count_ref.shape[0]
    for e in range(experts):
        count_ref[e] = 0
    row = lax.broadcasted_iota(jnp.int32, (requests, LANES), 0)
    col = lax.broadcasted_iota(jnp.int32, (requests, LANES), 1)
    share = jnp.zeros((requests, LANES), F32)
    for t in range(requests):
        for k in range(routes_ref.shape[0]):
            e = routes_ref[k, t]
            place = count_ref[e]
            count_ref[e] = place + 1
            share = share + jnp.where((row == t) & (col == (e + experts - FIRST[2]) % experts * SUB + place), share_ref[k, t], 0.0)
    share_out_ref[...] = share


def _final_body(
    states, sums_ref, act_ref, old_ref, rate_ref, gate_ref, skip_ref, step_ref, bias_ref, share_ref,
    gated_ref, mix_ref, y_ref,
):
    experts = sums_ref.shape[0]
    requests, _ = act_ref.shape
    totals = []
    for n in range(sums_ref.shape[1]):
        total = sums_ref[0, n].astype(F32)
        for e in range(1, experts):
            total = total + sums_ref[e, n].astype(F32)
        totals.append(total)
    projected = jnp.concatenate(
        [jnp.concatenate(totals[0:2], axis=1), jnp.concatenate(totals[2:4], axis=1)], axis=0
    )
    step = jnp.dot(projected.astype(BF16), step_ref[...], preferred_element_type=F32) + bias_ref[0:1]
    step = jnp.maximum(step, 0.0) + jnp.log1p(jnp.exp(-jnp.abs(step)))
    tail = jnp.concatenate(totals[4:6], axis=0)
    columns = jnp.transpose(tail + pltpu.roll(tail, LANES - 2 * states, 1))
    rest = share_ref[...]
    parts = []
    for _ in range(3):
        part = rest.astype(BF16).astype(F32)
        parts.append(part)
        rest = rest - part
    lane = lax.broadcasted_iota(jnp.int32, (SUB, LANES), 1)
    outs = []
    for e in range(experts):
        left = pltpu.roll(sums_ref[e, 4].astype(F32), LANES // 2, 1)
        outs.append(jnp.where(lane < LANES // 2, left, sums_ref[e, 5].astype(F32)))
    outs = jnp.concatenate(outs, axis=0).astype(BF16)
    both = jnp.concatenate([*parts, *(pltpu.roll(p, SUB // 2, 1) for p in parts)], axis=0).astype(BF16)
    terms = jnp.dot(both, outs, preferred_element_type=F32)
    halves = [
        sum(terms[(3 * h + i) * requests : (3 * h + i + 1) * requests] for i in reversed(range(3))) for h in range(2)
    ]
    mix_ref[...] = jnp.concatenate(halves, axis=1).astype(BF16)
    rate = rate_ref[...]
    flow = step * act_ref[...]
    for g in range(requests):
        inflow = columns[0:states, g : g + 1]
        readout = columns[states : 2 * states, g : g + 1]
        state = jnp.exp(step[g : g + 1] * rate) * old_ref[g] + inflow * flow[g : g + 1]
        y_ref[g : g + 1, :] = jnp.sum(readout * state, axis=0, keepdims=True)
    gated_ref[...] = ((y_ref[...] + skip_ref[...]) * gate_ref[...]).astype(BF16)


def _attend_body(
    requests, rep_ref, anchor_ref, len_ref, table_ref, query_ref, key_ref, value_ref, pool_ref, moved_ref, dep_ref,
    out_ref, pages_ref, keys_ref, values_ref,
):
    turn = (((1,), (1,)), ((), ()))
    head = key_ref.shape[1]
    heads = query_ref.shape[1] // head
    pool, _, _, page, _ = pool_ref.shape
    table = table_ref[...].astype(F32).astype(BF16)
    pages = table.shape[0]
    span = pages * page
    slots = _slots(rep_ref, anchor_ref, requests)
    row1 = lax.broadcasted_iota(jnp.int32, (requests, 1), 0)
    row = lax.broadcasted_iota(jnp.int32, (requests, requests), 0)
    col = lax.broadcasted_iota(jnp.int32, (requests, requests), 1)
    live = jnp.zeros((requests, 1), jnp.int32)
    order = jnp.full((requests, 1), -1, jnp.int32)
    pick = jnp.zeros((requests, requests), F32)
    live_of = [jnp.int32(0)] * MIG
    for g, (a, local, arrived, place) in enumerate(slots):
        length = len_ref[a]
        live = jnp.where(row1 == g, length, live)
        order = jnp.where((row1 == g) & arrived, place, order)
        pick = jnp.where((row == g) & (col == local), 1.0, pick)
        live_of = [jnp.where(arrived & (place == j), length, live_of[j]) for j in range(MIG)]
    mine = lax.dot_general(pick.astype(BF16), table, turn, preferred_element_type=F32).astype(jnp.int32)
    here = jnp.where(order < 0, live, 0)
    at = lax.broadcasted_iota(jnp.int32, (requests, pool * page), 1)
    which, token = at // page, at % page
    seen = jnp.zeros((requests, pool * page), jnp.bool_)
    for m in range(pages):
        seen = seen | ((mine[:, m : m + 1] == which) & (token + m * page < here))
    at = lax.broadcasted_iota(jnp.int32, (requests, MIG * span), 1)
    seen_moved = (at // span == order) & (at % span < live)
    down = lax.broadcasted_iota(jnp.int32, (span, head), 0)
    for i in range(moved_ref.shape[0]):
        m, c, h = i // 4, i // 2 % 2, i % 2
        ref = (keys_ref, values_ref)[c]
        for j in range(MIG):
            start = j * span + m * page + h * SUB
            ref[start : start + SUB, :] = moved_ref[_piece(i, moved_ref.shape[0]), j].astype(F32)
    for j in range(MIG):
        for c, ref in ((0, keys_ref), (1, values_ref)):
            block = ref[j * span : (j + 1) * span, :]
            pages_ref[j, 0, c] = jnp.where(down < live_of[j], block, 0.0).astype(BF16)
    moved_keys = keys_ref[...].astype(BF16)
    moved_values = values_ref[...].astype(BF16)
    pool_keys = pool_ref[:, 0, 0].reshape(pool * page, head)
    pool_values = pool_ref[:, 0, 1].reshape(pool * page, head)
    query = query_ref[...]
    queries = jnp.concatenate([query[:, h * head : (h + 1) * head] for h in range(heads)], axis=0)
    scale = 1.0 / math.sqrt(head)
    scores = lax.dot_general(queries, pool_keys, turn, preferred_element_type=F32) * scale
    scores_moved = lax.dot_general(queries, moved_keys, turn, preferred_element_type=F32) * scale
    new_key = jnp.concatenate([key_ref[...].astype(F32)] * heads, axis=0)
    new_value = jnp.concatenate([value_ref[...].astype(F32)] * heads, axis=0)
    own = jnp.sum(queries.astype(F32) * new_key, axis=1, keepdims=True) * scale
    far = F32(-1e30)
    seen = jnp.concatenate([jnp.where(seen, 1.0, 0.0)] * heads, axis=0) > 0.5
    seen_moved = jnp.concatenate([jnp.where(seen_moved, 1.0, 0.0)] * heads, axis=0) > 0.5
    scores = jnp.where(seen, scores, far)
    scores_moved = jnp.where(seen_moved, scores_moved, far)
    highest = jnp.maximum(
        jnp.maximum(jnp.max(scores, axis=1, keepdims=True), jnp.max(scores_moved, axis=1, keepdims=True)), own
    )
    e_pool = jnp.exp(scores - highest)
    e_moved = jnp.exp(scores_moved - highest)
    e_own = jnp.exp(own - highest)
    total = jnp.sum(e_pool, axis=1, keepdims=True) + jnp.sum(e_moved, axis=1, keepdims=True) + e_own
    w_pool = (e_pool / total).astype(BF16)
    w_moved = (e_moved / total).astype(BF16)
    w_own = (e_own / total).astype(BF16).astype(F32)
    context = jnp.dot(w_pool, pool_values, preferred_element_type=F32)
    context = context + jnp.dot(w_moved, moved_values, preferred_element_type=F32) + w_own * new_value
    for h in range(heads):
        out_ref[:, h * head : (h + 1) * head] = context[h * requests : (h + 1) * requests].astype(BF16)


def per_device(
    query,
    new_key,
    new_value,
    page_pool,
    block_table,
    lengths,
    anchor,
    conv_input,
    gate_input,
    window_state,
    scan_state,
    filter_taps,
    filter_bias,
    mix_weight,
    step_weight,
    step_bias,
    log_decay,
    skip_gain,
    routes,
    route_weight,
    expert_hidden,
    down_weight,
):
    requests, channels = query.shape
    replicas = lax.axis_size("rep")
    experts = lax.axis_size("exp")
    rep = lax.axis_index("rep").astype(jnp.int32).reshape(1)
    states = log_decay.shape[0]
    head = new_key.shape[1]
    pages, page = block_table.shape[1], page_pool.shape[3]
    slots = expert_hidden.shape[1]
    features = down_weight.shape[2]
    table = block_table.T
    window = jnp.transpose(window_state, (1, 0, 2))

    packed, keep, send = _call(
        lambda *refs: _pack_body(requests, *refs),
        "pack_leaving",
        [
            _shape((replicas, MIG + 1, SUB, LANES), BF16),
            _shape((slots, features // 2), BF16),
            _shape((slots, features // 2), BF16),
        ],
        [_smem()] * 3 + [_hbm()] * 5,
        [_vmem()] * 3,
        (rep, anchor, table, page_pool, window, scan_state, expert_hidden, down_weight),
        scratch=[
            pltpu.VMEM((MIG, states, channels), F32),
            pltpu.VMEM((MIG, pages, 2, page, head), BF16),
            pltpu.VMEM(window.shape, BF16),
            pltpu.VMEM(expert_hidden.shape[1:], BF16),
            pltpu.VMEM((PLANE, down_weight.shape[1], features // PLANE), BF16),
            pltpu.SemaphoreType.DMA((2 + MIG * (1 + pages) + PLANE,)),
        ],
        us=4,
        room=60,
    )
    turned = _turned(replicas, FIRST[0])
    spread = lax.all_to_all(packed, "rep", split_axis=0, concat_axis=0, tiled=True, axis_index_groups=turned)

    def at(z, x, c):
        return (z * 4 + x) * 2 + c

    every = [(z, x, c) for z in range(4) for x in range(4) for c in range(2)]
    got = lax.ppermute(send, "rep", [(at(z, x, c), at(z, x, 1 - c)) for z, x, c in every])
    width = features // PLANE
    by_x = _call(
        _fold_body,
        "fold_cores",
        [_shape((slots, width), F32)] + [_shape((slots, width), BF16)] * 3,
        [_vmem()] * 2,
        [_vmem()] * 4,
        (keep, got),
        us=0.5,
    )
    came = [by_x[0]] + [
        lax.ppermute(by_x[k], "rep", [(at(z, x, c), at(z, (x + k) % 4, c)) for z, x, c in every]) for k in (2, 1, 3)
    ]

    index = _call(
        lambda *refs: _route_body(requests, *refs),
        "route_pieces",
        _shape((replicas, LANES), jnp.int32),
        [_vmem(), _any()],
        _vmem(),
        (anchor.reshape(replicas, requests), by_x[0]),
        us=1,
    )
    onward = _call(
        _select_body,
        "select_pieces",
        _shape((replicas, MIG + 3, SUB, LANES), BF16),
        [_smem()] + [_vmem()] * 5,
        _vmem(),
        (index, spread, *came),
        us=1.5,
    )
    turned = _turned(replicas, FIRST[1])
    moved = lax.all_to_all(onward, "rep", split_axis=0, concat_axis=0, tiled=True, axis_index_groups=turned)

    base, which, taps, mix = _call(
        lambda *refs: _local_body(requests, *refs),
        "filter_local",
        [
            _shape((requests, channels), F32),
            _shape((requests, LANES), F32),
            _shape(filter_taps.shape, F32),
            _shape(mix_weight.shape[::-1], BF16),
        ],
        [_smem()] * 2 + [_vmem()] * 5 + [_any()],
        [_vmem()] * 4,
        (rep, anchor, window, conv_input, filter_taps, filter_bias.reshape(1, channels), mix_weight.T, came[3]),
        us=1.5,
    )
    sums, act = _call(
        _act_body,
        "filter_and_project",
        [_shape((experts, 6, SUB, LANES), BF16), _shape((requests, channels), F32)],
        [_vmem()] * 5,
        [_vmem()] * 2,
        (moved, base, which, taps, mix),
        scratch=[pltpu.VMEM((SUB, channels), F32)],
        us=1.5,
    )
    turned = _turned(experts, FIRST[2])
    sums_all = lax.all_to_all(sums, "exp", split_axis=0, concat_axis=0, tiled=True, axis_index_groups=turned)

    attended, pages_out = _call(
        lambda *refs: _attend_body(requests, *refs),
        "attend",
        [_shape((requests, channels), BF16), _shape((MIG, 1, 2, pages * page, head), BF16)],
        [_smem()] * 3 + [_vmem()] * 6 + [_any()],
        [_vmem()] * 2,
        (rep, anchor, lengths, table, query, new_key, new_value, page_pool, moved, act),
        scratch=[pltpu.VMEM((MIG * pages * page, head), F32)] * 2,
        us=2,
    )
    ready = _call(
        lambda *refs: _ready_body(requests, states, *refs),
        "ready_state",
        [
            _shape((requests, states, channels), F32),
            _shape((states, channels), F32),
            _shape((requests, channels), F32),
            _shape((requests, channels), F32),
            _shape(step_weight.shape, BF16),
            _shape((SUB, channels), F32),
            _shape((requests, LANES), F32),
        ],
        [_smem()] * 4 + [_vmem()] * 8,
        [_vmem()] * 7,
        (
            rep, anchor, routes.T, route_weight.T, moved, act, gate_input, scan_state, step_weight,
            step_bias.reshape(1, channels), log_decay, skip_gain.reshape(1, channels),
        ),
        scratch=[pltpu.VMEM((MIG, states, channels), F32), pltpu.SMEM((experts,), jnp.int32)],
        us=2,
    )
    gated, mixed = _call(
        lambda *refs: _final_body(states, *refs),
        "update_state",
        [_shape((requests, channels), BF16), _shape((requests, features // experts), BF16)],
        [_vmem()] * 9,
        [_vmem()] * 2,
        (sums_all, act, *ready),
        scratch=[pltpu.VMEM((requests, channels), F32)],
        us=2,
    )
    return (attended, pages_out, gated, mixed)


def solution(mesh):
    placed = (
        P("rep", "exp"),
        P("rep", "exp"),
        P("rep", "exp"),
        P("rep", "exp", None, None, None),
        P("rep", None),
        P(),
        P(),
        P("rep", "exp"),
        P("rep", "exp"),
        P("rep", None, "exp"),
        P("rep", None, "exp"),
        P(None, "exp"),
        P("exp"),
        P("exp", None),
        P(None, "exp"),
        P("exp"),
        P(None, "exp"),
        P("exp"),
        P("rep", None),
        P("rep", None),
        P("exp", None, "rep"),
        P("exp", "rep", None),
    )
    return jax.shard_map(
        per_device,
        mesh=mesh,
        in_specs=placed,
        out_specs=(
            P("rep", "exp"),
            P("rep", "exp", None, None, None),
            P("rep", "exp"),
            P("rep", "exp"),
        ),
        check_vma=False,
    )
```

```python
import math

import jax
import jax.numpy as jnp
from jax import lax
from jax.experimental import pallas as pl
from jax.experimental.pallas import tpu as pltpu
from jax.sharding import PartitionSpec as P

MIG = 2
LANES = 128
SUB = 8
ROWS = 16
PLANE = 8
FIRST = (20, 4, 8)
F32 = jnp.float32
BF16 = jnp.bfloat16


def _smem():
    return pl.BlockSpec(memory_space=pltpu.SMEM)


def _vmem():
    return pl.BlockSpec(memory_space=pltpu.VMEM)


def _any():
    return pl.BlockSpec(memory_space=pl.ANY)


def _hbm():
    return pl.BlockSpec(memory_space=pltpu.HBM)


def _shape(shape, dtype):
    return jax.ShapeDtypeStruct(shape, dtype)


def _call(body, name, out_shape, ins, outs, args, scratch=(), us=1.0, room=32):
    return pl.pallas_call(
        body,
        name=name,
        out_shape=out_shape,
        in_specs=ins,
        out_specs=outs,
        scratch_shapes=list(scratch),
        compiler_params=pltpu.CompilerParams(vmem_limit_bytes=room * 1024 * 1024),
        cost_estimate=pl.CostEstimate(flops=0, bytes_accessed=int(us * 3.5e6), transcendentals=0),
    )(*args)


def _turned(size, first):
    return [[(k + first) % size for k in range(size)]]


def _present(anchor_ref, base, requests):
    mask = jnp.int32(0)
    for g in range(requests):
        a = anchor_ref[base + g] - base
        inside = (a >= 0) & (a < requests)
        mask = mask | jnp.where(inside, jnp.int32(1) << jnp.clip(a, 0, requests - 1), 0)
    return mask


def _slots(rep_ref, anchor_ref, requests):
    base = rep_ref[0] * requests
    count = jnp.int32(0)
    found = []
    for g in range(requests):
        a = anchor_ref[base + g]
        local = a - base
        arrived = (local < 0) | (local >= requests)
        found.append((a, jnp.clip(local, 0, requests - 1), arrived, jnp.minimum(count, MIG - 1)))
        count = count + jnp.where(arrived, 1, 0)
    return found


def _pack_body(
    requests, rep_ref, anchor_ref, table_ref, pool_ref, window_ref, scan_ref, hidden_ref, weight_ref,
    out_ref, keep_ref, send_ref, scans_ref, pages_ref, win_ref, rows_ref, blocks_ref, sems,
):
    pages = table_ref.shape[0]
    taps, _, channels = window_ref.shape
    blocks = channels // LANES
    plane = PLANE
    width = weight_ref.shape[2] // plane
    r = rep_ref[0]
    x, core = (r // 2) % 4, r % 2
    hidden_copy = pltpu.make_async_copy(hidden_ref.at[0], rows_ref, sems.at[plane])
    hidden_copy.start()
    weights = []
    order = (4, 5, 6, 7, 0, 1, 2, 3)
    for f, p in enumerate(order):
        block = ((x + p) % 4) * 2 + (core + p // 4) % 2
        columns = pl.ds(pl.multiple_of(block * width, width), width)
        weights.append(
            pltpu.make_async_copy(weight_ref.at[0, :, columns], blocks_ref.at[f], sems.at[f])
        )
        weights[-1].start()
    copies = [pltpu.make_async_copy(window_ref, win_ref, sems.at[plane + 1])]
    copies[0].start()
    base = rep_ref[0] * requests
    mask = _present(anchor_ref, base, requests)
    first, second = jnp.int32(0), jnp.int32(0)
    for o in reversed(range(requests)):
        leaves = ((mask >> o) & 1) == 0
        second = jnp.where(leaves, first, second)
        first = jnp.where(leaves, o, first)
    leaving = (first, second)
    for j, o in enumerate(leaving):
        copies.append(pltpu.make_async_copy(scan_ref.at[o], scans_ref.at[j], sems.at[plane + 1 + len(copies)]))
        copies[-1].start()
        for m in range(pages):
            page = pool_ref.at[table_ref[m, o], 0]
            copies.append(pltpu.make_async_copy(page, pages_ref.at[j, m], sems.at[plane + 1 + len(copies)]))
            copies[-1].start()
    hidden_copy.wait()
    hidden = rows_ref[...]
    for f, p in enumerate(order):
        weights[f].wait()
        total = jnp.dot(hidden, blocks_ref[f], preferred_element_type=F32)
        at = slice(p % 4 * width, (p % 4 + 1) * width)
        if p < 4:
            keep_ref[:, at] = total.astype(BF16)
        else:
            send_ref[:, at] = total.astype(BF16)
    for copy in copies:
        copy.wait()
    row = lax.broadcasted_iota(jnp.int32, (requests, channels), 0)
    wins = []
    for j, o in enumerate(leaving):
        lines = [
            jnp.sum(jnp.where(row == o, win_ref[t].astype(F32), 0.0), axis=0, keepdims=True) for t in range(taps)
        ]
        wins.append([line[:, b * LANES : (b + 1) * LANES] for line in lines for b in range(blocks)])
    rows_each = scans_ref.shape[1] * blocks // out_ref.shape[0]
    per_block = scans_ref.shape[1] // rows_each
    blank = jnp.zeros((1, LANES), F32)
    for i in range(out_ref.shape[0]):
        b, q = i // per_block, i % per_block
        tail = []
        for j in range(MIG):
            tail.append(scans_ref[j, q * rows_each : (q + 1) * rows_each, b * LANES : (b + 1) * LANES])
            tail.append(wins[j][i] if i < len(wins[j]) else blank)
            tail.extend([blank] * (SUB // MIG - rows_each - 1))
        m, c, h = i // 4, i // 2 % 2, i % 2
        heads = [pages_ref[j, m, c].astype(F32)[h * SUB : (h + 1) * SUB] for j in range(MIG)]
        for j in range(MIG):
            out_ref[i, j] = heads[j].astype(BF16)
        out_ref[i, MIG] = jnp.concatenate(tail, axis=0).astype(BF16)


def _route_body(requests, anchor_ref, dep_ref, out_ref):
    anchors = anchor_ref[...]
    replicas = anchors.shape[0]
    home = lax.broadcasted_iota(jnp.int32, anchors.shape, 0)
    place = lax.broadcasted_iota(jnp.int32, anchors.shape, 1).astype(F32)
    source = anchors // requests
    bit = (jnp.int32(1) << (anchors - source * requests)).astype(F32)
    arrived = source != home
    staying = jnp.sum(jnp.where(arrived, 0.0, bit), axis=1, keepdims=True).astype(jnp.int32)
    first = ((~staying) & (staying + 1)).astype(F32)
    lowest = jnp.zeros(anchors.shape, F32)
    for s in range(replicas):
        lowest = jnp.where(source == s, first[s : s + 1], lowest)
    place_of = (source + replicas - FIRST[0]) % replicas
    item = (place_of * MIG).astype(F32) + jnp.where(lowest != bit, 1.0, 0.0)
    early = jnp.min(jnp.where(arrived, place, 99.0), axis=1, keepdims=True)
    one = jnp.sum(jnp.where(arrived & (place == early), item, 0.0), axis=1, keepdims=True)
    two = jnp.sum(jnp.where(arrived & (place != early), item, 0.0), axis=1, keepdims=True)
    lane = lax.broadcasted_iota(jnp.int32, out_ref.shape, 1)
    out_ref[...] = jnp.where(lane == 0, one, jnp.where(lane == 1, two, 0.0)).astype(jnp.int32)


def _fold_body(keep_ref, got_ref, o0, o1, o2, o3):
    width = o0.shape[1]
    for k, o in enumerate((o0, o1, o2, o3)):
        at = slice(k * width, (k + 1) * width)
        o[...] = (keep_ref[:, at].astype(F32) + got_ref[:, at].astype(F32)).astype(o.dtype)


def _piece(i, replicas):
    return (i + FIRST[0] - FIRST[1]) % replicas


def _select_body(index_ref, in_ref, e0, e1, e2, e3, dep_ref, out_ref):
    replicas = out_ref.shape[0]
    row = lax.broadcasted_iota(jnp.int32, (SUB, LANES), 0)
    half = SUB // MIG
    cap = e0.shape[0] // replicas
    blocks = e0.shape[1] // LANES
    total = (e0[...] + e1[...].astype(F32)) + (e2[...].astype(F32) + e3[...].astype(F32))
    for t in range(replicas):
        d = (t + FIRST[1]) % replicas
        tails = []
        for j in range(MIG):
            i = index_ref[d, j]
            rank = i % MIG
            out_ref[t, j] = in_ref[i // MIG, rank]
            tail = in_ref[i // MIG, MIG].astype(F32)
            tails.append(jnp.where(rank == j, tail, pltpu.roll(tail, half, 0)))
        tail = jnp.where(row < half, tails[0], tails[1])
        rows = total[d * cap : (d + 1) * cap]
        experts = [rows[:, b * LANES : (b + 1) * LANES] for b in range(blocks)]
        out_ref[t, MIG] = tail.astype(BF16)
        for h in range(2):
            pair = experts[h * blocks // 2 : (h + 1) * blocks // 2]
            out_ref[t, MIG + 1 + h] = jnp.concatenate(pair, axis=0).astype(BF16)


def _local_body(
    requests, rep_ref, anchor_ref, window_ref, conv_ref, taps_ref, bias_ref, mix_ref, dep_ref,
    base_ref, which_ref, taps_out_ref, mix_out_ref,
):
    taps = window_ref.shape[0]
    weights = taps_ref[...]
    row = lax.broadcasted_iota(jnp.int32, (requests, requests), 0)
    col = lax.broadcasted_iota(jnp.int32, (requests, requests), 1)
    row_w = lax.broadcasted_iota(jnp.int32, which_ref.shape, 0)
    col_w = lax.broadcasted_iota(jnp.int32, which_ref.shape, 1)
    pick = jnp.zeros((requests, requests), F32)
    which = jnp.zeros(which_ref.shape, F32)
    for g, (_, local, arrived, order) in enumerate(_slots(rep_ref, anchor_ref, requests)):
        pick = jnp.where((row == g) & (col == local) & ~arrived, 1.0, pick)
        which = jnp.where((row_w == g) & (col_w == order) & arrived, 1.0, which)
    pick = pick.astype(BF16)
    mixed = conv_ref[...].astype(F32) * weights[taps : taps + 1] + bias_ref[...]
    for t in range(taps):
        mixed = mixed + jnp.dot(pick, window_ref[t], preferred_element_type=F32) * weights[t : t + 1]
    base_ref[...] = mixed
    which_ref[...] = which
    taps_out_ref[...] = weights
    mix_out_ref[...] = mix_ref[...]


def _act_body(moved_ref, base_ref, which_ref, taps_ref, mix_ref, out_ref, act_ref, win_ref):
    requests, channels = base_ref.shape
    blocks = channels // LANES
    weights = taps_ref[...]
    taps = weights.shape[0] - 1
    mixed = base_ref[...]
    for j in range(MIG):
        for t in range(taps):
            for b in range(blocks):
                at = j * (SUB // MIG) + 2
                tile = moved_ref[_piece(t * blocks + b, moved_ref.shape[0]), MIG].astype(F32)
                win_ref[t : t + 1, b * LANES : (b + 1) * LANES] = tile[at : at + 1]
        line = jnp.sum(win_ref[0:taps, :] * weights[0:taps], axis=0, keepdims=True)
        mixed = mixed + which_ref[:, j : j + 1] * line
    act = mixed * (1.0 / (1.0 + jnp.exp(-mixed)))
    act_ref[...] = act
    turn = (((1,), (1,)), ((), ()))
    partial = lax.dot_general(act.astype(BF16), mix_ref[...], turn, preferred_element_type=F32)
    rank = 2 * LANES
    high = partial.astype(BF16).astype(F32)
    low = (partial - high)[:, rank:]
    fill = jnp.zeros((requests, LANES - 2 * low.shape[1]), F32)
    tail = jnp.concatenate([high[:, rank:], low, fill], axis=1)
    experts, replicas = out_ref.shape[0], moved_ref.shape[0]
    lane = lax.broadcasted_iota(jnp.int32, (SUB, LANES), 1)
    steps = [
        high[h * SUB : (h + 1) * SUB, b * LANES : (b + 1) * LANES].astype(BF16) for h in range(2) for b in range(2)
    ]
    for f in range(PLANE):
        for q in range(2):
            block = moved_ref[(f - FIRST[1]) % replicas, MIG + 1 + q].astype(F32)
            for z in range(1, replicas // PLANE):
                block = block + moved_ref[(z * PLANE + f - FIRST[1]) % replicas, MIG + 1 + q].astype(F32)
            e = (2 * f + q - FIRST[2]) % experts
            for n, step in enumerate(steps):
                out_ref[e, n] = step
            for h, part in enumerate((pltpu.roll(block, LANES // 2, 1), block)):
                rows = tail[h * SUB : (h + 1) * SUB]
                out_ref[e, len(steps) + h] = jnp.where(lane < LANES // 2, rows, part).astype(BF16)


def _ready_body(
    requests, states, rep_ref, anchor_ref, routes_ref, share_ref, moved_ref, act_ref, gate_ref, scan_ref, step_ref,
    bias_ref, decay_ref, skip_ref, old_ref, rate_ref, gate_out_ref, skip_out_ref, step_out_ref, bias_out_ref,
    share_out_ref, arr_ref, count_ref,
):
    slots = _slots(rep_ref, anchor_ref, requests)
    blocks = act_ref.shape[1] // LANES
    rows_each = states * blocks // moved_ref.shape[0]
    per_block = states // rows_each
    for i in range(moved_ref.shape[0]):
        b, q = i // per_block, i % per_block
        tail = moved_ref[_piece(i, moved_ref.shape[0]), MIG].astype(F32)
        for j in range(MIG):
            at = j * (SUB // MIG)
            arr_ref[j, q * rows_each : (q + 1) * rows_each, b * LANES : (b + 1) * LANES] = tail[at : at + rows_each]
    for g, (_, local, arrived, order) in enumerate(slots):
        old_ref[g] = jnp.where(arrived, arr_ref[order], scan_ref[local])
    rate_ref[...] = -jnp.exp(decay_ref[...])
    gate = gate_ref[...].astype(F32)
    gate_out_ref[...] = gate * (1.0 / (1.0 + jnp.exp(-gate)))
    skip_out_ref[...] = skip_ref[...] * act_ref[...]
    step_out_ref[...] = step_ref[...]
    bias_out_ref[...] = jnp.broadcast_to(bias_ref[...], bias_out_ref.shape)
    experts = count_ref.shape[0]
    for e in range(experts):
        count_ref[e] = 0
    row = lax.broadcasted_iota(jnp.int32, (requests, LANES), 0)
    col = lax.broadcasted_iota(jnp.int32, (requests, LANES), 1)
    share = jnp.zeros((requests, LANES), F32)
    for t in range(requests):
        for k in range(routes_ref.shape[0]):
            e = routes_ref[k, t]
            place = count_ref[e]
            count_ref[e] = place + 1
            share = share + jnp.where((row == t) & (col == (e + experts - FIRST[2]) % experts * SUB + place), share_ref[k, t], 0.0)
    share_out_ref[...] = share


def _final_body(
    states, sums_ref, act_ref, old_ref, rate_ref, gate_ref, skip_ref, step_ref, bias_ref, share_ref,
    gated_ref, mix_ref, y_ref,
):
    experts = sums_ref.shape[0]
    requests, _ = act_ref.shape
    totals = []
    for n in range(sums_ref.shape[1]):
        total = sums_ref[0, n].astype(F32)
        for e in range(1, experts):
            total = total + sums_ref[e, n].astype(F32)
        totals.append(total)
    projected = jnp.concatenate(
        [jnp.concatenate(totals[0:2], axis=1), jnp.concatenate(totals[2:4], axis=1)], axis=0
    )
    step = jnp.dot(projected.astype(BF16), step_ref[...], preferred_element_type=F32) + bias_ref[0:1]
    step = jnp.maximum(step, 0.0) + jnp.log1p(jnp.exp(-jnp.abs(step)))
    tail = jnp.concatenate(totals[4:6], axis=0)
    columns = jnp.transpose(tail + pltpu.roll(tail, LANES - 2 * states, 1))
    rest = share_ref[...]
    parts = []
    for _ in range(3):
        part = rest.astype(BF16).astype(F32)
        parts.append(part)
        rest = rest - part
    lane = lax.broadcasted_iota(jnp.int32, (SUB, LANES), 1)
    outs = []
    for e in range(experts):
        left = pltpu.roll(sums_ref[e, 4].astype(F32), LANES // 2, 1)
        outs.append(jnp.where(lane < LANES // 2, left, sums_ref[e, 5].astype(F32)))
    outs = jnp.concatenate(outs, axis=0).astype(BF16)
    both = jnp.concatenate([*parts, *(pltpu.roll(p, SUB // 2, 1) for p in parts)], axis=0).astype(BF16)
    terms = jnp.dot(both, outs, preferred_element_type=F32)
    halves = [
        sum(terms[(3 * h + i) * requests : (3 * h + i + 1) * requests] for i in reversed(range(3))) for h in range(2)
    ]
    mix_ref[...] = jnp.concatenate(halves, axis=1).astype(BF16)
    rate = rate_ref[...]
    flow = step * act_ref[...]
    for g in range(requests):
        inflow = columns[0:states, g : g + 1]
        readout = columns[states : 2 * states, g : g + 1]
        state = jnp.exp(step[g : g + 1] * rate) * old_ref[g] + inflow * flow[g : g + 1]
        y_ref[g : g + 1, :] = jnp.sum(readout * state, axis=0, keepdims=True)
    gated_ref[...] = ((y_ref[...] + skip_ref[...]) * gate_ref[...]).astype(BF16)


def _attend_body(
    requests, rep_ref, anchor_ref, len_ref, table_ref, query_ref, key_ref, value_ref, pool_ref, moved_ref, dep_ref,
    out_ref, pages_ref, keys_ref, values_ref,
):
    turn = (((1,), (1,)), ((), ()))
    head = key_ref.shape[1]
    heads = query_ref.shape[1] // head
    pool, _, _, page, _ = pool_ref.shape
    table = table_ref[...].astype(F32).astype(BF16)
    pages = table.shape[0]
    span = pages * page
    slots = _slots(rep_ref, anchor_ref, requests)
    row1 = lax.broadcasted_iota(jnp.int32, (requests, 1), 0)
    row = lax.broadcasted_iota(jnp.int32, (requests, requests), 0)
    col = lax.broadcasted_iota(jnp.int32, (requests, requests), 1)
    live = jnp.zeros((requests, 1), jnp.int32)
    order = jnp.full((requests, 1), -1, jnp.int32)
    pick = jnp.zeros((requests, requests), F32)
    live_of = [jnp.int32(0)] * MIG
    for g, (a, local, arrived, place) in enumerate(slots):
        length = len_ref[a]
        live = jnp.where(row1 == g, length, live)
        order = jnp.where((row1 == g) & arrived, place, order)
        pick = jnp.where((row == g) & (col == local), 1.0, pick)
        live_of = [jnp.where(arrived & (place == j), length, live_of[j]) for j in range(MIG)]
    mine = lax.dot_general(pick.astype(BF16), table, turn, preferred_element_type=F32).astype(jnp.int32)
    here = jnp.where(order < 0, live, 0)
    at = lax.broadcasted_iota(jnp.int32, (requests, pool * page), 1)
    which, token = at // page, at % page
    seen = jnp.zeros((requests, pool * page), jnp.bool_)
    for m in range(pages):
        seen = seen | ((mine[:, m : m + 1] == which) & (token + m * page < here))
    at = lax.broadcasted_iota(jnp.int32, (requests, MIG * span), 1)
    seen_moved = (at // span == order) & (at % span < live)
    down = lax.broadcasted_iota(jnp.int32, (span, head), 0)
    for i in range(moved_ref.shape[0]):
        m, c, h = i // 4, i // 2 % 2, i % 2
        ref = (keys_ref, values_ref)[c]
        for j in range(MIG):
            start = j * span + m * page + h * SUB
            ref[start : start + SUB, :] = moved_ref[_piece(i, moved_ref.shape[0]), j].astype(F32)
    for j in range(MIG):
        for c, ref in ((0, keys_ref), (1, values_ref)):
            block = ref[j * span : (j + 1) * span, :]
            pages_ref[j, 0, c] = jnp.where(down < live_of[j], block, 0.0).astype(BF16)
    moved_keys = keys_ref[...].astype(BF16)
    moved_values = values_ref[...].astype(BF16)
    pool_keys = pool_ref[:, 0, 0].reshape(pool * page, head)
    pool_values = pool_ref[:, 0, 1].reshape(pool * page, head)
    query = query_ref[...]
    queries = jnp.concatenate([query[:, h * head : (h + 1) * head] for h in range(heads)], axis=0)
    scale = 1.0 / math.sqrt(head)
    scores = lax.dot_general(queries, pool_keys, turn, preferred_element_type=F32) * scale
    scores_moved = lax.dot_general(queries, moved_keys, turn, preferred_element_type=F32) * scale
    new_key = jnp.concatenate([key_ref[...].astype(F32)] * heads, axis=0)
    new_value = jnp.concatenate([value_ref[...].astype(F32)] * heads, axis=0)
    own = jnp.sum(queries.astype(F32) * new_key, axis=1, keepdims=True) * scale
    far = F32(-1e30)
    seen = jnp.concatenate([jnp.where(seen, 1.0, 0.0)] * heads, axis=0) > 0.5
    seen_moved = jnp.concatenate([jnp.where(seen_moved, 1.0, 0.0)] * heads, axis=0) > 0.5
    scores = jnp.where(seen, scores, far)
    scores_moved = jnp.where(seen_moved, scores_moved, far)
    highest = jnp.maximum(
        jnp.maximum(jnp.max(scores, axis=1, keepdims=True), jnp.max(scores_moved, axis=1, keepdims=True)), own
    )
    e_pool = jnp.exp(scores - highest)
    e_moved = jnp.exp(scores_moved - highest)
    e_own = jnp.exp(own - highest)
    total = jnp.sum(e_pool, axis=1, keepdims=True) + jnp.sum(e_moved, axis=1, keepdims=True) + e_own
    w_pool = (e_pool / total).astype(BF16)
    w_moved = (e_moved / total).astype(BF16)
    w_own = (e_own / total).astype(BF16).astype(F32)
    context = jnp.dot(w_pool, pool_values, preferred_element_type=F32)
    context = context + jnp.dot(w_moved, moved_values, preferred_element_type=F32) + w_own * new_value
    for h in range(heads):
        out_ref[:, h * head : (h + 1) * head] = context[h * requests : (h + 1) * requests].astype(BF16)


def per_device(
    query,
    new_key,
    new_value,
    page_pool,
    block_table,
    lengths,
    anchor,
    conv_input,
    gate_input,
    window_state,
    scan_state,
    filter_taps,
    filter_bias,
    mix_weight,
    step_weight,
    step_bias,
    log_decay,
    skip_gain,
    routes,
    route_weight,
    expert_hidden,
    down_weight,
):
    requests, channels = query.shape
    replicas = lax.axis_size("rep")
    experts = lax.axis_size("exp")
    rep = lax.axis_index("rep").astype(jnp.int32).reshape(1)
    states = log_decay.shape[0]
    head = new_key.shape[1]
    pages, page = block_table.shape[1], page_pool.shape[3]
    slots = expert_hidden.shape[1]
    features = down_weight.shape[2]
    table = block_table.T
    window = jnp.transpose(window_state, (1, 0, 2))

    packed, keep, send = _call(
        lambda *refs: _pack_body(requests, *refs),
        "pack_leaving",
        [
            _shape((replicas, MIG + 1, SUB, LANES), BF16),
            _shape((slots, features // 2), BF16),
            _shape((slots, features // 2), BF16),
        ],
        [_smem()] * 3 + [_hbm()] * 5,
        [_vmem()] * 3,
        (rep, anchor, table, page_pool, window, scan_state, expert_hidden, down_weight),
        scratch=[
            pltpu.VMEM((MIG, states, channels), F32),
            pltpu.VMEM((MIG, pages, 2, page, head), BF16),
            pltpu.VMEM(window.shape, BF16),
            pltpu.VMEM(expert_hidden.shape[1:], BF16),
            pltpu.VMEM((PLANE, down_weight.shape[1], features // PLANE), BF16),
            pltpu.SemaphoreType.DMA((2 + MIG * (1 + pages) + PLANE,)),
        ],
        us=4,
        room=60,
    )
    turned = _turned(replicas, FIRST[0])
    spread = lax.all_to_all(packed, "rep", split_axis=0, concat_axis=0, tiled=True, axis_index_groups=turned)

    def at(z, x, c):
        return (z * 4 + x) * 2 + c

    every = [(z, x, c) for z in range(4) for x in range(4) for c in range(2)]
    got = lax.ppermute(send, "rep", [(at(z, x, c), at(z, x, 1 - c)) for z, x, c in every])
    width = features // PLANE
    by_x = _call(
        _fold_body,
        "fold_cores",
        [_shape((slots, width), F32)] + [_shape((slots, width), BF16)] * 3,
        [_vmem()] * 2,
        [_vmem()] * 4,
        (keep, got),
        us=0.5,
    )
    came = [by_x[0]] + [
        lax.ppermute(by_x[k], "rep", [(at(z, x, c), at(z, (x + k) % 4, c)) for z, x, c in every]) for k in (2, 1, 3)
    ]

    index = _call(
        lambda *refs: _route_body(requests, *refs),
        "route_pieces",
        _shape((replicas, LANES), jnp.int32),
        [_vmem(), _any()],
        _vmem(),
        (anchor.reshape(replicas, requests), by_x[0]),
        us=1,
    )
    base, which, taps, mix = _call(
        lambda *refs: _local_body(requests, *refs),
        "filter_local",
        [
            _shape((requests, channels), F32),
            _shape((requests, LANES), F32),
            _shape(filter_taps.shape, F32),
            _shape(mix_weight.shape[::-1], BF16),
        ],
        [_smem()] * 2 + [_vmem()] * 5 + [_any()],
        [_vmem()] * 4,
        (rep, anchor, window, conv_input, filter_taps, filter_bias.reshape(1, channels), mix_weight.T, index),
        us=1.5,
    )
    onward = _call(
        _select_body,
        "select_pieces",
        _shape((replicas, MIG + 3, SUB, LANES), BF16),
        [_smem()] + [_vmem()] * 5 + [_any()],
        _vmem(),
        (index, spread, *came, which),
        us=1.5,
    )
    turned = _turned(replicas, FIRST[1])
    moved = lax.all_to_all(onward, "rep", split_axis=0, concat_axis=0, tiled=True, axis_index_groups=turned)

    sums, act = _call(
        _act_body,
        "filter_and_project",
        [_shape((experts, 6, SUB, LANES), BF16), _shape((requests, channels), F32)],
        [_vmem()] * 5,
        [_vmem()] * 2,
        (moved, base, which, taps, mix),
        scratch=[pltpu.VMEM((SUB, channels), F32)],
        us=1.5,
    )
    turned = _turned(experts, FIRST[2])
    sums_all = lax.all_to_all(sums, "exp", split_axis=0, concat_axis=0, tiled=True, axis_index_groups=turned)

    attended, pages_out = _call(
        lambda *refs: _attend_body(requests, *refs),
        "attend",
        [_shape((requests, channels), BF16), _shape((MIG, 1, 2, pages * page, head), BF16)],
        [_smem()] * 3 + [_vmem()] * 6 + [_any()],
        [_vmem()] * 2,
        (rep, anchor, lengths, table, query, new_key, new_value, page_pool, moved, act),
        scratch=[pltpu.VMEM((MIG * pages * page, head), F32)] * 2,
        us=2,
    )
    ready = _call(
        lambda *refs: _ready_body(requests, states, *refs),
        "ready_state",
        [
            _shape((requests, states, channels), F32),
            _shape((states, channels), F32),
            _shape((requests, channels), F32),
            _shape((requests, channels), F32),
            _shape(step_weight.shape, BF16),
            _shape((SUB, channels), F32),
            _shape((requests, LANES), F32),
        ],
        [_smem()] * 4 + [_vmem()] * 8,
        [_vmem()] * 7,
        (
            rep, anchor, routes.T, route_weight.T, moved, act, gate_input, scan_state, step_weight,
            step_bias.reshape(1, channels), log_decay, skip_gain.reshape(1, channels),
        ),
        scratch=[pltpu.VMEM((MIG, states, channels), F32), pltpu.SMEM((experts,), jnp.int32)],
        us=2,
    )
    gated, mixed = _call(
        lambda *refs: _final_body(states, *refs),
        "update_state",
        [_shape((requests, channels), BF16), _shape((requests, features // experts), BF16)],
        [_vmem()] * 9,
        [_vmem()] * 2,
        (sums_all, act, *ready),
        scratch=[pltpu.VMEM((requests, channels), F32)],
        us=2,
    )
    return (attended, pages_out, gated, mixed)


def solution(mesh):
    placed = (
        P("rep", "exp"),
        P("rep", "exp"),
        P("rep", "exp"),
        P("rep", "exp", None, None, None),
        P("rep", None),
        P(),
        P(),
        P("rep", "exp"),
        P("rep", "exp"),
        P("rep", None, "exp"),
        P("rep", None, "exp"),
        P(None, "exp"),
        P("exp"),
        P("exp", None),
        P(None, "exp"),
        P("exp"),
        P(None, "exp"),
        P("exp"),
        P("rep", None),
        P("rep", None),
        P("exp", None, "rep"),
        P("exp", "rep", None),
    )
    return jax.shard_map(
        per_device,
        mesh=mesh,
        in_specs=placed,
        out_specs=(
            P("rep", "exp"),
            P("rep", "exp", None, None, None),
            P("rep", "exp"),
            P("rep", "exp"),
        ),
        check_vma=False,
    )
```

```python
import math

import jax
import jax.numpy as jnp
from jax import lax
from jax.experimental import pallas as pl
from jax.experimental.pallas import tpu as pltpu
from jax.sharding import PartitionSpec as P

MIG = 2
LANES = 128
SUB = 8
ROWS = 16
PLANE = 8
FIRST = (20, 4, 10)
F32 = jnp.float32
BF16 = jnp.bfloat16


def _smem():
    return pl.BlockSpec(memory_space=pltpu.SMEM)


def _vmem():
    return pl.BlockSpec(memory_space=pltpu.VMEM)


def _any():
    return pl.BlockSpec(memory_space=pl.ANY)


def _hbm():
    return pl.BlockSpec(memory_space=pltpu.HBM)


def _shape(shape, dtype):
    return jax.ShapeDtypeStruct(shape, dtype)


def _call(body, name, out_shape, ins, outs, args, scratch=(), us=1.0, room=32):
    return pl.pallas_call(
        body,
        name=name,
        out_shape=out_shape,
        in_specs=ins,
        out_specs=outs,
        scratch_shapes=list(scratch),
        compiler_params=pltpu.CompilerParams(vmem_limit_bytes=room * 1024 * 1024),
        cost_estimate=pl.CostEstimate(flops=0, bytes_accessed=int(us * 3.5e6), transcendentals=0),
    )(*args)


def _turned(size, first):
    return [[(k + first) % size for k in range(size)]]


def _present(anchor_ref, base, requests):
    mask = jnp.int32(0)
    for g in range(requests):
        a = anchor_ref[base + g] - base
        inside = (a >= 0) & (a < requests)
        mask = mask | jnp.where(inside, jnp.int32(1) << jnp.clip(a, 0, requests - 1), 0)
    return mask


def _slots(rep_ref, anchor_ref, requests):
    base = rep_ref[0] * requests
    count = jnp.int32(0)
    found = []
    for g in range(requests):
        a = anchor_ref[base + g]
        local = a - base
        arrived = (local < 0) | (local >= requests)
        found.append((a, jnp.clip(local, 0, requests - 1), arrived, jnp.minimum(count, MIG - 1)))
        count = count + jnp.where(arrived, 1, 0)
    return found


def _pack_body(
    requests, rep_ref, anchor_ref, table_ref, pool_ref, window_ref, scan_ref, hidden_ref, weight_ref,
    out_ref, keep_ref, send_ref, scans_ref, pages_ref, win_ref, rows_ref, blocks_ref, sems,
):
    pages = table_ref.shape[0]
    taps, _, channels = window_ref.shape
    blocks = channels // LANES
    plane = PLANE
    width = weight_ref.shape[2] // plane
    r = rep_ref[0]
    x, core = (r // 2) % 4, r % 2
    hidden_copy = pltpu.make_async_copy(hidden_ref.at[0], rows_ref, sems.at[plane])
    hidden_copy.start()
    weights = []
    order = (4, 5, 6, 7, 0, 1, 2, 3)
    for f, p in enumerate(order):
        block = ((x + p) % 4) * 2 + (core + p // 4) % 2
        columns = pl.ds(pl.multiple_of(block * width, width), width)
        weights.append(
            pltpu.make_async_copy(weight_ref.at[0, :, columns], blocks_ref.at[f], sems.at[f])
        )
        weights[-1].start()
    copies = [pltpu.make_async_copy(window_ref, win_ref, sems.at[plane + 1])]
    copies[0].start()
    base = rep_ref[0] * requests
    mask = _present(anchor_ref, base, requests)
    first, second = jnp.int32(0), jnp.int32(0)
    for o in reversed(range(requests)):
        leaves = ((mask >> o) & 1) == 0
        second = jnp.where(leaves, first, second)
        first = jnp.where(leaves, o, first)
    leaving = (first, second)
    for j, o in enumerate(leaving):
        copies.append(pltpu.make_async_copy(scan_ref.at[o], scans_ref.at[j], sems.at[plane + 1 + len(copies)]))
        copies[-1].start()
        for m in range(pages):
            page = pool_ref.at[table_ref[m, o], 0]
            copies.append(pltpu.make_async_copy(page, pages_ref.at[j, m], sems.at[plane + 1 + len(copies)]))
            copies[-1].start()
    hidden_copy.wait()
    hidden = rows_ref[...]
    for f, p in enumerate(order):
        weights[f].wait()
        total = jnp.dot(hidden, blocks_ref[f], preferred_element_type=F32)
        at = slice(p % 4 * width, (p % 4 + 1) * width)
        if p < 4:
            keep_ref[:, at] = total.astype(BF16)
        else:
            send_ref[:, at] = total.astype(BF16)
    for copy in copies:
        copy.wait()
    row = lax.broadcasted_iota(jnp.int32, (requests, channels), 0)
    wins = []
    for j, o in enumerate(leaving):
        lines = [
            jnp.sum(jnp.where(row == o, win_ref[t].astype(F32), 0.0), axis=0, keepdims=True) for t in range(taps)
        ]
        wins.append([line[:, b * LANES : (b + 1) * LANES] for line in lines for b in range(blocks)])
    rows_each = scans_ref.shape[1] * blocks // out_ref.shape[0]
    per_block = scans_ref.shape[1] // rows_each
    blank = jnp.zeros((1, LANES), F32)
    for i in range(out_ref.shape[0]):
        b, q = i // per_block, i % per_block
        tail = []
        for j in range(MIG):
            tail.append(scans_ref[j, q * rows_each : (q + 1) * rows_each, b * LANES : (b + 1) * LANES])
            tail.append(wins[j][i] if i < len(wins[j]) else blank)
            tail.extend([blank] * (SUB // MIG - rows_each - 1))
        m, c, h = i // 4, i // 2 % 2, i % 2
        heads = [pages_ref[j, m, c].astype(F32)[h * SUB : (h + 1) * SUB] for j in range(MIG)]
        for j in range(MIG):
            out_ref[i, j] = heads[j].astype(BF16)
        out_ref[i, MIG] = jnp.concatenate(tail, axis=0).astype(BF16)


def _route_body(requests, anchor_ref, dep_ref, out_ref):
    anchors = anchor_ref[...]
    replicas = anchors.shape[0]
    home = lax.broadcasted_iota(jnp.int32, anchors.shape, 0)
    place = lax.broadcasted_iota(jnp.int32, anchors.shape, 1).astype(F32)
    source = anchors // requests
    bit = (jnp.int32(1) << (anchors - source * requests)).astype(F32)
    arrived = source != home
    staying = jnp.sum(jnp.where(arrived, 0.0, bit), axis=1, keepdims=True).astype(jnp.int32)
    first = ((~staying) & (staying + 1)).astype(F32)
    lowest = jnp.zeros(anchors.shape, F32)
    for s in range(replicas):
        lowest = jnp.where(source == s, first[s : s + 1], lowest)
    place_of = (source + replicas - FIRST[0]) % replicas
    item = (place_of * MIG).astype(F32) + jnp.where(lowest != bit, 1.0, 0.0)
    early = jnp.min(jnp.where(arrived, place, 99.0), axis=1, keepdims=True)
    one = jnp.sum(jnp.where(arrived & (place == early), item, 0.0), axis=1, keepdims=True)
    two = jnp.sum(jnp.where(arrived & (place != early), item, 0.0), axis=1, keepdims=True)
    lane = lax.broadcasted_iota(jnp.int32, out_ref.shape, 1)
    out_ref[...] = jnp.where(lane == 0, one, jnp.where(lane == 1, two, 0.0)).astype(jnp.int32)


def _fold_body(keep_ref, got_ref, o0, o1, o2, o3):
    width = o0.shape[1]
    for k, o in enumerate((o0, o1, o2, o3)):
        at = slice(k * width, (k + 1) * width)
        o[...] = (keep_ref[:, at].astype(F32) + got_ref[:, at].astype(F32)).astype(o.dtype)


def _piece(i, replicas):
    return (i + FIRST[0] - FIRST[1]) % replicas


def _select_body(index_ref, in_ref, e0, e1, e2, e3, dep_ref, out_ref):
    replicas = out_ref.shape[0]
    row = lax.broadcasted_iota(jnp.int32, (SUB, LANES), 0)
    half = SUB // MIG
    cap = e0.shape[0] // replicas
    blocks = e0.shape[1] // LANES
    total = (e0[...] + e1[...].astype(F32)) + (e2[...].astype(F32) + e3[...].astype(F32))
    for t in range(replicas):
        d = (t + FIRST[1]) % replicas
        tails = []
        for j in range(MIG):
            i = index_ref[d, j]
            rank = i % MIG
            out_ref[t, j] = in_ref[i // MIG, rank]
            tail = in_ref[i // MIG, MIG].astype(F32)
            tails.append(jnp.where(rank == j, tail, pltpu.roll(tail, half, 0)))
        tail = jnp.where(row < half, tails[0], tails[1])
        rows = total[d * cap : (d + 1) * cap]
        experts = [rows[:, b * LANES : (b + 1) * LANES] for b in range(blocks)]
        out_ref[t, MIG] = tail.astype(BF16)
        for h in range(2):
            pair = experts[h * blocks // 2 : (h + 1) * blocks // 2]
            out_ref[t, MIG + 1 + h] = jnp.concatenate(pair, axis=0).astype(BF16)


def _local_body(
    requests, rep_ref, anchor_ref, window_ref, conv_ref, taps_ref, bias_ref, mix_ref, dep_ref,
    base_ref, which_ref, taps_out_ref, mix_out_ref,
):
    taps = window_ref.shape[0]
    weights = taps_ref[...]
    row = lax.broadcasted_iota(jnp.int32, (requests, requests), 0)
    col = lax.broadcasted_iota(jnp.int32, (requests, requests), 1)
    row_w = lax.broadcasted_iota(jnp.int32, which_ref.shape, 0)
    col_w = lax.broadcasted_iota(jnp.int32, which_ref.shape, 1)
    pick = jnp.zeros((requests, requests), F32)
    which = jnp.zeros(which_ref.shape, F32)
    for g, (_, local, arrived, order) in enumerate(_slots(rep_ref, anchor_ref, requests)):
        pick = jnp.where((row == g) & (col == local) & ~arrived, 1.0, pick)
        which = jnp.where((row_w == g) & (col_w == order) & arrived, 1.0, which)
    pick = pick.astype(BF16)
    mixed = conv_ref[...].astype(F32) * weights[taps : taps + 1] + bias_ref[...]
    for t in range(taps):
        mixed = mixed + jnp.dot(pick, window_ref[t], preferred_element_type=F32) * weights[t : t + 1]
    base_ref[...] = mixed
    which_ref[...] = which
    taps_out_ref[...] = weights
    mix_out_ref[...] = mix_ref[...]


def _act_body(moved_ref, base_ref, which_ref, taps_ref, mix_ref, out_ref, act_ref, win_ref):
    requests, channels = base_ref.shape
    blocks = channels // LANES
    weights = taps_ref[...]
    taps = weights.shape[0] - 1
    mixed = base_ref[...]
    for j in range(MIG):
        for t in range(taps):
            for b in range(blocks):
                at = j * (SUB // MIG) + 2
                tile = moved_ref[_piece(t * blocks + b, moved_ref.shape[0]), MIG].astype(F32)
                win_ref[t : t + 1, b * LANES : (b + 1) * LANES] = tile[at : at + 1]
        line = jnp.sum(win_ref[0:taps, :] * weights[0:taps], axis=0, keepdims=True)
        mixed = mixed + which_ref[:, j : j + 1] * line
    act = mixed * (1.0 / (1.0 + jnp.exp(-mixed)))
    act_ref[...] = act
    turn = (((1,), (1,)), ((), ()))
    partial = lax.dot_general(act.astype(BF16), mix_ref[...], turn, preferred_element_type=F32)
    rank = 2 * LANES
    high = partial.astype(BF16).astype(F32)
    low = (partial - high)[:, rank:]
    fill = jnp.zeros((requests, LANES - 2 * low.shape[1]), F32)
    tail = jnp.concatenate([high[:, rank:], low, fill], axis=1)
    experts, replicas = out_ref.shape[0], moved_ref.shape[0]
    lane = lax.broadcasted_iota(jnp.int32, (SUB, LANES), 1)
    steps = [
        high[h * SUB : (h + 1) * SUB, b * LANES : (b + 1) * LANES].astype(BF16) for h in range(2) for b in range(2)
    ]
    for f in range(PLANE):
        for q in range(2):
            block = moved_ref[(f - FIRST[1]) % replicas, MIG + 1 + q].astype(F32)
            for z in range(1, replicas // PLANE):
                block = block + moved_ref[(z * PLANE + f - FIRST[1]) % replicas, MIG + 1 + q].astype(F32)
            e = (2 * f + q - FIRST[2]) % experts
            for n, step in enumerate(steps):
                out_ref[e, n] = step
            for h, part in enumerate((pltpu.roll(block, LANES // 2, 1), block)):
                rows = tail[h * SUB : (h + 1) * SUB]
                out_ref[e, len(steps) + h] = jnp.where(lane < LANES // 2, rows, part).astype(BF16)


def _ready_body(
    requests, states, rep_ref, anchor_ref, routes_ref, share_ref, moved_ref, act_ref, gate_ref, scan_ref, step_ref,
    bias_ref, decay_ref, skip_ref, old_ref, rate_ref, gate_out_ref, skip_out_ref, step_out_ref, bias_out_ref,
    share_out_ref, arr_ref, count_ref,
):
    slots = _slots(rep_ref, anchor_ref, requests)
    blocks = act_ref.shape[1] // LANES
    rows_each = states * blocks // moved_ref.shape[0]
    per_block = states // rows_each
    for i in range(moved_ref.shape[0]):
        b, q = i // per_block, i % per_block
        tail = moved_ref[_piece(i, moved_ref.shape[0]), MIG].astype(F32)
        for j in range(MIG):
            at = j * (SUB // MIG)
            arr_ref[j, q * rows_each : (q + 1) * rows_each, b * LANES : (b + 1) * LANES] = tail[at : at + rows_each]
    for g, (_, local, arrived, order) in enumerate(slots):
        old_ref[g] = jnp.where(arrived, arr_ref[order], scan_ref[local])
    rate_ref[...] = -jnp.exp(decay_ref[...])
    gate = gate_ref[...].astype(F32)
    gate_out_ref[...] = gate * (1.0 / (1.0 + jnp.exp(-gate)))
    skip_out_ref[...] = skip_ref[...] * act_ref[...]
    step_out_ref[...] = step_ref[...]
    bias_out_ref[...] = jnp.broadcast_to(bias_ref[...], bias_out_ref.shape)
    experts = count_ref.shape[0]
    for e in range(experts):
        count_ref[e] = 0
    row = lax.broadcasted_iota(jnp.int32, (requests, LANES), 0)
    col = lax.broadcasted_iota(jnp.int32, (requests, LANES), 1)
    share = jnp.zeros((requests, LANES), F32)
    for t in range(requests):
        for k in range(routes_ref.shape[0]):
            e = routes_ref[k, t]
            place = count_ref[e]
            count_ref[e] = place + 1
            share = share + jnp.where((row == t) & (col == (e + experts - FIRST[2]) % experts * SUB + place), share_ref[k, t], 0.0)
    share_out_ref[...] = share


def _final_body(
    states, sums_ref, act_ref, old_ref, rate_ref, gate_ref, skip_ref, step_ref, bias_ref, share_ref,
    gated_ref, mix_ref, y_ref,
):
    experts = sums_ref.shape[0]
    requests, _ = act_ref.shape
    totals = []
    for n in range(sums_ref.shape[1]):
        total = sums_ref[0, n].astype(F32)
        for e in range(1, experts):
            total = total + sums_ref[e, n].astype(F32)
        totals.append(total)
    projected = jnp.concatenate(
        [jnp.concatenate(totals[0:2], axis=1), jnp.concatenate(totals[2:4], axis=1)], axis=0
    )
    step = jnp.dot(projected.astype(BF16), step_ref[...], preferred_element_type=F32) + bias_ref[0:1]
    step = jnp.maximum(step, 0.0) + jnp.log1p(jnp.exp(-jnp.abs(step)))
    tail = jnp.concatenate(totals[4:6], axis=0)
    columns = jnp.transpose(tail + pltpu.roll(tail, LANES - 2 * states, 1))
    rest = share_ref[...]
    parts = []
    for _ in range(3):
        part = rest.astype(BF16).astype(F32)
        parts.append(part)
        rest = rest - part
    lane = lax.broadcasted_iota(jnp.int32, (SUB, LANES), 1)
    outs = []
    for e in range(experts):
        left = pltpu.roll(sums_ref[e, 4].astype(F32), LANES // 2, 1)
        outs.append(jnp.where(lane < LANES // 2, left, sums_ref[e, 5].astype(F32)))
    outs = jnp.concatenate(outs, axis=0).astype(BF16)
    both = jnp.concatenate([*parts, *(pltpu.roll(p, SUB // 2, 1) for p in parts)], axis=0).astype(BF16)
    terms = jnp.dot(both, outs, preferred_element_type=F32)
    halves = [
        sum(terms[(3 * h + i) * requests : (3 * h + i + 1) * requests] for i in reversed(range(3))) for h in range(2)
    ]
    mix_ref[...] = jnp.concatenate(halves, axis=1).astype(BF16)
    rate = rate_ref[...]
    flow = step * act_ref[...]
    for g in range(requests):
        inflow = columns[0:states, g : g + 1]
        readout = columns[states : 2 * states, g : g + 1]
        state = jnp.exp(step[g : g + 1] * rate) * old_ref[g] + inflow * flow[g : g + 1]
        y_ref[g : g + 1, :] = jnp.sum(readout * state, axis=0, keepdims=True)
    gated_ref[...] = ((y_ref[...] + skip_ref[...]) * gate_ref[...]).astype(BF16)


def _attend_body(
    requests, rep_ref, anchor_ref, len_ref, table_ref, query_ref, key_ref, value_ref, pool_ref, moved_ref, dep_ref,
    out_ref, pages_ref, keys_ref, values_ref,
):
    turn = (((1,), (1,)), ((), ()))
    head = key_ref.shape[1]
    heads = query_ref.shape[1] // head
    pool, _, _, page, _ = pool_ref.shape
    table = table_ref[...].astype(F32).astype(BF16)
    pages = table.shape[0]
    span = pages * page
    slots = _slots(rep_ref, anchor_ref, requests)
    row1 = lax.broadcasted_iota(jnp.int32, (requests, 1), 0)
    row = lax.broadcasted_iota(jnp.int32, (requests, requests), 0)
    col = lax.broadcasted_iota(jnp.int32, (requests, requests), 1)
    live = jnp.zeros((requests, 1), jnp.int32)
    order = jnp.full((requests, 1), -1, jnp.int32)
    pick = jnp.zeros((requests, requests), F32)
    live_of = [jnp.int32(0)] * MIG
    for g, (a, local, arrived, place) in enumerate(slots):
        length = len_ref[a]
        live = jnp.where(row1 == g, length, live)
        order = jnp.where((row1 == g) & arrived, place, order)
        pick = jnp.where((row == g) & (col == local), 1.0, pick)
        live_of = [jnp.where(arrived & (place == j), length, live_of[j]) for j in range(MIG)]
    mine = lax.dot_general(pick.astype(BF16), table, turn, preferred_element_type=F32).astype(jnp.int32)
    here = jnp.where(order < 0, live, 0)
    at = lax.broadcasted_iota(jnp.int32, (requests, pool * page), 1)
    which, token = at // page, at % page
    seen = jnp.zeros((requests, pool * page), jnp.bool_)
    for m in range(pages):
        seen = seen | ((mine[:, m : m + 1] == which) & (token + m * page < here))
    at = lax.broadcasted_iota(jnp.int32, (requests, MIG * span), 1)
    seen_moved = (at // span == order) & (at % span < live)
    down = lax.broadcasted_iota(jnp.int32, (span, head), 0)
    for i in range(moved_ref.shape[0]):
        m, c, h = i // 4, i // 2 % 2, i % 2
        ref = (keys_ref, values_ref)[c]
        for j in range(MIG):
            start = j * span + m * page + h * SUB
            ref[start : start + SUB, :] = moved_ref[_piece(i, moved_ref.shape[0]), j].astype(F32)
    for j in range(MIG):
        for c, ref in ((0, keys_ref), (1, values_ref)):
            block = ref[j * span : (j + 1) * span, :]
            pages_ref[j, 0, c] = jnp.where(down < live_of[j], block, 0.0).astype(BF16)
    moved_keys = keys_ref[...].astype(BF16)
    moved_values = values_ref[...].astype(BF16)
    pool_keys = pool_ref[:, 0, 0].reshape(pool * page, head)
    pool_values = pool_ref[:, 0, 1].reshape(pool * page, head)
    query = query_ref[...]
    queries = jnp.concatenate([query[:, h * head : (h + 1) * head] for h in range(heads)], axis=0)
    scale = 1.0 / math.sqrt(head)
    scores = lax.dot_general(queries, pool_keys, turn, preferred_element_type=F32) * scale
    scores_moved = lax.dot_general(queries, moved_keys, turn, preferred_element_type=F32) * scale
    new_key = jnp.concatenate([key_ref[...].astype(F32)] * heads, axis=0)
    new_value = jnp.concatenate([value_ref[...].astype(F32)] * heads, axis=0)
    own = jnp.sum(queries.astype(F32) * new_key, axis=1, keepdims=True) * scale
    far = F32(-1e30)
    seen = jnp.concatenate([jnp.where(seen, 1.0, 0.0)] * heads, axis=0) > 0.5
    seen_moved = jnp.concatenate([jnp.where(seen_moved, 1.0, 0.0)] * heads, axis=0) > 0.5
    scores = jnp.where(seen, scores, far)
    scores_moved = jnp.where(seen_moved, scores_moved, far)
    highest = jnp.maximum(
        jnp.maximum(jnp.max(scores, axis=1, keepdims=True), jnp.max(scores_moved, axis=1, keepdims=True)), own
    )
    e_pool = jnp.exp(scores - highest)
    e_moved = jnp.exp(scores_moved - highest)
    e_own = jnp.exp(own - highest)
    total = jnp.sum(e_pool, axis=1, keepdims=True) + jnp.sum(e_moved, axis=1, keepdims=True) + e_own
    w_pool = (e_pool / total).astype(BF16)
    w_moved = (e_moved / total).astype(BF16)
    w_own = (e_own / total).astype(BF16).astype(F32)
    context = jnp.dot(w_pool, pool_values, preferred_element_type=F32)
    context = context + jnp.dot(w_moved, moved_values, preferred_element_type=F32) + w_own * new_value
    for h in range(heads):
        out_ref[:, h * head : (h + 1) * head] = context[h * requests : (h + 1) * requests].astype(BF16)


def per_device(
    query,
    new_key,
    new_value,
    page_pool,
    block_table,
    lengths,
    anchor,
    conv_input,
    gate_input,
    window_state,
    scan_state,
    filter_taps,
    filter_bias,
    mix_weight,
    step_weight,
    step_bias,
    log_decay,
    skip_gain,
    routes,
    route_weight,
    expert_hidden,
    down_weight,
):
    requests, channels = query.shape
    replicas = lax.axis_size("rep")
    experts = lax.axis_size("exp")
    rep = lax.axis_index("rep").astype(jnp.int32).reshape(1)
    states = log_decay.shape[0]
    head = new_key.shape[1]
    pages, page = block_table.shape[1], page_pool.shape[3]
    slots = expert_hidden.shape[1]
    features = down_weight.shape[2]
    table = block_table.T
    window = jnp.transpose(window_state, (1, 0, 2))

    packed, keep, send = _call(
        lambda *refs: _pack_body(requests, *refs),
        "pack_leaving",
        [
            _shape((replicas, MIG + 1, SUB, LANES), BF16),
            _shape((slots, features // 2), BF16),
            _shape((slots, features // 2), BF16),
        ],
        [_smem()] * 3 + [_hbm()] * 5,
        [_vmem()] * 3,
        (rep, anchor, table, page_pool, window, scan_state, expert_hidden, down_weight),
        scratch=[
            pltpu.VMEM((MIG, states, channels), F32),
            pltpu.VMEM((MIG, pages, 2, page, head), BF16),
            pltpu.VMEM(window.shape, BF16),
            pltpu.VMEM(expert_hidden.shape[1:], BF16),
            pltpu.VMEM((PLANE, down_weight.shape[1], features // PLANE), BF16),
            pltpu.SemaphoreType.DMA((2 + MIG * (1 + pages) + PLANE,)),
        ],
        us=4,
        room=60,
    )
    turned = _turned(replicas, FIRST[0])
    spread = lax.all_to_all(packed, "rep", split_axis=0, concat_axis=0, tiled=True, axis_index_groups=turned)

    def at(z, x, c):
        return (z * 4 + x) * 2 + c

    every = [(z, x, c) for z in range(4) for x in range(4) for c in range(2)]
    got = lax.ppermute(send, "rep", [(at(z, x, c), at(z, x, 1 - c)) for z, x, c in every])
    width = features // PLANE
    by_x = _call(
        _fold_body,
        "fold_cores",
        [_shape((slots, width), F32)] + [_shape((slots, width), BF16)] * 3,
        [_vmem()] * 2,
        [_vmem()] * 4,
        (keep, got),
        us=0.5,
    )
    came = [by_x[0]] + [
        lax.ppermute(by_x[k], "rep", [(at(z, x, c), at(z, (x + k) % 4, c)) for z, x, c in every]) for k in (2, 1, 3)
    ]

    index = _call(
        lambda *refs: _route_body(requests, *refs),
        "route_pieces",
        _shape((replicas, LANES), jnp.int32),
        [_vmem(), _any()],
        _vmem(),
        (anchor.reshape(replicas, requests), by_x[0]),
        us=1,
    )
    base, which, taps, mix = _call(
        lambda *refs: _local_body(requests, *refs),
        "filter_local",
        [
            _shape((requests, channels), F32),
            _shape((requests, LANES), F32),
            _shape(filter_taps.shape, F32),
            _shape(mix_weight.shape[::-1], BF16),
        ],
        [_smem()] * 2 + [_vmem()] * 5 + [_any()],
        [_vmem()] * 4,
        (rep, anchor, window, conv_input, filter_taps, filter_bias.reshape(1, channels), mix_weight.T, index),
        us=1.5,
    )
    onward = _call(
        _select_body,
        "select_pieces",
        _shape((replicas, MIG + 3, SUB, LANES), BF16),
        [_smem()] + [_vmem()] * 5 + [_any()],
        _vmem(),
        (index, spread, *came, which),
        us=1.5,
    )
    turned = _turned(replicas, FIRST[1])
    moved = lax.all_to_all(onward, "rep", split_axis=0, concat_axis=0, tiled=True, axis_index_groups=turned)

    sums, act = _call(
        _act_body,
        "filter_and_project",
        [_shape((experts, 6, SUB, LANES), BF16), _shape((requests, channels), F32)],
        [_vmem()] * 5,
        [_vmem()] * 2,
        (moved, base, which, taps, mix),
        scratch=[pltpu.VMEM((SUB, channels), F32)],
        us=1.5,
    )
    turned = _turned(experts, FIRST[2])
    sums_all = lax.all_to_all(sums, "exp", split_axis=0, concat_axis=0, tiled=True, axis_index_groups=turned)

    attended, pages_out = _call(
        lambda *refs: _attend_body(requests, *refs),
        "attend",
        [_shape((requests, channels), BF16), _shape((MIG, 1, 2, pages * page, head), BF16)],
        [_smem()] * 3 + [_vmem()] * 6 + [_any()],
        [_vmem()] * 2,
        (rep, anchor, lengths, table, query, new_key, new_value, page_pool, moved, act),
        scratch=[pltpu.VMEM((MIG * pages * page, head), F32)] * 2,
        us=2,
    )
    ready = _call(
        lambda *refs: _ready_body(requests, states, *refs),
        "ready_state",
        [
            _shape((requests, states, channels), F32),
            _shape((states, channels), F32),
            _shape((requests, channels), F32),
            _shape((requests, channels), F32),
            _shape(step_weight.shape, BF16),
            _shape((SUB, channels), F32),
            _shape((requests, LANES), F32),
        ],
        [_smem()] * 4 + [_vmem()] * 8,
        [_vmem()] * 7,
        (
            rep, anchor, routes.T, route_weight.T, moved, act, gate_input, scan_state, step_weight,
            step_bias.reshape(1, channels), log_decay, skip_gain.reshape(1, channels),
        ),
        scratch=[pltpu.VMEM((MIG, states, channels), F32), pltpu.SMEM((experts,), jnp.int32)],
        us=2,
    )
    gated, mixed = _call(
        lambda *refs: _final_body(states, *refs),
        "update_state",
        [_shape((requests, channels), BF16), _shape((requests, features // experts), BF16)],
        [_vmem()] * 9,
        [_vmem()] * 2,
        (sums_all, act, *ready),
        scratch=[pltpu.VMEM((requests, channels), F32)],
        us=2,
    )
    return (attended, pages_out, gated, mixed)


def solution(mesh):
    placed = (
        P("rep", "exp"),
        P("rep", "exp"),
        P("rep", "exp"),
        P("rep", "exp", None, None, None),
        P("rep", None),
        P(),
        P(),
        P("rep", "exp"),
        P("rep", "exp"),
        P("rep", None, "exp"),
        P("rep", None, "exp"),
        P(None, "exp"),
        P("exp"),
        P("exp", None),
        P(None, "exp"),
        P("exp"),
        P(None, "exp"),
        P("exp"),
        P("rep", None),
        P("rep", None),
        P("exp", None, "rep"),
        P("exp", "rep", None),
    )
    return jax.shard_map(
        per_device,
        mesh=mesh,
        in_specs=placed,
        out_specs=(
            P("rep", "exp"),
            P("rep", "exp", None, None, None),
            P("rep", "exp"),
            P("rep", "exp"),
        ),
        check_vma=False,
    )
```

```python
import math

import jax
import jax.numpy as jnp
from jax import lax
from jax.experimental import pallas as pl
from jax.experimental.pallas import tpu as pltpu
from jax.sharding import PartitionSpec as P

MIG = 2
LANES = 128
SUB = 8
ROWS = 16
PLANE = 8
FIRST = (20, 4, 10)
F32 = jnp.float32
BF16 = jnp.bfloat16


def _smem():
    return pl.BlockSpec(memory_space=pltpu.SMEM)


def _vmem():
    return pl.BlockSpec(memory_space=pltpu.VMEM)


def _any():
    return pl.BlockSpec(memory_space=pl.ANY)


def _hbm():
    return pl.BlockSpec(memory_space=pltpu.HBM)


def _shape(shape, dtype):
    return jax.ShapeDtypeStruct(shape, dtype)


def _call(body, name, out_shape, ins, outs, args, scratch=(), us=1.0, room=32):
    return pl.pallas_call(
        body,
        name=name,
        out_shape=out_shape,
        in_specs=ins,
        out_specs=outs,
        scratch_shapes=list(scratch),
        compiler_params=pltpu.CompilerParams(vmem_limit_bytes=room * 1024 * 1024),
        cost_estimate=pl.CostEstimate(flops=0, bytes_accessed=int(us * 3.5e6), transcendentals=0),
    )(*args)


def _turned(size, first):
    return [[(k + first) % size for k in range(size)]]


def _present(anchor_ref, base, requests):
    mask = jnp.int32(0)
    for g in range(requests):
        a = anchor_ref[base + g] - base
        inside = (a >= 0) & (a < requests)
        mask = mask | jnp.where(inside, jnp.int32(1) << jnp.clip(a, 0, requests - 1), 0)
    return mask


def _slots(rep_ref, anchor_ref, requests):
    base = rep_ref[0] * requests
    count = jnp.int32(0)
    found = []
    for g in range(requests):
        a = anchor_ref[base + g]
        local = a - base
        arrived = (local < 0) | (local >= requests)
        found.append((a, jnp.clip(local, 0, requests - 1), arrived, jnp.minimum(count, MIG - 1)))
        count = count + jnp.where(arrived, 1, 0)
    return found


def _pack_body(
    requests, rep_ref, anchor_ref, table_ref, pool_ref, window_ref, scan_ref, hidden_ref, weight_ref,
    out_ref, mine_ref, keep_ref, send_ref, scans_ref, pages_ref, win_ref, rows_ref, blocks_ref, sems,
):
    pages = table_ref.shape[0]
    taps, _, channels = window_ref.shape
    blocks = channels // LANES
    plane = PLANE
    width = weight_ref.shape[2] // plane
    r = rep_ref[0]
    x, core = (r // 2) % 4, r % 2
    hidden_copy = pltpu.make_async_copy(hidden_ref.at[0], rows_ref, sems.at[plane])
    hidden_copy.start()
    weights = []
    order = (4, 5, 6, 7, 0, 1, 2, 3)
    for f, p in enumerate(order):
        block = ((x + p) % 4) * 2 + (core + p // 4) % 2
        columns = pl.ds(pl.multiple_of(block * width, width), width)
        weights.append(
            pltpu.make_async_copy(weight_ref.at[0, :, columns], blocks_ref.at[f], sems.at[f])
        )
        weights[-1].start()
    copies = [pltpu.make_async_copy(window_ref, win_ref, sems.at[plane + 1])]
    copies[0].start()
    base = rep_ref[0] * requests
    mask = _present(anchor_ref, base, requests)
    first, second = jnp.int32(0), jnp.int32(0)
    for o in reversed(range(requests)):
        leaves = ((mask >> o) & 1) == 0
        second = jnp.where(leaves, first, second)
        first = jnp.where(leaves, o, first)
    leaving = (first, second)
    for j, o in enumerate(leaving):
        copies.append(pltpu.make_async_copy(scan_ref.at[o], scans_ref.at[j], sems.at[plane + 1 + len(copies)]))
        copies[-1].start()
        for m in range(pages):
            page = pool_ref.at[table_ref[m, o], 0]
            copies.append(pltpu.make_async_copy(page, pages_ref.at[j, m], sems.at[plane + 1 + len(copies)]))
            copies[-1].start()
    hidden_copy.wait()
    hidden = rows_ref[...]
    for f, p in enumerate(order):
        weights[f].wait()
        total = jnp.dot(hidden, blocks_ref[f], preferred_element_type=F32)
        at = slice(p % 4 * width, (p % 4 + 1) * width)
        if p == 0:
            mine_ref[...] = total.astype(BF16)
        elif p < 4:
            keep_ref[:, (p - 1) * width : p * width] = total.astype(BF16)
        else:
            send_ref[:, at] = total.astype(BF16)
    for copy in copies:
        copy.wait()
    row = lax.broadcasted_iota(jnp.int32, (requests, channels), 0)
    wins = []
    for j, o in enumerate(leaving):
        lines = [
            jnp.sum(jnp.where(row == o, win_ref[t].astype(F32), 0.0), axis=0, keepdims=True) for t in range(taps)
        ]
        wins.append([line[:, b * LANES : (b + 1) * LANES] for line in lines for b in range(blocks)])
    rows_each = scans_ref.shape[1] * blocks // out_ref.shape[0]
    per_block = scans_ref.shape[1] // rows_each
    blank = jnp.zeros((1, LANES), F32)
    for i in range(out_ref.shape[0]):
        b, q = i // per_block, i % per_block
        tail = []
        for j in range(MIG):
            tail.append(scans_ref[j, q * rows_each : (q + 1) * rows_each, b * LANES : (b + 1) * LANES])
            tail.append(wins[j][i] if i < len(wins[j]) else blank)
            tail.extend([blank] * (SUB // MIG - rows_each - 1))
        m, c, h = i // 4, i // 2 % 2, i % 2
        heads = [pages_ref[j, m, c].astype(F32)[h * SUB : (h + 1) * SUB] for j in range(MIG)]
        for j in range(MIG):
            out_ref[i, j] = heads[j].astype(BF16)
        out_ref[i, MIG] = jnp.concatenate(tail, axis=0).astype(BF16)


def _route_body(requests, anchor_ref, dep_ref, out_ref):
    anchors = anchor_ref[...]
    replicas = anchors.shape[0]
    home = lax.broadcasted_iota(jnp.int32, anchors.shape, 0)
    place = lax.broadcasted_iota(jnp.int32, anchors.shape, 1).astype(F32)
    source = anchors // requests
    bit = (jnp.int32(1) << (anchors - source * requests)).astype(F32)
    arrived = source != home
    staying = jnp.sum(jnp.where(arrived, 0.0, bit), axis=1, keepdims=True).astype(jnp.int32)
    first = ((~staying) & (staying + 1)).astype(F32)
    lowest = jnp.zeros(anchors.shape, F32)
    for s in range(replicas):
        lowest = jnp.where(source == s, first[s : s + 1], lowest)
    place_of = (source + replicas - FIRST[0]) % replicas
    item = (place_of * MIG).astype(F32) + jnp.where(lowest != bit, 1.0, 0.0)
    early = jnp.min(jnp.where(arrived, place, 99.0), axis=1, keepdims=True)
    one = jnp.sum(jnp.where(arrived & (place == early), item, 0.0), axis=1, keepdims=True)
    two = jnp.sum(jnp.where(arrived & (place != early), item, 0.0), axis=1, keepdims=True)
    lane = lax.broadcasted_iota(jnp.int32, out_ref.shape, 1)
    out_ref[...] = jnp.where(lane == 0, one, jnp.where(lane == 1, two, 0.0)).astype(jnp.int32)


def _fold_body(keep_ref, got_ref, o1, o2, o3):
    width = o1.shape[1]
    for k, o in enumerate((o1, o2, o3)):
        mine = keep_ref[:, k * width : (k + 1) * width].astype(F32)
        o[...] = (mine + got_ref[:, (k + 1) * width : (k + 2) * width].astype(F32)).astype(o.dtype)


def _piece(i, replicas):
    return (i + FIRST[0] - FIRST[1]) % replicas


def _select_body(index_ref, in_ref, mine_ref, got_ref, e1, e2, e3, dep_ref, out_ref):
    replicas = out_ref.shape[0]
    row = lax.broadcasted_iota(jnp.int32, (SUB, LANES), 0)
    half = SUB // MIG
    cap = e1.shape[0] // replicas
    width = e1.shape[1]
    blocks = width // LANES
    total = mine_ref[...].astype(F32) + got_ref[:, :width].astype(F32)
    total = (total + e1[...].astype(F32)) + (e2[...].astype(F32) + e3[...].astype(F32))
    for t in range(replicas):
        d = (t + FIRST[1]) % replicas
        tails = []
        for j in range(MIG):
            i = index_ref[d, j]
            rank = i % MIG
            out_ref[t, j] = in_ref[i // MIG, rank]
            tail = in_ref[i // MIG, MIG].astype(F32)
            tails.append(jnp.where(rank == j, tail, pltpu.roll(tail, half, 0)))
        tail = jnp.where(row < half, tails[0], tails[1])
        rows = total[d * cap : (d + 1) * cap]
        experts = [rows[:, b * LANES : (b + 1) * LANES] for b in range(blocks)]
        out_ref[t, MIG] = tail.astype(BF16)
        for h in range(2):
            pair = experts[h * blocks // 2 : (h + 1) * blocks // 2]
            out_ref[t, MIG + 1 + h] = jnp.concatenate(pair, axis=0).astype(BF16)


def _local_body(
    requests, rep_ref, anchor_ref, window_ref, conv_ref, taps_ref, bias_ref, mix_ref, dep_ref,
    base_ref, which_ref, taps_out_ref, mix_out_ref,
):
    taps = window_ref.shape[0]
    weights = taps_ref[...]
    row = lax.broadcasted_iota(jnp.int32, (requests, requests), 0)
    col = lax.broadcasted_iota(jnp.int32, (requests, requests), 1)
    row_w = lax.broadcasted_iota(jnp.int32, which_ref.shape, 0)
    col_w = lax.broadcasted_iota(jnp.int32, which_ref.shape, 1)
    pick = jnp.zeros((requests, requests), F32)
    which = jnp.zeros(which_ref.shape, F32)
    for g, (_, local, arrived, order) in enumerate(_slots(rep_ref, anchor_ref, requests)):
        pick = jnp.where((row == g) & (col == local) & ~arrived, 1.0, pick)
        which = jnp.where((row_w == g) & (col_w == order) & arrived, 1.0, which)
    pick = pick.astype(BF16)
    mixed = conv_ref[...].astype(F32) * weights[taps : taps + 1] + bias_ref[...]
    for t in range(taps):
        mixed = mixed + jnp.dot(pick, window_ref[t], preferred_element_type=F32) * weights[t : t + 1]
    base_ref[...] = mixed
    which_ref[...] = which
    taps_out_ref[...] = weights
    mix_out_ref[...] = mix_ref[...]


def _act_body(moved_ref, base_ref, which_ref, taps_ref, mix_ref, out_ref, act_ref, win_ref):
    requests, channels = base_ref.shape
    blocks = channels // LANES
    weights = taps_ref[...]
    taps = weights.shape[0] - 1
    mixed = base_ref[...]
    for j in range(MIG):
        for t in range(taps):
            for b in range(blocks):
                at = j * (SUB // MIG) + 2
                tile = moved_ref[_piece(t * blocks + b, moved_ref.shape[0]), MIG].astype(F32)
                win_ref[t : t + 1, b * LANES : (b + 1) * LANES] = tile[at : at + 1]
        line = jnp.sum(win_ref[0:taps, :] * weights[0:taps], axis=0, keepdims=True)
        mixed = mixed + which_ref[:, j : j + 1] * line
    act = mixed * (1.0 / (1.0 + jnp.exp(-mixed)))
    act_ref[...] = act
    turn = (((1,), (1,)), ((), ()))
    partial = lax.dot_general(act.astype(BF16), mix_ref[...], turn, preferred_element_type=F32)
    rank = 2 * LANES
    high = partial.astype(BF16).astype(F32)
    low = (partial - high)[:, rank:]
    fill = jnp.zeros((requests, LANES - 2 * low.shape[1]), F32)
    tail = jnp.concatenate([high[:, rank:], low, fill], axis=1)
    experts, replicas = out_ref.shape[0], moved_ref.shape[0]
    lane = lax.broadcasted_iota(jnp.int32, (SUB, LANES), 1)
    steps = [
        high[h * SUB : (h + 1) * SUB, b * LANES : (b + 1) * LANES].astype(BF16) for h in range(2) for b in range(2)
    ]
    for f in range(PLANE):
        for q in range(2):
            block = moved_ref[(f - FIRST[1]) % replicas, MIG + 1 + q].astype(F32)
            for z in range(1, replicas // PLANE):
                block = block + moved_ref[(z * PLANE + f - FIRST[1]) % replicas, MIG + 1 + q].astype(F32)
            e = (2 * f + q - FIRST[2]) % experts
            for n, step in enumerate(steps):
                out_ref[e, n] = step
            for h, part in enumerate((pltpu.roll(block, LANES // 2, 1), block)):
                rows = tail[h * SUB : (h + 1) * SUB]
                out_ref[e, len(steps) + h] = jnp.where(lane < LANES // 2, rows, part).astype(BF16)


def _ready_body(
    requests, states, rep_ref, anchor_ref, routes_ref, share_ref, moved_ref, act_ref, gate_ref, scan_ref, step_ref,
    bias_ref, decay_ref, skip_ref, old_ref, rate_ref, gate_out_ref, skip_out_ref, step_out_ref, bias_out_ref,
    share_out_ref, arr_ref, count_ref,
):
    slots = _slots(rep_ref, anchor_ref, requests)
    blocks = act_ref.shape[1] // LANES
    rows_each = states * blocks // moved_ref.shape[0]
    per_block = states // rows_each
    for i in range(moved_ref.shape[0]):
        b, q = i // per_block, i % per_block
        tail = moved_ref[_piece(i, moved_ref.shape[0]), MIG].astype(F32)
        for j in range(MIG):
            at = j * (SUB // MIG)
            arr_ref[j, q * rows_each : (q + 1) * rows_each, b * LANES : (b + 1) * LANES] = tail[at : at + rows_each]
    for g, (_, local, arrived, order) in enumerate(slots):
        old_ref[g] = jnp.where(arrived, arr_ref[order], scan_ref[local])
    rate_ref[...] = -jnp.exp(decay_ref[...])
    gate = gate_ref[...].astype(F32)
    gate_out_ref[...] = gate * (1.0 / (1.0 + jnp.exp(-gate)))
    skip_out_ref[...] = skip_ref[...] * act_ref[...]
    step_out_ref[...] = step_ref[...]
    bias_out_ref[...] = jnp.broadcast_to(bias_ref[...], bias_out_ref.shape)
    experts = count_ref.shape[0]
    for e in range(experts):
        count_ref[e] = 0
    row = lax.broadcasted_iota(jnp.int32, (requests, LANES), 0)
    col = lax.broadcasted_iota(jnp.int32, (requests, LANES), 1)
    share = jnp.zeros((requests, LANES), F32)
    for t in range(requests):
        for k in range(routes_ref.shape[0]):
            e = routes_ref[k, t]
            place = count_ref[e]
            count_ref[e] = place + 1
            share = share + jnp.where((row == t) & (col == (e + experts - FIRST[2]) % experts * SUB + place), share_ref[k, t], 0.0)
    share_out_ref[...] = share


def _final_body(
    states, sums_ref, act_ref, old_ref, rate_ref, gate_ref, skip_ref, step_ref, bias_ref, share_ref,
    gated_ref, mix_ref, y_ref,
):
    experts = sums_ref.shape[0]
    requests, _ = act_ref.shape
    totals = []
    for n in range(sums_ref.shape[1]):
        total = sums_ref[0, n].astype(F32)
        for e in range(1, experts):
            total = total + sums_ref[e, n].astype(F32)
        totals.append(total)
    projected = jnp.concatenate(
        [jnp.concatenate(totals[0:2], axis=1), jnp.concatenate(totals[2:4], axis=1)], axis=0
    )
    step = jnp.dot(projected.astype(BF16), step_ref[...], preferred_element_type=F32) + bias_ref[0:1]
    step = jnp.maximum(step, 0.0) + jnp.log1p(jnp.exp(-jnp.abs(step)))
    tail = jnp.concatenate(totals[4:6], axis=0)
    columns = jnp.transpose(tail + pltpu.roll(tail, LANES - 2 * states, 1))
    rest = share_ref[...]
    parts = []
    for _ in range(3):
        part = rest.astype(BF16).astype(F32)
        parts.append(part)
        rest = rest - part
    lane = lax.broadcasted_iota(jnp.int32, (SUB, LANES), 1)
    outs = []
    for e in range(experts):
        left = pltpu.roll(sums_ref[e, 4].astype(F32), LANES // 2, 1)
        outs.append(jnp.where(lane < LANES // 2, left, sums_ref[e, 5].astype(F32)))
    outs = jnp.concatenate(outs, axis=0).astype(BF16)
    both = jnp.concatenate([*parts, *(pltpu.roll(p, SUB // 2, 1) for p in parts)], axis=0).astype(BF16)
    terms = jnp.dot(both, outs, preferred_element_type=F32)
    halves = [
        sum(terms[(3 * h + i) * requests : (3 * h + i + 1) * requests] for i in reversed(range(3))) for h in range(2)
    ]
    mix_ref[...] = jnp.concatenate(halves, axis=1).astype(BF16)
    rate = rate_ref[...]
    flow = step * act_ref[...]
    for g in range(requests):
        inflow = columns[0:states, g : g + 1]
        readout = columns[states : 2 * states, g : g + 1]
        state = jnp.exp(step[g : g + 1] * rate) * old_ref[g] + inflow * flow[g : g + 1]
        y_ref[g : g + 1, :] = jnp.sum(readout * state, axis=0, keepdims=True)
    gated_ref[...] = ((y_ref[...] + skip_ref[...]) * gate_ref[...]).astype(BF16)


def _attend_body(
    requests, rep_ref, anchor_ref, len_ref, table_ref, query_ref, key_ref, value_ref, pool_ref, moved_ref, dep_ref,
    out_ref, pages_ref, keys_ref, values_ref,
):
    turn = (((1,), (1,)), ((), ()))
    head = key_ref.shape[1]
    heads = query_ref.shape[1] // head
    pool, _, _, page, _ = pool_ref.shape
    table = table_ref[...].astype(F32).astype(BF16)
    pages = table.shape[0]
    span = pages * page
    slots = _slots(rep_ref, anchor_ref, requests)
    row1 = lax.broadcasted_iota(jnp.int32, (requests, 1), 0)
    row = lax.broadcasted_iota(jnp.int32, (requests, requests), 0)
    col = lax.broadcasted_iota(jnp.int32, (requests, requests), 1)
    live = jnp.zeros((requests, 1), jnp.int32)
    order = jnp.full((requests, 1), -1, jnp.int32)
    pick = jnp.zeros((requests, requests), F32)
    live_of = [jnp.int32(0)] * MIG
    for g, (a, local, arrived, place) in enumerate(slots):
        length = len_ref[a]
        live = jnp.where(row1 == g, length, live)
        order = jnp.where((row1 == g) & arrived, place, order)
        pick = jnp.where((row == g) & (col == local), 1.0, pick)
        live_of = [jnp.where(arrived & (place == j), length, live_of[j]) for j in range(MIG)]
    mine = lax.dot_general(pick.astype(BF16), table, turn, preferred_element_type=F32).astype(jnp.int32)
    here = jnp.where(order < 0, live, 0)
    at = lax.broadcasted_iota(jnp.int32, (requests, pool * page), 1)
    which, token = at // page, at % page
    seen = jnp.zeros((requests, pool * page), jnp.bool_)
    for m in range(pages):
        seen = seen | ((mine[:, m : m + 1] == which) & (token + m * page < here))
    at = lax.broadcasted_iota(jnp.int32, (requests, MIG * span), 1)
    seen_moved = (at // span == order) & (at % span < live)
    down = lax.broadcasted_iota(jnp.int32, (span, head), 0)
    for i in range(moved_ref.shape[0]):
        m, c, h = i // 4, i // 2 % 2, i % 2
        ref = (keys_ref, values_ref)[c]
        for j in range(MIG):
            start = j * span + m * page + h * SUB
            ref[start : start + SUB, :] = moved_ref[_piece(i, moved_ref.shape[0]), j].astype(F32)
    for j in range(MIG):
        for c, ref in ((0, keys_ref), (1, values_ref)):
            block = ref[j * span : (j + 1) * span, :]
            pages_ref[j, 0, c] = jnp.where(down < live_of[j], block, 0.0).astype(BF16)
    moved_keys = keys_ref[...].astype(BF16)
    moved_values = values_ref[...].astype(BF16)
    pool_keys = pool_ref[:, 0, 0].reshape(pool * page, head)
    pool_values = pool_ref[:, 0, 1].reshape(pool * page, head)
    query = query_ref[...]
    queries = jnp.concatenate([query[:, h * head : (h + 1) * head] for h in range(heads)], axis=0)
    scale = 1.0 / math.sqrt(head)
    scores = lax.dot_general(queries, pool_keys, turn, preferred_element_type=F32) * scale
    scores_moved = lax.dot_general(queries, moved_keys, turn, preferred_element_type=F32) * scale
    new_key = jnp.concatenate([key_ref[...].astype(F32)] * heads, axis=0)
    new_value = jnp.concatenate([value_ref[...].astype(F32)] * heads, axis=0)
    own = jnp.sum(queries.astype(F32) * new_key, axis=1, keepdims=True) * scale
    far = F32(-1e30)
    seen = jnp.concatenate([jnp.where(seen, 1.0, 0.0)] * heads, axis=0) > 0.5
    seen_moved = jnp.concatenate([jnp.where(seen_moved, 1.0, 0.0)] * heads, axis=0) > 0.5
    scores = jnp.where(seen, scores, far)
    scores_moved = jnp.where(seen_moved, scores_moved, far)
    highest = jnp.maximum(
        jnp.maximum(jnp.max(scores, axis=1, keepdims=True), jnp.max(scores_moved, axis=1, keepdims=True)), own
    )
    e_pool = jnp.exp(scores - highest)
    e_moved = jnp.exp(scores_moved - highest)
    e_own = jnp.exp(own - highest)
    total = jnp.sum(e_pool, axis=1, keepdims=True) + jnp.sum(e_moved, axis=1, keepdims=True) + e_own
    w_pool = (e_pool / total).astype(BF16)
    w_moved = (e_moved / total).astype(BF16)
    w_own = (e_own / total).astype(BF16).astype(F32)
    context = jnp.dot(w_pool, pool_values, preferred_element_type=F32)
    context = context + jnp.dot(w_moved, moved_values, preferred_element_type=F32) + w_own * new_value
    for h in range(heads):
        out_ref[:, h * head : (h + 1) * head] = context[h * requests : (h + 1) * requests].astype(BF16)


def per_device(
    query,
    new_key,
    new_value,
    page_pool,
    block_table,
    lengths,
    anchor,
    conv_input,
    gate_input,
    window_state,
    scan_state,
    filter_taps,
    filter_bias,
    mix_weight,
    step_weight,
    step_bias,
    log_decay,
    skip_gain,
    routes,
    route_weight,
    expert_hidden,
    down_weight,
):
    requests, channels = query.shape
    replicas = lax.axis_size("rep")
    experts = lax.axis_size("exp")
    rep = lax.axis_index("rep").astype(jnp.int32).reshape(1)
    states = log_decay.shape[0]
    head = new_key.shape[1]
    pages, page = block_table.shape[1], page_pool.shape[3]
    slots = expert_hidden.shape[1]
    features = down_weight.shape[2]
    table = block_table.T
    window = jnp.transpose(window_state, (1, 0, 2))

    packed, mine, keep, send = _call(
        lambda *refs: _pack_body(requests, *refs),
        "pack_leaving",
        [
            _shape((replicas, MIG + 1, SUB, LANES), BF16),
            _shape((slots, features // PLANE), BF16),
            _shape((slots, 3 * features // PLANE), BF16),
            _shape((slots, features // 2), BF16),
        ],
        [_smem()] * 3 + [_hbm()] * 5,
        [_vmem()] * 4,
        (rep, anchor, table, page_pool, window, scan_state, expert_hidden, down_weight),
        scratch=[
            pltpu.VMEM((MIG, states, channels), F32),
            pltpu.VMEM((MIG, pages, 2, page, head), BF16),
            pltpu.VMEM(window.shape, BF16),
            pltpu.VMEM(expert_hidden.shape[1:], BF16),
            pltpu.VMEM((PLANE, down_weight.shape[1], features // PLANE), BF16),
            pltpu.SemaphoreType.DMA((2 + MIG * (1 + pages) + PLANE,)),
        ],
        us=4,
        room=60,
    )
    turned = _turned(replicas, FIRST[0])
    spread = lax.all_to_all(packed, "rep", split_axis=0, concat_axis=0, tiled=True, axis_index_groups=turned)

    def at(z, x, c):
        return (z * 4 + x) * 2 + c

    every = [(z, x, c) for z in range(4) for x in range(4) for c in range(2)]
    got = lax.ppermute(send, "rep", [(at(z, x, c), at(z, x, 1 - c)) for z, x, c in every])
    width = features // PLANE
    by_x = _call(
        _fold_body,
        "fold_cores",
        [_shape((slots, width), BF16)] * 3,
        [_vmem()] * 2,
        [_vmem()] * 3,
        (keep, got),
        us=0.5,
    )
    came = [
        lax.ppermute(by_x[k - 1], "rep", [(at(z, x, c), at(z, (x + k) % 4, c)) for z, x, c in every]) for k in (2, 1, 3)
    ]

    index = _call(
        lambda *refs: _route_body(requests, *refs),
        "route_pieces",
        _shape((replicas, LANES), jnp.int32),
        [_vmem(), _any()],
        _vmem(),
        (anchor.reshape(replicas, requests), by_x[0]),
        us=1,
    )
    base, which, taps, mix = _call(
        lambda *refs: _local_body(requests, *refs),
        "filter_local",
        [
            _shape((requests, channels), F32),
            _shape((requests, LANES), F32),
            _shape(filter_taps.shape, F32),
            _shape(mix_weight.shape[::-1], BF16),
        ],
        [_smem()] * 2 + [_vmem()] * 5 + [_any()],
        [_vmem()] * 4,
        (rep, anchor, window, conv_input, filter_taps, filter_bias.reshape(1, channels), mix_weight.T, index),
        us=1.5,
    )
    onward = _call(
        _select_body,
        "select_pieces",
        _shape((replicas, MIG + 3, SUB, LANES), BF16),
        [_smem()] + [_vmem()] * 6 + [_any()],
        _vmem(),
        (index, spread, mine, got, *came, which),
        us=1.5,
    )
    turned = _turned(replicas, FIRST[1])
    moved = lax.all_to_all(onward, "rep", split_axis=0, concat_axis=0, tiled=True, axis_index_groups=turned)

    sums, act = _call(
        _act_body,
        "filter_and_project",
        [_shape((experts, 6, SUB, LANES), BF16), _shape((requests, channels), F32)],
        [_vmem()] * 5,
        [_vmem()] * 2,
        (moved, base, which, taps, mix),
        scratch=[pltpu.VMEM((SUB, channels), F32)],
        us=1.5,
    )
    turned = _turned(experts, FIRST[2])
    sums_all = lax.all_to_all(sums, "exp", split_axis=0, concat_axis=0, tiled=True, axis_index_groups=turned)

    attended, pages_out = _call(
        lambda *refs: _attend_body(requests, *refs),
        "attend",
        [_shape((requests, channels), BF16), _shape((MIG, 1, 2, pages * page, head), BF16)],
        [_smem()] * 3 + [_vmem()] * 6 + [_any()],
        [_vmem()] * 2,
        (rep, anchor, lengths, table, query, new_key, new_value, page_pool, moved, act),
        scratch=[pltpu.VMEM((MIG * pages * page, head), F32)] * 2,
        us=2,
    )
    ready = _call(
        lambda *refs: _ready_body(requests, states, *refs),
        "ready_state",
        [
            _shape((requests, states, channels), F32),
            _shape((states, channels), F32),
            _shape((requests, channels), F32),
            _shape((requests, channels), F32),
            _shape(step_weight.shape, BF16),
            _shape((SUB, channels), F32),
            _shape((requests, LANES), F32),
        ],
        [_smem()] * 4 + [_vmem()] * 8,
        [_vmem()] * 7,
        (
            rep, anchor, routes.T, route_weight.T, moved, act, gate_input, scan_state, step_weight,
            step_bias.reshape(1, channels), log_decay, skip_gain.reshape(1, channels),
        ),
        scratch=[pltpu.VMEM((MIG, states, channels), F32), pltpu.SMEM((experts,), jnp.int32)],
        us=2,
    )
    gated, mixed = _call(
        lambda *refs: _final_body(states, *refs),
        "update_state",
        [_shape((requests, channels), BF16), _shape((requests, features // experts), BF16)],
        [_vmem()] * 9,
        [_vmem()] * 2,
        (sums_all, act, *ready),
        scratch=[pltpu.VMEM((requests, channels), F32)],
        us=2,
    )
    return (attended, pages_out, gated, mixed)


def solution(mesh):
    placed = (
        P("rep", "exp"),
        P("rep", "exp"),
        P("rep", "exp"),
        P("rep", "exp", None, None, None),
        P("rep", None),
        P(),
        P(),
        P("rep", "exp"),
        P("rep", "exp"),
        P("rep", None, "exp"),
        P("rep", None, "exp"),
        P(None, "exp"),
        P("exp"),
        P("exp", None),
        P(None, "exp"),
        P("exp"),
        P(None, "exp"),
        P("exp"),
        P("rep", None),
        P("rep", None),
        P("exp", None, "rep"),
        P("exp", "rep", None),
    )
    return jax.shard_map(
        per_device,
        mesh=mesh,
        in_specs=placed,
        out_specs=(
            P("rep", "exp"),
            P("rep", "exp", None, None, None),
            P("rep", "exp"),
            P("rep", "exp"),
        ),
        check_vma=False,
    )
```
